32 devices in a mesh: img: 16 (over z, y, x), row: 2 (over core).
Axes of the slice: x: 2, y: 2, z: 4, core: 2. Of those that a mesh axis runs over, the one named last changes fastest.
Arguments:
- images: bfloat16 [48, 16, 16, 1024], P('img', 'row'), may hold values from -6 to 6
- extents: int32 [48, 2], P('img'), may hold values from 9 to 16, as said below
- entry_weight: bfloat16 [1024, 256], replicated, may hold values from -0.1875 to 0.1875
- middle_weight: bfloat16 [3, 3, 256, 256], replicated, may hold values from -0.125 to 0.125
- closing_weight: bfloat16 [256, 1024], replicated, may hold values from -0.375 to 0.375
- widen_weight: bfloat16 [1024, 512], replicated, may hold values from -0.1875 to 0.1875
- strided_weight: bfloat16 [3, 3, 512, 512], replicated, may hold values from -0.09375 to 0.09375
- expand_weight: bfloat16 [512, 2048], replicated, may hold values from -0.25 to 0.25
- shortcut_weight: bfloat16 [1024, 2048], replicated, may hold values from -0.1875 to 0.1875
- entry_affine: float32 [2, 256], replicated, may hold values from 0.5 to 1.5
- middle_affine: float32 [2, 256], replicated, may hold values from 0.5 to 1.5
- closing_affine: float32 [2, 1024], replicated, may hold values from 0.5 to 1.5
- widen_affine: float32 [2, 512], replicated, may hold values from 0.5 to 1.5
- strided_affine: float32 [2, 512], replicated, may hold values from 0.5 to 1.5
- expand_affine: float32 [2, 2048], replicated, may hold values from 0.5 to 1.5
- shortcut_affine: float32 [2, 2048], replicated, may hold values from 0.5 to 1.5
- cotangent: bfloat16 [48, 8, 8, 2048], P('img', 'row'), may hold values from -6 to 6
Outputs:
- features: bfloat16 [48, 8, 8, 2048], P('img', 'row')
- image_grads: bfloat16 [48, 16, 16, 1024], P('img', 'row')
- entry_gradient: float32 [1024, 256], P('row')
- middle_gradient: float32 [3, 3, 256, 256], P(None, None, 'row')
- closing_gradient: float32 [256, 1024], P('row')
- widen_gradient: float32 [1024, 512], P('row')
- strided_gradient: float32 [3, 3, 512, 512], P(None, None, 'row')
- expand_gradient: float32 [512, 2048], P('row')
- shortcut_gradient: float32 [1024, 2048], P('row')
- affine_entry: float32 [2, 256], replicated
- affine_middle: float32 [2, 256], replicated
- affine_closing: float32 [2, 1024], replicated
- affine_widen: float32 [2, 512], replicated
- affine_strided: float32 [2, 512], replicated
- affine_expand: float32 [2, 2048], replicated
- affine_shortcut: float32 [2, 2048], replicated
The draws below stay inside these ranges and needn't reach their ends.
Inputs may be any that keep to these rules, and one draw needn't show every extreme that they name: Row and column extents of each image's valid region, which starts at its top-left cell; in every draw some image is valid on all 16 x 16 cells.
All inputs are finite; a program needn't handle non-finite values.
Results may differ from the reference program's by a relative error of at most 0.019.
Values may be sent and summed in bfloat16 or wider, within the bound.
No kernel may reach another device: no remote copies, remote signals or barrier semaphores. Data moves between devices by JAX's collectives and lax.ppermute only.
A program may use at most 192 MiB of HBM per device.

```python
import jax
import jax.numpy as jnp
from jax import lax

C_IN = 1024
MID1 = 256
MID2 = 512
C_OUT = 2048
GRID = 16
IMAGES = 48
HALF = 8


def draw_extents(key, part):
    key = jax.random.fold_in(key, 7)
    first, second = jax.random.split(key)
    sizes = jax.random.randint(first, (IMAGES, 2), GRID // 2 + 1, GRID + 1)
    chosen = jax.random.randint(second, (), 0, IMAGES)
    sizes = jnp.where((jnp.arange(IMAGES) == chosen)[:, None], GRID, sizes)
    return sizes.astype(jnp.int32)


def block_levels(stream_key, dims, pieces, smallest, high):
    loudness, own = 1.0, jax.random.fold_in(stream_key, 6)
    for dim, parts in pieces:
        steps = jnp.exp(jax.random.uniform(jax.random.fold_in(own, dim), (parts,), jnp.float32, smallest / len(pieces), high / len(pieces)))
        loudness = loudness * jnp.repeat(steps, dims[dim] // parts).reshape([-1 if axis == dim else 1 for axis in range(len(dims))])
    return loudness


def noise(rng, extent, deviation, most, cuts=(), held_as=jnp.bfloat16):
    values = jax.random.normal(rng, extent, jnp.float32) * deviation
    if len(cuts) > 0:
        values = block_levels(rng, extent, cuts, -0.22, 0.18) * values
    return jnp.clip(values, min=-most, max=most).astype(held_as)


def setup_inputs(seed: int = 0) -> dict:
    keys = jax.random.split(jax.random.key(seed), 18)
    images = noise(keys[0], (IMAGES, GRID, GRID, C_IN), 1.0, 6.0, ((0, 16), (1, 2)))
    extents = draw_extents(jax.random.fold_in(keys[17], 71), 0)
    entry_weight = noise(keys[2], (C_IN, MID1), C_IN ** -0.5, 0.1875)
    middle_weight = noise(keys[3], (3, 3, MID1, MID1), (9 * MID1) ** -0.5, 0.125)
    closing_weight = noise(keys[4], (MID1, C_IN), MID1 ** -0.5, 0.375)
    widen_weight = noise(keys[5], (C_IN, MID2), C_IN ** -0.5, 0.1875)
    strided_weight = noise(keys[6], (3, 3, MID2, MID2), (9 * MID2) ** -0.5, 0.09375)
    expand_weight = noise(keys[7], (MID2, C_OUT), MID2 ** -0.5, 0.25)
    shortcut_weight = noise(keys[8], (C_IN, C_OUT), C_IN ** -0.5, 0.1875)
    entry_affine = jnp.clip(jax.random.uniform(keys[9], (2, MID1), jnp.float32, 0.5, 1.5), 0.5, 1.5)
    middle_affine = jnp.clip(jax.random.uniform(keys[10], (2, MID1), jnp.float32, 0.5, 1.5), 0.5, 1.5)
    closing_affine = jnp.clip(jax.random.uniform(keys[11], (2, C_IN), jnp.float32, 0.5, 1.5), 0.5, 1.5)
    widen_affine = jnp.clip(jax.random.uniform(keys[12], (2, MID2), jnp.float32, 0.5, 1.5), 0.5, 1.5)
    strided_affine = jnp.clip(jax.random.uniform(keys[13], (2, MID2), jnp.float32, 0.5, 1.5), 0.5, 1.5)
    expand_affine = jnp.clip(jax.random.uniform(keys[14], (2, C_OUT), jnp.float32, 0.5, 1.5), 0.5, 1.5)
    shortcut_affine = jnp.clip(jax.random.uniform(keys[15], (2, C_OUT), jnp.float32, 0.5, 1.5), 0.5, 1.5)
    cotangent = noise(keys[16], (IMAGES, HALF, HALF, C_OUT), 1.0, 6.0, ((0, 16), (1, 2)))
    return dict(images=images, extents=extents, entry_weight=entry_weight, middle_weight=middle_weight, closing_weight=closing_weight, widen_weight=widen_weight, strided_weight=strided_weight, expand_weight=expand_weight, shortcut_weight=shortcut_weight, entry_affine=entry_affine, middle_affine=middle_affine, closing_affine=closing_affine, widen_affine=widen_affine, strided_affine=strided_affine, expand_affine=expand_affine, shortcut_affine=shortcut_affine, cotangent=cotangent)


EPS = 1e-05
DIMS = ('NHWC', 'HWIO', 'NHWC')
HIGH = lax.Precision.HIGHEST

@jax.custom_vjp
def low(v):
    return lax.optimization_barrier(v.astype(jnp.bfloat16)).astype(jnp.float32)

@jax.custom_vjp
def low_back(v):
    return v

def low_keep(v):
    return (low(v), None)

def low_pass(kept, grad):
    return (grad,)

def back_keep(v):
    return (v, None)

def back_low(kept, grad):
    return (low(grad),)
low.defvjp(low_keep, low_pass)
low_back.defvjp(back_keep, back_low)

def silu(value):
    return value * jax.nn.sigmoid(value)

def pointwise(left, weight):
    return jnp.einsum('bhwc,cm->bhwm', left, weight, precision=HIGH)

def convolve(left, kernel, stride):
    return lax.conv_general_dilated(left, kernel, (stride, stride), ((1, 1), (1, 1)), dimension_numbers=DIMS, precision=HIGH)

def normalize(value, mask, count, params):
    mean = lax.optimization_barrier(jnp.sum(value * mask, axis=(0, 1, 2))) / count
    centred = (value - mean) * mask
    spread = lax.optimization_barrier(jnp.sum(centred * centred, axis=(0, 1, 2))) / count
    return (value - mean) * lax.rsqrt(spread + EPS) * params[0] + params[1]

def reference(images, extents, entry_weight, middle_weight, closing_weight, widen_weight, strided_weight, expand_weight, shortcut_weight, entry_affine, middle_affine, closing_affine, widen_affine, strided_affine, expand_affine, shortcut_affine, cotangent):
    line = jnp.arange(GRID).astype(jnp.int32)
    inside = (line[None, :, None] < extents[:, 0][:, None, None]) & (line[None, None, :] < extents[:, 1][:, None, None])
    mask = inside.astype(jnp.float32)[..., None]
    small_mask = mask[:, ::2, ::2]
    count = jnp.sum(mask)
    small_count = jnp.sum(small_mask)

    def forward(source, entry_w, middle_w, closing_w, widen_w, strided_w, expand_w, shortcut_w, entry_p, middle_p, closing_p, widen_p, strided_p, expand_p, shortcut_p):
        entry_in = source * mask
        entry_raw = low_back(pointwise(entry_in, entry_w))
        entry_act = low(silu(normalize(entry_raw, mask, count, entry_p)) * mask)
        middle_raw = low_back(convolve(entry_act, middle_w, 1))
        middle_act = low(silu(normalize(middle_raw, mask, count, middle_p)) * mask)
        closing_raw = low_back(pointwise(middle_act, closing_w))
        block_out = low(silu(normalize(closing_raw, mask, count, closing_p) + entry_in) * mask)
        widen_raw = low_back(pointwise(block_out, widen_w))
        widen_act = low(silu(normalize(widen_raw, mask, count, widen_p)) * mask)
        strided_raw = low_back(convolve(widen_act, strided_w, 2))
        strided_act = low(silu(normalize(strided_raw, small_mask, small_count, strided_p)) * small_mask)
        expand_raw = low_back(pointwise(strided_act, expand_w))
        shortcut_raw = low_back(pointwise(block_out[:, ::2, ::2], shortcut_w))
        joined = normalize(expand_raw, small_mask, small_count, expand_p) + normalize(shortcut_raw, small_mask, small_count, shortcut_p)
        return silu(joined) * small_mask
    inputs = (images.astype(jnp.float32), entry_weight.astype(jnp.float32), middle_weight.astype(jnp.float32), closing_weight.astype(jnp.float32), widen_weight.astype(jnp.float32), strided_weight.astype(jnp.float32), expand_weight.astype(jnp.float32), shortcut_weight.astype(jnp.float32), entry_affine, middle_affine, closing_affine, widen_affine, strided_affine, expand_affine, shortcut_affine)
    features, pullback = jax.vjp(forward, *inputs)
    grads = pullback(cotangent.astype(jnp.float32))
    return (features.astype(jnp.bfloat16), grads[0].astype(jnp.bfloat16), grads[1], grads[2], grads[3], grads[4], grads[5], grads[6], grads[7], grads[8], grads[9], grads[10], grads[11], grads[12], grads[13], grads[14])
```

```python
import jax
import jax.numpy as jnp
from jax import lax
from jax.sharding import PartitionSpec as P

EPS = 1e-05
DIMS = ("NHWC", "HWIO", "NHWC")
BOTH = ("img", "row")
F32 = jnp.float32
BF16 = jnp.bfloat16


def swap_rows(value):
    count = lax.axis_size("row")
    return lax.ppermute(value, "row", [(i, (i + 1) % count) for i in range(count)])


def edge(value, step):
    count = lax.axis_size("row")
    pairs = [(i, i + step) for i in range(count) if 0 <= i + step < count]
    return lax.ppermute(value, "row", pairs)


def gather_all(vector):
    count = lax.axis_size("img") * lax.axis_size("row")
    spread = jnp.broadcast_to(vector[None], (count,) + vector.shape)
    return lax.all_to_all(spread, BOTH, 0, 0, tiled=True)


def gather_img(vector):
    count = lax.axis_size("img")
    spread = jnp.broadcast_to(vector[None], (count,) + vector.shape)
    return lax.all_to_all(spread, "img", 0, 0, tiled=True)


def sum_all(vector):
    return jnp.sum(gather_all(vector), axis=0)


def sum_split(parts):
    row = lax.axis_index("row")
    half = parts.shape[1] // 2
    low, high = parts[:, :half], parts[:, half:]
    mine = jnp.where(row == 0, low, high) + swap_rows(jnp.where(row == 0, high, low))
    total = jnp.sum(gather_img(mine.reshape(-1)), axis=0).reshape(mine.shape)
    other = swap_rows(total)
    first = jnp.where(row == 0, total, other)
    second = jnp.where(row == 0, other, total)
    return jnp.concatenate([first, second], axis=1)


def local_stats(value, mask, local_count):
    axes = tuple(range(value.ndim - 1))
    total = jnp.sum(value * mask, axis=axes)
    mean = total / jnp.maximum(local_count, 1.0)
    centred = (value - mean) * mask
    return total, jnp.sum(centred * centred, axis=axes)


def join_stats(totals, squares, counts, count):
    mean = jnp.sum(totals, axis=0) / count
    means = totals / jnp.maximum(counts, 1.0)[:, None]
    shift = means - mean
    spread = jnp.sum(squares + counts[:, None] * (shift * shift), axis=0) / count
    return mean, lax.rsqrt(spread + EPS)


def norm_stats(value, mask, counts, local_count, count):
    total, square = local_stats(value, mask, local_count)
    width = total.shape[0]
    gathered = gather_all(jnp.concatenate([total, square]))
    return join_stats(gathered[:, :width], gathered[:, width:], counts, count)


def activate(value):
    gate = jax.nn.sigmoid(value)
    return (value * gate, gate * (1.0 + value * (1.0 - gate)))


def pointwise(left, weight):
    return jnp.einsum("brgc,cm->brgm", left, weight, preferred_element_type=F32)


def pointwise_back(grad, weight):
    return jnp.einsum("brgm,cm->brgc", grad, weight, preferred_element_type=F32)


def conv_valid(left, kernel, stride):
    return lax.conv_general_dilated(
        left, kernel, (stride, stride), "VALID", dimension_numbers=DIMS, preferred_element_type=F32
    )


def flip_kernel(kernel):
    return jnp.transpose(kernel[::-1, ::-1], (0, 1, 3, 2))


def half_channels(value):
    row = lax.axis_index("row")
    half = value.shape[-1] // 2
    low, high = value[..., :half], value[..., half:]
    own = jnp.where(row == 0, low, high)
    return own, swap_rows(jnp.where(row == 0, high, low))


def in_order(own, other):
    row = lax.axis_index("row")
    return jnp.concatenate([jnp.where(row == 0, own, other), jnp.where(row == 0, other, own)], axis=1)


def weight_grad(left, grad):
    return jnp.einsum("brgc,brgm->cm", left, grad, preferred_element_type=F32)


def tap_grads(padded, grad, stride):
    height, width = grad.shape[1], grad.shape[2]
    pieces = []
    for row_tap in range(3):
        for col_tap in range(3):
            pieces.append(
                lax.slice(
                    padded,
                    (0, row_tap, col_tap, 0),
                    (
                        padded.shape[0],
                        row_tap + stride * (height - 1) + 1,
                        col_tap + stride * (width - 1) + 1,
                        padded.shape[3],
                    ),
                    (1, stride, stride, 1),
                )
            )
    return [weight_grad(piece, grad) for piece in pieces]


def orders():
    bits = lax.axis_size("img").bit_length() - 1
    ascending = list(range(bits))
    swapped = ascending[:]
    if bits > 1:
        swapped[0], swapped[1] = 1, 0
    return ascending, swapped


def permute_bit(value, bit):
    count = lax.axis_size("img")
    return lax.ppermute(value, "img", [(i, i ^ (1 << bit)) for i in range(count)])


def permute_pair(pair, bits):
    if bits[0] == bits[1]:
        moved = permute_bit(jnp.stack(pair), bits[0])
        return [moved[0], moved[1]]
    return [permute_bit(value, bit) for value, bit in zip(pair, bits)]


def reduce_pair(pair):
    place = lax.axis_index("img")
    for bits in zip(*orders()):
        kept, sent = [], []
        for value, bit in zip(pair, bits):
            half = value.shape[0] // 2
            mine = (place >> bit) & 1
            kept.append(lax.dynamic_slice_in_dim(value, mine * half, half, 0))
            sent.append(lax.dynamic_slice_in_dim(value, (1 - mine) * half, half, 0))
        moved = permute_pair(sent, bits)
        pair = [(a.astype(F32) + b.astype(F32)).astype(BF16) for a, b in zip(kept, moved)]
    return pair


def gather_pair(pair):
    place = lax.axis_index("img")
    for bits in reversed(list(zip(*orders()))):
        moved = permute_pair(pair, bits)
        joined = []
        for own, other, bit in zip(pair, moved, bits):
            upper = ((place >> bit) & 1) == 1
            joined.append(
                jnp.concatenate([jnp.where(upper, other, own), jnp.where(upper, own, other)], axis=0)
            )
        pair = joined
    return pair


def sum_over_chips(packed, axis=0):
    pair = gather_pair(reduce_pair(jnp.split(packed, 2, axis=axis)))
    return jnp.concatenate(pair, axis=axis)


def sum_over_chips_short(packed):
    members = lax.axis_size("img")
    parts = packed.reshape(members, packed.shape[0] // members, packed.shape[1])
    moved = lax.all_to_all(parts, "img", 0, 0, tiled=True)
    share = jnp.sum(moved.astype(F32), axis=0).astype(BF16)
    spread = jnp.broadcast_to(share[None], (members,) + share.shape)
    return lax.all_to_all(spread, "img", 0, 0, tiled=True).reshape(packed.shape)


def per_device(
    images,
    extents,
    entry_weight,
    middle_weight,
    closing_weight,
    widen_weight,
    strided_weight,
    expand_weight,
    shortcut_weight,
    entry_affine,
    middle_affine,
    closing_affine,
    widen_affine,
    strided_affine,
    expand_affine,
    shortcut_affine,
    cotangent,
):
    height = images.shape[1]
    width = images.shape[2]
    offset = lax.axis_index("row") * height
    line = offset + jnp.arange(height)
    column = jnp.arange(width)
    inside = (line[None, :, None] < extents[:, 0][:, None, None]) & (
        column[None, None, :] < extents[:, 1][:, None, None]
    )
    mask = inside.astype(F32)[..., None]
    small_mask = mask[:, ::2, ::2]
    mine = jnp.sum(mask)
    mine_small = jnp.sum(small_mask)
    column_pad = ((0, 0), (0, 0), (1, 1), (0, 0))

    def column_sums(grad, unit):
        return jnp.concatenate([jnp.sum(grad * unit, axis=(0, 1, 2)), jnp.sum(grad, axis=(0, 1, 2))])

    def raw_grad(grad, unit, scale, gain_grad, bias_grad, m, n, params):
        value = params[0] * scale / n * (n * grad - bias_grad - unit * gain_grad) * m
        return value.astype(BF16)

    def norm_back(grad, unit, scale, m, n, params):
        sums = sum_all(column_sums(grad, unit)).reshape(2, -1)
        return raw_grad(grad, unit, scale, sums[0], sums[1], m, n, params), sums

    entry_in = images * mask.astype(BF16)
    entry_raw = pointwise(entry_in, entry_weight)
    total, square = local_stats(entry_raw, mask, mine)
    counts = jnp.zeros((128,), F32).at[0].set(mine).at[1].set(mine_small)
    gathered = gather_all(jnp.concatenate([total, square, counts]))
    mid = total.shape[0]
    full_counts, small_counts = gathered[:, 2 * mid], gathered[:, 2 * mid + 1]
    count, small_count = jnp.sum(full_counts), jnp.sum(small_counts)
    mean, entry_scale = join_stats(gathered[:, :mid], gathered[:, mid : 2 * mid], full_counts, count)
    entry_unit = (entry_raw - mean) * entry_scale
    entry_value, entry_slope = activate(entry_unit * entry_affine[0] + entry_affine[1])
    entry_act = (entry_value * mask).astype(BF16)
    above = edge(entry_act[:, -1:], 1)
    below = edge(entry_act[:, :1], -1)
    entry_padded = jnp.pad(jnp.concatenate([above, entry_act, below], axis=1), column_pad)
    middle_raw = conv_valid(entry_padded, middle_weight, 1)
    mean, middle_scale = norm_stats(middle_raw, mask, full_counts, mine, count)
    middle_unit = (middle_raw - mean) * middle_scale
    middle_value, middle_slope = activate(middle_unit * middle_affine[0] + middle_affine[1])
    middle_act = (middle_value * mask).astype(BF16)
    closing_raw = pointwise(middle_act, closing_weight)
    mean, closing_scale = norm_stats(closing_raw, mask, full_counts, mine, count)
    closing_unit = (closing_raw - mean) * closing_scale
    block_value, block_slope = activate(
        closing_unit * closing_affine[0] + closing_affine[1] + entry_in.astype(F32)
    )
    block_out = (block_value * mask).astype(BF16)

    widen_raw = pointwise(block_out, widen_weight)
    mean, widen_scale = norm_stats(widen_raw, mask, full_counts, mine, count)
    widen_unit = (widen_raw - mean) * widen_scale
    widen_value, widen_slope = activate(widen_unit * widen_affine[0] + widen_affine[1])
    widen_act = (widen_value * mask).astype(BF16)
    above = edge(widen_act[:, -1:], 1)
    strided_padded = jnp.pad(
        jnp.concatenate([above, widen_act], axis=1), ((0, 0), (0, 0), (1, 0), (0, 0))
    )
    strided_raw = conv_valid(strided_padded, strided_weight, 2)
    mean, strided_scale = norm_stats(strided_raw, small_mask, small_counts, mine_small, small_count)
    strided_unit = (strided_raw - mean) * strided_scale
    strided_value, strided_slope = activate(strided_unit * strided_affine[0] + strided_affine[1])
    strided_act = (strided_value * small_mask).astype(BF16)
    shortcut_in = block_out[:, ::2, ::2]
    expand_raw = pointwise(strided_act, expand_weight)
    shortcut_raw = pointwise(shortcut_in, shortcut_weight)

    row = lax.axis_index("row")
    raws = jnp.concatenate([expand_raw, shortcut_raw], axis=-1)
    total, square = local_stats(raws, small_mask, mine_small)
    pair = jnp.stack([total, square])
    half = total.shape[0] // 2
    low, high = pair[:, :half], pair[:, half:]
    own = jnp.where(row == 0, low, high)
    other = swap_rows(jnp.where(row == 0, high, low))
    pair_counts = small_counts.reshape(-1, lax.axis_size("row"))
    here = lax.axis_index("img")
    both = jnp.sum(lax.dynamic_index_in_dim(pair_counts, here, 0, keepdims=False))
    theirs = both - mine_small
    own_mean = own[0] / jnp.maximum(mine_small, 1.0)
    other_mean = other[0] / jnp.maximum(theirs, 1.0)
    gap = own_mean - other_mean
    joined = jnp.concatenate(
        [own[0] + other[0], own[1] + other[1] + gap * gap * (mine_small * theirs / jnp.maximum(both, 1.0))]
    )
    gathered = gather_img(joined)
    mean, scale = join_stats(
        gathered[:, :half], gathered[:, half:], jnp.sum(pair_counts, axis=1), small_count
    )
    packed = jnp.stack([mean, scale])
    other = swap_rows(packed)
    first = jnp.where(row == 0, packed, other)
    second = jnp.where(row == 0, other, packed)
    expand_unit = (expand_raw - first[0]) * first[1]
    shortcut_unit = (shortcut_raw - second[0]) * second[1]
    expand_scale, shortcut_scale = first[1], second[1]
    final_value, final_slope = activate(
        expand_unit * expand_affine[0]
        + expand_affine[1]
        + (shortcut_unit * shortcut_affine[0] + shortcut_affine[1])
    )
    features = (final_value * small_mask).astype(BF16)

    final_grad = cotangent.astype(F32) * small_mask * final_slope
    axes = (0, 1, 2)
    sums = sum_split(
        jnp.stack(
            [
                jnp.sum(final_grad * expand_unit, axis=axes),
                jnp.sum(final_grad * shortcut_unit, axis=axes),
                jnp.sum(final_grad, axis=axes),
            ]
        )
    )
    affine_expand = jnp.stack([sums[0], sums[2]])
    affine_shortcut = jnp.stack([sums[1], sums[2]])
    expand_grad = raw_grad(
        final_grad, expand_unit, expand_scale, sums[0], sums[2], small_mask, small_count, expand_affine
    )
    shortcut_grad = raw_grad(
        final_grad, shortcut_unit, shortcut_scale, sums[1], sums[2], small_mask, small_count, shortcut_affine
    )
    strided_back = pointwise_back(expand_grad, expand_weight) * small_mask * strided_slope
    last_own = jnp.concatenate([shortcut_grad, expand_grad], axis=-1)
    last_other = swap_rows(last_own)
    wide = shortcut_grad.shape[-1]
    short_left = jnp.concatenate(half_channels(shortcut_in), axis=1)
    expand_left = jnp.concatenate(half_channels(strided_act), axis=1)
    last_both = jnp.concatenate([last_own, last_other], axis=1)
    first_wave = jnp.concatenate(
        [
            weight_grad(short_left, last_both[..., :wide]).astype(BF16),
            weight_grad(expand_left, last_both[..., wide:]).astype(BF16),
        ],
        axis=0,
    )
    first_total = sum_over_chips(first_wave)

    strided_grad, affine_strided = norm_back(
        strided_back, strided_unit, strided_scale, small_mask, small_count, strided_affine
    )
    strided_all = in_order(strided_grad, swap_rows(strided_grad))
    spread_grad = lax.conv_general_dilated(
        strided_grad,
        flip_kernel(strided_weight),
        (1, 1),
        ((2, 2), (2, 2)),
        lhs_dilation=(2, 2),
        dimension_numbers=DIMS,
        preferred_element_type=F32,
    )
    spill = edge(spread_grad[:, :1, 1:].astype(BF16), -1).astype(F32)
    widen_back = spread_grad[:, 1:, 1:] + jnp.pad(spill, ((0, 0), (height - 1, 0), (0, 0), (0, 0)))
    widen_back = widen_back * mask * widen_slope
    widen_grad, affine_widen = norm_back(widen_back, widen_unit, widen_scale, mask, count, widen_affine)
    widen_left = jnp.pad(in_order(*half_channels(widen_act)), ((0, 0), (1, 0), (1, 0), (0, 0)))
    block_left = jnp.concatenate(half_channels(block_out), axis=1)
    second_wave = jnp.concatenate(
        tap_grads(widen_left, strided_all, 2)
        + [weight_grad(block_left, jnp.concatenate([widen_grad, swap_rows(widen_grad)], axis=1))],
        axis=0,
    ).astype(BF16)
    second_total = sum_over_chips(second_wave)

    short_spread = lax.pad(
        pointwise_back(shortcut_grad, shortcut_weight),
        F32(0),
        ((0, 0, 0), (0, 1, 1), (0, 1, 1), (0, 0, 0)),
    )
    block_back = (pointwise_back(widen_grad, widen_weight) + short_spread) * mask * block_slope
    closing_grad, affine_closing = norm_back(
        block_back, closing_unit, closing_scale, mask, count, closing_affine
    )
    middle_back = pointwise_back(closing_grad, closing_weight) * mask * middle_slope
    middle_grad, affine_middle = norm_back(
        middle_back, middle_unit, middle_scale, mask, count, middle_affine
    )
    middle_other = swap_rows(middle_grad)
    middle_all = in_order(middle_grad, middle_other)
    upper = row == 0
    above = jnp.where(upper, jnp.zeros_like(middle_other[:, -1:]), middle_other[:, -1:])
    below = jnp.where(upper, middle_other[:, :1], jnp.zeros_like(middle_other[:, :1]))
    grad_rim = jnp.concatenate([above, middle_grad, below], axis=1)
    entry_back = (
        conv_valid(jnp.pad(grad_rim, column_pad), flip_kernel(middle_weight), 1) * mask * entry_slope
    )
    entry_grad, affine_entry = norm_back(entry_back, entry_unit, entry_scale, mask, count, entry_affine)
    image_grads = ((block_back + pointwise_back(entry_grad, entry_weight)) * mask).astype(BF16)

    closing_left = jnp.concatenate(half_channels(middle_act), axis=1)
    closing_both = jnp.concatenate([closing_grad, swap_rows(closing_grad)], axis=1)
    entry_left = jnp.pad(in_order(*half_channels(entry_act)), ((0, 0), (1, 1), (1, 1), (0, 0)))
    image_left = jnp.concatenate(half_channels(entry_in), axis=1)
    block = closing_both.shape[-1] // 4
    third_wave = jnp.concatenate(
        tap_grads(entry_left, middle_all, 1)
        + [weight_grad(closing_left, closing_both[..., i * block : (i + 1) * block]) for i in range(4)],
        axis=0,
    ).astype(BF16)
    third_total = sum_over_chips(third_wave, axis=1)
    last_wave = weight_grad(
        image_left, jnp.concatenate([entry_grad, swap_rows(entry_grad)], axis=1)
    ).astype(BF16)
    entry_total = sum_over_chips_short(last_wave)

    short_rows = short_left.shape[-1]
    tap_rows = 9 * widen_left.shape[-1]
    shortcut_total = first_total[:short_rows].astype(F32)
    expand_total = first_total[short_rows:].astype(F32)
    strided_total = second_total[:tap_rows].astype(F32).reshape(3, 3, -1, second_total.shape[1])
    widen_total = second_total[tap_rows:].astype(F32)
    tap_rows = 9 * entry_left.shape[-1]
    middle_total = third_total[:tap_rows].astype(F32).reshape(3, 3, -1, third_total.shape[1])
    rest = third_total[tap_rows:].astype(F32)
    rows = closing_left.shape[-1]
    closing_total = jnp.concatenate([rest[i * rows : (i + 1) * rows] for i in range(4)], axis=1)
    return (
        features,
        image_grads,
        entry_total.astype(F32),
        middle_total,
        closing_total,
        widen_total,
        strided_total,
        expand_total,
        shortcut_total,
        affine_entry,
        affine_middle,
        affine_closing,
        affine_widen,
        affine_strided,
        affine_expand,
        affine_shortcut,
    )


def solution(mesh):
    image = P("img", "row", None, None)
    return jax.shard_map(
        per_device,
        mesh=mesh,
        in_specs=(image, P("img", None)) + (P(),) * 14 + (image,),
        out_specs=(
            image,
            image,
            P("row", None),
            P(None, None, "row", None),
            P("row", None),
            P("row", None),
            P(None, None, "row", None),
            P("row", None),
            P("row", None),
        )
        + (P(),) * 7,
        check_vma=False,
    )
```

```python
import functools
import math

import jax
import jax.numpy as jnp
from jax import lax
from jax.experimental import pallas as pl
from jax.experimental.pallas import tpu as pltpu
from jax.sharding import PartitionSpec as P

EPS = 1e-05
BOTH = ("img", "row")
F32 = jnp.float32
BF16 = jnp.bfloat16
LANES = 128
MIB = 1 << 20


def swap_rows(value):
    count = lax.axis_size("row")
    return lax.ppermute(value, "row", [(i, (i + 1) % count) for i in range(count)])


def gather_all(message):
    return lax.all_to_all(message, BOTH, 0, 0, tiled=True)


def gather_img(message):
    return lax.all_to_all(message, "img", 0, 0, tiled=True)


def orders():
    bits = lax.axis_size("img").bit_length() - 1
    ascending = list(range(bits))
    swapped = ascending[:]
    if bits > 1:
        swapped[0], swapped[1] = 1, 0
    return ascending, swapped


def permute_bit(value, bit):
    count = lax.axis_size("img")
    return lax.ppermute(value, "img", [(i, i ^ (1 << bit)) for i in range(count)])


class Late:
    def __init__(self, source, buffer, semaphores):
        self.buffer = buffer
        self.shape, self.ndim, self.dtype = buffer.shape, len(buffer.shape), buffer.dtype
        parts = parts_of(self.shape)
        if parts == 1:
            self.copies = [pltpu.make_async_copy(source, buffer, semaphores.at[0])]
        else:
            self.copies = [
                pltpu.make_async_copy(source.at[i], buffer.at[i], semaphores.at[i]) for i in range(parts)
            ]
        for copy in self.copies:
            copy.start()
        self.waiting = set(range(parts))

    def ready(self, part=None):
        for i in sorted(self.waiting):
            if part is None or i == part:
                self.copies[i].wait()
                self.waiting.remove(i)
        return self.buffer

    def __getitem__(self, index):
        first = index[0] if isinstance(index, tuple) else index
        part = first if isinstance(first, int) and len(self.copies) > 1 else None
        return self.ready(part)[index]


def parts_of(shape):
    return shape[0] if len(shape) >= 3 and shape[0] == 3 else 1


class Saved:
    def __init__(self, target, buffer, semaphore):
        self.target, self.buffer, self.semaphore, self.copy = target, buffer, semaphore, None
        self.shape, self.ndim, self.dtype = buffer.shape, len(buffer.shape), buffer.dtype

    def send(self):
        if self.copy is None:
            self.copy = pltpu.make_async_copy(self.buffer, self.target, self.semaphore)
            self.copy.start()

    def __getitem__(self, index):
        return self.buffer[index]

    def __setitem__(self, index, value):
        self.buffer[index] = value


def send(*results):
    for result in results:
        if isinstance(result, Saved):
            result.send()


def call(kernel, outs, *operands, scratch=(), smem=(), late=(), flops=0, keep=(), limit=24):
    late = [place for place in (range(len(operands)) if late is None else late) if place not in smem]
    saved = [place for place in range(len(outs)) if place not in keep]
    moved = sum(x.size * x.dtype.itemsize for x in operands) + sum(
        math.prod(shape) * jnp.dtype(dtype).itemsize for shape, dtype in outs
    )

    def place_of_operand(place):
        if place in smem:
            return pltpu.SMEM
        return pl.ANY if place in late else pltpu.VMEM

    operands = [
        pltpu.with_memory_space_constraint(x, pltpu.HBM) if place in late else x for place, x in enumerate(operands)
    ]
    buffers = [pltpu.VMEM(operands[place].shape, operands[place].dtype) for place in late]
    buffers += [pltpu.VMEM(*outs[place]) for place in saved]
    semaphores = [pltpu.SemaphoreType.DMA((parts_of(operands[place].shape),)) for place in late]
    semaphores += [pltpu.SemaphoreType.DMA] * len(saved)

    def body(*refs):
        refs = list(refs)
        inputs, refs = refs[: len(operands)], refs[len(operands) :]
        results, refs = refs[: len(outs)], refs[len(outs) :]
        own, refs = refs[: len(scratch)], refs[len(scratch) :]
        space, marks = refs[: len(buffers)], refs[len(buffers) :]
        for number, place in enumerate(late):
            inputs[place] = Late(inputs[place], space[number], marks[number])
        for number, place in enumerate(saved):
            number += len(late)
            results[place] = Saved(results[place], space[number], marks[number])
        kernel(*inputs, *results, *own)
        for place in late:
            inputs[place].ready()
        for place in saved:
            results[place].send()
        for place in saved:
            results[place].copy.wait()

    return pl.pallas_call(
        body,
        out_shape=[
            (pltpu.VMEM if place in keep else pltpu.HBM)(shape, dtype) for place, (shape, dtype) in enumerate(outs)
        ],
        in_specs=[pl.BlockSpec(memory_space=place_of_operand(place)) for place in range(len(operands))],
        out_specs=[
            pl.BlockSpec(memory_space=pltpu.VMEM if place in keep else pl.ANY) for place in range(len(outs))
        ],
        scratch_shapes=[pltpu.VMEM(shape, dtype) for shape, dtype in scratch] + buffers + semaphores,
        compiler_params=pltpu.CompilerParams(vmem_limit_bytes=limit * MIB),
        cost_estimate=pl.CostEstimate(flops=flops, bytes_accessed=moved, transcendentals=0),
    )(*operands)


def dot(left, right):
    return jnp.dot(left, right, preferred_element_type=F32)


def dot_back(grad, weight):
    return lax.dot_general(grad, weight, (((1,), (1,)), ((), ())), preferred_element_type=F32)


def wide(mask, width):
    return mask if width == LANES else jnp.concatenate([mask] * (width // LANES), axis=1)


def column_sum(value):
    return jnp.sum(value, axis=0, keepdims=True)


def spread_message(message, rows):
    tile = rows[...]
    for device in range(message.shape[0]):
        message[device] = tile


def put_row(rows, place, vector):
    for block in range(vector.shape[1] // LANES):
        rows[place + block : place + block + 1, :] = vector[:, block * LANES : (block + 1) * LANES]


def local_stats(raw, mask, rows, place=0):
    blocks = raw.shape[1] // LANES
    number = jnp.maximum(column_sum(mask[...]), 1.0)
    for block in range(blocks):
        columns = slice(block * LANES, (block + 1) * LANES)
        total = column_sum(raw[:, columns] * mask[...])
        centred = (raw[:, columns] - total / number) * mask[...]
        rows[place + block : place + block + 1, :] = total
        rows[place + blocks + block : place + blocks + block + 1, :] = column_sum(centred * centred)


def total_count(counts, place):
    return functools.reduce(
        jnp.add, [counts[i, place : place + 1, :] for i in range(counts.shape[0])]
    )


def join_stats(gathered, counts, place, stats, blocks):
    devices = gathered.shape[0]
    count = total_count(counts, place)
    mean = functools.reduce(jnp.add, [gathered[i, :blocks, :] for i in range(devices)]) / count
    spread = functools.reduce(jnp.add, [gathered[i, blocks : 2 * blocks, :] for i in range(devices)])
    for i in range(devices):
        number = counts[i, place : place + 1, :]
        shift = gathered[i, :blocks, :] / jnp.maximum(number, 1.0) - mean
        spread = spread + number * (shift * shift)
    scale = lax.rsqrt(spread / count + EPS)
    for block in range(blocks):
        columns = slice(block * LANES, (block + 1) * LANES)
        stats[0:1, columns] = mean[block : block + 1, :]
        stats[1:2, columns] = scale[block : block + 1, :]


def join_sums(gathered, affine):
    total = functools.reduce(jnp.add, [gathered[i] for i in range(gathered.shape[0])])
    blocks = affine.shape[1] // LANES
    for block in range(blocks):
        columns = slice(block * LANES, (block + 1) * LANES)
        affine[0:1, columns] = total[block : block + 1, :]
        affine[1:2, columns] = total[blocks + block : blocks + block + 1, :]


def chunks(rows, width, chunk=32, block=256):
    for start in range(0, width, block):
        for row in range(0, rows, chunk):
            yield slice(row, row + min(chunk, rows - row)), slice(start, start + min(block, width - start))


def silu_parts(value):
    gate = jax.nn.sigmoid(value)
    return value * gate, gate * (1.0 + value * (1.0 - gate))


def normed(raw, stats, params, columns):
    unit = (raw - stats[0:1, columns]) * stats[1:2, columns]
    return unit, unit * params[0:1, columns] + params[1:2, columns]


def act_pass(raw, mask, stats, params, unit, slope, act, skip=None, keep=None):
    rows, width = raw.shape
    for here, columns in chunks(rows, width):
        u, value = normed(raw[here, columns], stats, params, columns)
        if skip is not None:
            value = value + skip[here, columns].astype(F32)
        m = wide(mask[here, :], columns.stop - columns.start)
        out, rise = silu_parts(value)
        out = out * m
        unit[here, columns] = u
        slope[here, columns] = rise * m
        if act is not None:
            act[here, columns] = out.astype(BF16)
        if keep is not None:
            keep(here, columns, out)


def back_pass(back, unit, slope, rows):
    blocks = back.shape[1] // LANES
    for block in range(blocks):
        columns = slice(block * LANES, (block + 1) * LANES)
        value = back[:, columns] * slope[:, columns]
        back[:, columns] = value
        rows[block : block + 1, :] = column_sum(value * unit[:, columns])
        rows[blocks + block : blocks + block + 1, :] = column_sum(value)


def raw_grad(back, unit, mask, sums, stats, params, count, columns):
    width = columns.stop - columns.start
    n = wide(count, width)
    factor = params[0:1, columns] * stats[1:2, columns]
    centred = back - sums[1:2, columns] / n - unit * (sums[0:1, columns] / n)
    return factor * centred * wide(mask, width)


def grad_pass(back, unit, mask, sums, stats, params, count, grad, keep=None):
    for here, columns in chunks(*back.shape):
        value = raw_grad(
            back[here, columns], unit[here, columns], mask[here, :], sums, stats, params, count, columns
        )
        grad[here, columns] = value.astype(BF16)
        if keep is not None:
            keep(here, columns, value)


def valid(extents, image, first_row, columns, shape, step):
    place = lax.broadcasted_iota(jnp.int32, shape, 0)
    row = first_row + step * (place // columns)
    column = step * (place % columns)
    return jnp.where((row < extents[image, 0]) & (column < extents[image, 1]), 1.0, 0.0).astype(F32)


def own_half(core, size):
    return pl.ds(pl.multiple_of(core[0] * size, LANES), size)


def other_half(core, size):
    return pl.ds(pl.multiple_of((1 - core[0]) * size, LANES), size)


def give_half(core, value, give):
    give[...] = value[:, other_half(core, give.shape[1])]
    send(give)


def entry_kernel(
    dims, extents, flag, core, images, weight,
    entry_in, mask, small, above, below, small_below, raw, edge, message, give, rows,
):
    batch, height, width = dims
    pixels = height * width
    upper = flag[0]
    for b in range(batch):
        mask[b * pixels : (b + 1) * pixels, :] = valid(extents, b, 0, width, (pixels, LANES), 1)
        small[b * pixels // 4 : (b + 1) * pixels // 4, :] = valid(
            extents, b, 0, width // 2, (pixels // 4, LANES), 2
        )
        line = slice(b * width, (b + 1) * width)
        above[line, :] = valid(extents, b, -1, width, (width, LANES), 1) * (1.0 - upper)
        below[line, :] = valid(extents, b, height, width, (width, LANES), 1) * upper
        small_below[b * width // 2 : (b + 1) * width // 2, :] = (
            valid(extents, b, height, width // 2, (width // 2, LANES), 2) * upper
        )
    for here, columns in chunks(*images.shape):
        m = wide(mask[here, :], columns.stop - columns.start)
        entry_in[here, columns] = (images[here, columns].astype(F32) * m).astype(BF16)
    send(entry_in, mask, small, above, below, small_below)
    give_half(core, entry_in, give)
    raw[...] = dot(entry_in[...], weight[...])
    for b in range(batch):
        first = raw[b * pixels : b * pixels + width, :]
        last = raw[(b + 1) * pixels - width : (b + 1) * pixels, :]
        edge[b * width : (b + 1) * width, :] = last * upper + first * (1.0 - upper)
    rows[...] = jnp.zeros_like(rows)
    local_stats(raw, mask, rows)
    blocks = raw.shape[1] // LANES
    rows[2 * blocks : 2 * blocks + 1, :] = column_sum(mask[...])
    rows[2 * blocks + 1 : 2 * blocks + 2, :] = column_sum(small[...])
    spread_message(message, rows)


def put_blocks(target, here, columns, value):
    for start in range(columns.start, columns.stop, LANES):
        offset = start - columns.start
        target[start // LANES, here, :] = value[:, offset : offset + LANES]


def column_masks(rows, width):
    place = lax.broadcasted_iota(jnp.int32, (rows, LANES), 0) % width
    return (
        jnp.where(place == 0, 0.0, 1.0).astype(F32),
        jnp.where(place == width - 1, 0.0, 1.0).astype(F32),
    )


def fill_triple(padded, triple, batch, lines, width):
    size = lines * width
    channels = padded.shape[1]
    left_ok, right_ok = column_masks(size, width)
    for b in range(batch):
        start = 8 + b * size
        for c in range(0, channels, LANES):
            columns = slice(c, c + LANES)
            triple[b, :, c : c + LANES] = (padded[start - 1 : start - 1 + size, columns] * left_ok).astype(BF16)
            triple[b, :, channels + c : channels + c + LANES] = padded[start : start + size, columns].astype(BF16)
            triple[b, :, 2 * channels + c : 2 * channels + c + LANES] = (
                padded[start + 1 : start + 1 + size, columns] * right_ok
            ).astype(BF16)


def middle_kernel(
    dims, core, gathered, raw, halo, mask, above, below, params, weight,
    unit, slope, stats, out, message, triple, give, rows, padded,
):
    batch, height, width = dims
    pixels = height * width
    size = pixels + 2 * width
    blocks = raw.shape[1] // LANES
    join_stats(gathered, gathered, 2 * blocks, stats, blocks)
    everything = slice(0, raw.shape[1])
    _, value = normed(halo[...], stats, params, everything)
    rim, _ = silu_parts(value)
    padded[0:8, :] = jnp.zeros((8, raw.shape[1]), F32)
    padded[8 + batch * size :, :] = jnp.zeros((8, raw.shape[1]), F32)
    for b in range(batch):
        line = slice(b * width, (b + 1) * width)
        top = 8 + b * size
        padded[top : top + width, :] = rim[line] * wide(above[line, :], raw.shape[1])
        padded[top + size - width : top + size, :] = rim[line] * wide(below[line, :], raw.shape[1])

    def keep(here, columns, value):
        b = here.start // pixels
        start = 8 + b * size + width + here.start - b * pixels
        padded[start : start + here.stop - here.start, columns] = value

    act_pass(raw, mask, stats, params, unit, slope, None, keep=keep)
    send(unit, slope, stats)
    fill_triple(padded, triple, batch, height + 2, width)
    send(triple)
    give_taps(core, triple, give)
    total = None
    for tap in range(3):
        left = triple[:, tap * width : tap * width + pixels, :].reshape(batch * pixels, -1)
        part = dot(left, weight[tap])
        total = part if total is None else total + part
    out[...] = total
    local_stats(out, mask, rows)
    spread_message(message, rows)


def give_taps(core, taps, give):
    full, half = taps.shape[2] // 3, give.shape[2] // 3
    for tap in range(3):
        start = pl.multiple_of(tap * full + (1 - core[0]) * half, LANES)
        give[:, :, tap * half : (tap + 1) * half] = taps[:, :, pl.ds(start, half)]
    send(give)


def closing_kernel(
    core, gathered, counts, raw, mask, params, weight, act, unit, slope, stats, out, message, give, rows
):
    blocks = raw.shape[1] // LANES
    join_stats(gathered, counts, 4, stats, blocks)
    act_pass(raw, mask, stats, params, unit, slope, act)
    send(unit, slope, act, stats)
    give_half(core, act, give)
    out[...] = dot(act[...], weight[...])
    local_stats(out, mask, rows)
    spread_message(message, rows)


def widen_kernel(
    dims, core, gathered, counts, raw, entry_in, mask, params, weight,
    act, unit, slope, stats, short, out, edge, message, give, give_short, rows, even,
):
    batch, height, width = dims
    pixels = height * width
    blocks = raw.shape[1] // LANES
    join_stats(gathered, counts, 4, stats, blocks)

    def keep(here, columns, value):
        put_blocks(even, here, columns, value)

    act_pass(raw, mask, stats, params, unit, slope, act, skip=entry_in, keep=keep)
    send(unit, slope, act, stats)
    give_half(core, act, give)
    out[...] = dot(act[...], weight[...])
    for b in range(batch):
        edge[b * width : (b + 1) * width, :] = out[(b + 1) * pixels - width : (b + 1) * pixels, :]
    local_stats(out, mask, rows)
    spread_message(message, rows)
    for c in range(0, raw.shape[1], LANES):
        columns = slice(c, c + LANES)
        lines = []
        for b in range(batch):
            for i in range(height // 2):
                lines.append(even[c // LANES, pl.ds(b * pixels + 2 * i * width, width // 2, stride=2), :])
        short[:, columns] = jnp.concatenate(lines, axis=0).astype(BF16)
    send(short)
    give_half(core, short, give_short)


def shortcut_kernel(short, small, weight, out, rows):
    out[...] = dot(short[...], weight[...])
    send(out)
    local_stats(out, small, rows)


def strided_kernel(
    dims, core, gathered, counts, raw, halo, mask, small, above, params, weight,
    unit, slope, stats, out, message, taps, give, rows, padded,
):
    batch, height, width = dims
    pixels = height * width
    size = pixels + width
    half, half_width = height // 2, width // 2
    blocks = raw.shape[1] // LANES
    join_stats(gathered, counts, 4, stats, blocks)
    everything = slice(0, raw.shape[1])
    _, value = normed(halo[...], stats, params, everything)
    rim, _ = silu_parts(value)
    for block in range(padded.shape[0]):
        padded[block, 0:8, :] = jnp.zeros((8, LANES), F32)
    for b in range(batch):
        line = slice(b * width, (b + 1) * width)
        start = 8 + b * size
        put_blocks(padded, slice(start, start + width), everything, rim[line] * wide(above[line, :], raw.shape[1]))

    def keep(here, columns, value):
        b = here.start // pixels
        start = 8 + b * size + width + here.start - b * pixels
        put_blocks(padded, slice(start, start + here.stop - here.start), columns, value)

    act_pass(raw, mask, stats, params, unit, slope, None, keep=keep)
    send(unit, slope, stats)
    lines = height + 1
    not_first, _ = column_masks(lines * half_width, half_width)
    channels = raw.shape[1]
    for block in range(channels // LANES):
        for b in range(batch):
            start = 8 + b * size
            before = padded[block, pl.ds(start - 1, lines * half_width, stride=2), :] * not_first
            at = padded[block, pl.ds(start, lines * half_width, stride=2), :]
            after = padded[block, pl.ds(start + 1, lines * half_width, stride=2), :]
            for k, value in enumerate((before, at, after)):
                value = value.reshape(lines, half_width, LANES)
                place = k * channels + block * LANES
                for tap in range(3):
                    pieces = [value[tap + 2 * i] for i in range(half)]
                    taps[tap, b * half * half_width : (b + 1) * half * half_width, place : place + LANES] = (
                        jnp.concatenate(pieces, axis=0).astype(BF16)
                    )
    send(taps)
    give_taps(core, taps, give)
    total = None
    for tap in range(3):
        part = dot(taps[tap], weight[tap])
        total = part if total is None else total + part
    out[...] = total
    local_stats(out, small, rows)
    spread_message(message, rows)


def expand_kernel(
    gathered, counts, raw, small, params, weight, short_rows, flag, core,
    act, unit, slope, stats, out, mine, theirs, give, rows,
):
    blocks = raw.shape[1] // LANES
    join_stats(gathered, counts, 5, stats, blocks)
    act_pass(raw, small, stats, params, unit, slope, act)
    send(unit, slope, act, stats)
    give_half(core, act, give)
    out[...] = dot(act[...], weight[...])
    local_stats(out, small, rows)
    upper = flag[0]
    size = rows.shape[0]
    number = jnp.broadcast_to(column_sum(small[...]), (8, LANES))
    mine[:size, :] = rows[...] * upper + short_rows[...] * (1.0 - upper)
    theirs[:size, :] = rows[...] * (1.0 - upper) + short_rows[...] * upper
    mine[size:, :] = number
    theirs[size:, :] = number


def pair_kernel(mine, other, message):
    size = mine.shape[0] - 8
    blocks = size // 2
    first, second = mine[size : size + 1, :], other[size : size + 1, :]
    both = first + second
    gap = mine[:blocks, :] / jnp.maximum(first, 1.0) - other[:blocks, :] / jnp.maximum(second, 1.0)
    weight = first * second / jnp.maximum(both, 1.0)
    total = mine[:blocks, :] + other[:blocks, :]
    square = mine[blocks:size, :] + other[blocks:size, :] + gap * gap * weight
    number = jnp.broadcast_to(both, (8, LANES))
    for i in range(message.shape[0]):
        message[i, :blocks, :] = total
        message[i, blocks:size, :] = square
        message[i, size:, :] = number


def join_kernel(gathered, stats):
    size = gathered.shape[1] - 8
    stats[...] = jnp.zeros_like(stats)
    join_stats(gathered, gathered, size, stats, size // 2)


def final_kernel(
    own, other, flag, expand_raw, short_raw, small, expand_params, short_params, cotangent,
    features, grad, expand_unit, short_unit, expand_stats, short_stats, mine, theirs, rows,
):
    upper = flag[0]
    expand_stats[...] = own[...] * upper + other[...] * (1.0 - upper)
    short_stats[...] = own[...] * (1.0 - upper) + other[...] * upper
    height, width = expand_raw.shape
    blocks = width // LANES
    for block in range(blocks):
        columns = slice(block * LANES, (block + 1) * LANES)
        first, first_value = normed(expand_raw[:, columns], expand_stats, expand_params, columns)
        second, second_value = normed(short_raw[:, columns], short_stats, short_params, columns)
        out, rise = silu_parts(first_value + second_value)
        features[:, columns] = (out * small[...]).astype(BF16)
        value = cotangent[:, columns].astype(F32) * (rise * small[...])
        grad[:, columns] = value
        expand_unit[:, columns] = first
        short_unit[:, columns] = second
        rows[block : block + 1, :] = column_sum(value * first)
        rows[blocks + block : blocks + block + 1, :] = column_sum(value * second)
        rows[2 * blocks + block : 2 * blocks + block + 1, :] = column_sum(value)
    half = blocks // 2
    for stat in range(3):
        low = rows[stat * blocks : stat * blocks + half, :]
        high = rows[stat * blocks + half : (stat + 1) * blocks, :]
        mine[stat * half : (stat + 1) * half, :] = low * upper + high * (1.0 - upper)
        theirs[stat * half : (stat + 1) * half, :] = low * (1.0 - upper) + high * upper


def last_grads_kernel(
    batch, own, other, flag, counts, grad, expand_unit, short_unit, expand_stats, short_stats,
    expand_params, short_params, small, weight, slope, unit,
    expand_affine, short_affine, expand_grad, short_grad, back, edge, message, rows,
):
    upper = flag[0]
    half = own.shape[0] // 3
    for stat in range(3):
        part = slice(stat * half, (stat + 1) * half)
        low = own[part, :] * upper + other[part, :] * (1.0 - upper)
        high = own[part, :] * (1.0 - upper) + other[part, :] * upper
        for block in range(2 * half):
            value = low[block : block + 1, :] if block < half else high[block - half : block - half + 1, :]
            columns = slice(block * LANES, (block + 1) * LANES)
            if stat == 0:
                expand_affine[0:1, columns] = value
            elif stat == 1:
                short_affine[0:1, columns] = value
            else:
                expand_affine[1:2, columns] = value
                short_affine[1:2, columns] = value
    count = total_count(counts, 5)
    for here, columns in chunks(*grad.shape):
        expand_grad[here, columns] = raw_grad(
            grad[here, columns], expand_unit[here, columns], small[here, :], expand_affine, expand_stats,
            expand_params, count, columns,
        ).astype(BF16)
        short_grad[here, columns] = raw_grad(
            grad[here, columns], short_unit[here, columns], small[here, :], short_affine, short_stats,
            short_params, count, columns,
        ).astype(BF16)
    send(expand_grad, short_grad, expand_affine, short_affine)
    back[...] = dot_back(expand_grad[...], weight[...])
    back_pass(back, unit, slope, rows)
    spread_message(message, rows)
    pixels = back.shape[0] // batch
    line = edge.shape[0] // (2 * batch)
    for b in range(batch):
        edge[b * line : (b + 1) * line, :] = back[b * pixels : b * pixels + line, :]
        edge[(batch + b) * line : (batch + b + 1) * line, :] = unit[b * pixels : b * pixels + line, :]


def short_back_kernel(dims, grad, weight, out):
    batch, height, width = dims
    pixels = height * width
    small = dot_back(grad[...], weight[...])
    out[...] = jnp.zeros(out.shape, out.dtype)
    half = width // 2
    for block in range(out.shape[0]):
        columns = slice(block * LANES, (block + 1) * LANES)
        for b in range(batch):
            for i in range(height // 2):
                place = b * pixels // 4 + i * half
                start = b * pixels + 2 * i * width
                out[block, pl.ds(start, half, stride=2), :] = small[place : place + half, columns]


def widen_back_kernel(
    dims, gathered, counts, back, unit, halo, small, small_below, stats, params, weight, out_unit, out_slope,
    affine, grad, out, message, rows, padded, full,
):
    batch, height, width = dims
    pixels = height * width
    half, half_width = height // 2, width // 2
    size = (half + 1) * half_width
    join_sums(gathered, affine)
    count = total_count(counts, 5)
    channels = back.shape[1]
    everything = slice(0, channels)
    line = batch * half_width
    rim = raw_grad(
        halo[:line, :], halo[line:, :], small_below[...], affine, stats, params, count, everything
    ).astype(BF16).astype(F32)
    for b in range(batch):
        stop = (b + 1) * size
        padded[stop - half_width : stop, :] = rim[b * half_width : (b + 1) * half_width]
    padded[batch * size :, :] = jnp.zeros((8, channels), F32)
    small_pixels = half * half_width
    for here, columns in chunks(back.shape[0], channels, chunk=small_pixels):
        value = raw_grad(
            back[here, columns], unit[here, columns], small[here, :], affine, stats, params, count, columns
        ).astype(BF16)
        grad[here, columns] = value
        b = here.start // small_pixels
        padded[b * size : b * size + small_pixels, columns] = value.astype(F32)
    send(grad, affine)
    _, not_last = column_masks(small_pixels, half_width)
    not_last = wide(not_last, channels)

    def moved(down, right):
        pieces = []
        for b in range(batch):
            start = b * size + down * half_width + right
            piece = padded[start : start + small_pixels, :]
            pieces.append(piece * not_last if right else piece)
        return jnp.concatenate(pieces, axis=0).astype(BF16)

    here, right, down, across = moved(0, 0), moved(0, 1), moved(1, 0), moved(1, 1)
    phases = {
        (0, 0): dot_back(here, weight[1, 1]),
        (0, 1): dot_back(here, weight[1, 2]) + dot_back(right, weight[1, 0]),
        (1, 0): dot_back(here, weight[2, 1]) + dot_back(down, weight[0, 1]),
        (1, 1): dot_back(here, weight[2, 2])
        + dot_back(right, weight[2, 0])
        + dot_back(down, weight[0, 2])
        + dot_back(across, weight[0, 0]),
    }
    for (a, e), value in phases.items():
        for b in range(batch):
            for i in range(half):
                place = b * small_pixels + i * half_width
                start = b * pixels + (2 * i + a) * width + e
                for block in range(full.shape[0]):
                    full[block, pl.ds(start, half_width, stride=2), :] = value[
                        place : place + half_width, block * LANES : (block + 1) * LANES
                    ]
    for block in range(full.shape[0]):
        out[:, block * LANES : (block + 1) * LANES] = full[block]
    back_pass(out, out_unit, out_slope, rows)
    spread_message(message, rows)


def block_back_kernel(
    gathered, counts, back, unit, mask, stats, params, weight, short_back, out_unit, out_slope,
    affine, grad, out, message, again, rows,
):
    join_sums(gathered, affine)
    grad_pass(back, unit, mask, affine, stats, params, total_count(counts, 4), grad)
    send(grad, affine)
    short = jnp.concatenate([short_back[block] for block in range(short_back.shape[0])], axis=1)
    out[...] = dot_back(grad[...], weight[...]) + short
    back_pass(out, out_unit, out_slope, rows)
    again[...] = out[...]
    send(again)
    spread_message(message, rows)


def middle_back_kernel(
    dims, flag, gathered, counts, back, unit, mask, stats, params, weight, out_unit, out_slope,
    affine, grad, out, edge, message, rows,
):
    batch, height, width = dims
    pixels = height * width
    upper = flag[0]
    join_sums(gathered, affine)
    grad_pass(back, unit, mask, affine, stats, params, total_count(counts, 4), grad)
    send(grad, affine)
    out[...] = dot_back(grad[...], weight[...])
    back_pass(out, out_unit, out_slope, rows)
    spread_message(message, rows)
    for place, source in ((0, out), (batch, out_unit)):
        for b in range(batch):
            first = source[b * pixels : b * pixels + width, :]
            last = source[(b + 1) * pixels - width : (b + 1) * pixels, :]
            edge[(place + b) * width : (place + b + 1) * width, :] = last * upper + first * (1.0 - upper)


def entry_back_kernel(
    dims, gathered, counts, back, unit, halo, mask, above, below, stats, params, weight, out_unit, out_slope,
    affine, grad, out, message, rows, padded, triple,
):
    batch, height, width = dims
    pixels = height * width
    size = pixels + 2 * width
    join_sums(gathered, affine)
    count = total_count(counts, 4)
    channels = back.shape[1]
    everything = slice(0, channels)
    line = batch * width
    padded[0:8, :] = jnp.zeros((8, channels), F32)
    padded[8 + batch * size :, :] = jnp.zeros((8, channels), F32)
    up = raw_grad(halo[:line, :], halo[line:, :], above[...], affine, stats, params, count, everything)
    down = raw_grad(halo[:line, :], halo[line:, :], below[...], affine, stats, params, count, everything)
    for b in range(batch):
        here = slice(b * width, (b + 1) * width)
        top = 8 + b * size
        padded[top : top + width, :] = up[here]
        padded[top + size - width : top + size, :] = down[here]

    def keep(here, columns, value):
        b = here.start // pixels
        start = 8 + b * size + width + here.start - b * pixels
        padded[start : start + here.stop - here.start, columns] = value

    grad_pass(back, unit, mask, affine, stats, params, count, grad, keep=keep)
    send(grad, affine)
    fill_triple(padded, triple, batch, height + 2, width)
    total = None
    for row_tap in range(3):
        shift = (2 - row_tap) * width
        for col_tap in range(3):
            side = (2 - col_tap) * channels
            left = triple[:, shift : shift + pixels, side : side + channels].reshape(batch * pixels, channels)
            part = dot_back(left, weight[row_tap, col_tap])
            total = part if total is None else total + part
    out[...] = total
    back_pass(out, out_unit, out_slope, rows)
    spread_message(message, rows)


def images_kernel(gathered, counts, back, unit, mask, stats, params, weight, block_back, affine, grad, out):
    join_sums(gathered, affine)
    grad_pass(back, unit, mask, affine, stats, params, total_count(counts, 4), grad)
    send(grad, affine)
    step = 256
    for start in range(0, out.shape[1], step):
        columns = slice(start, start + step)
        value = dot_back(grad[...], weight[columns, :]) + block_back[:, columns]
        out[:, columns] = (value * wide(mask[...], step)).astype(BF16)


def dot_pixels(left, grad):
    return lax.dot_general(left, grad, (((0,), (0,)), ((), ())), preferred_element_type=F32)


def chip_grad(core, left, left_other, grad, grad_other, columns=slice(None)):
    half = left_other.shape[1]
    return dot_pixels(left[:, own_half(core, half)], grad[:, columns]) + dot_pixels(
        left_other[...], grad_other[:, columns]
    )


def deal(place, full, kept, sent):
    groups = len(kept)
    rows, width = full.shape[0] // 2, full.shape[1] // groups
    for group in range(groups):
        columns = slice(group * width, (group + 1) * width)
        mine = place[group]
        sent[group][...] = full[pl.ds(pl.multiple_of((1 - mine) * rows, 16), rows), columns]
        send(sent[group])
        kept[group][...] = full[pl.ds(pl.multiple_of(mine * rows, 16), rows), columns]
        send(kept[group])


def first_wave_kernel(
    core, place, short, short_other, strided, strided_other,
    short_grad, short_grad_other, expand_grad, expand_grad_other,
    kept_a, kept_b, sent_a, sent_b, full,
):
    rows = short_other.shape[1]
    step = 512
    for start in range(0, full.shape[1], step):
        columns = slice(start, start + step)
        full[:rows, columns] = chip_grad(
            core, short, short_other, short_grad, short_grad_other, columns
        ).astype(BF16)
        full[rows:, columns] = chip_grad(
            core, strided, strided_other, expand_grad, expand_grad_other, columns
        ).astype(BF16)
    deal(place, full, (kept_a, kept_b), (sent_a, sent_b))


def second_wave_kernel(
    core, place, taps, taps_other, strided_grad, strided_grad_other, block, block_other, widen_grad, widen_grad_other,
    kept_a, kept_b, sent_a, sent_b, full,
):
    half = taps_other.shape[2] // 3
    channels = 2 * half
    for row_tap in range(3):
        for col_tap in range(3):
            start = pl.multiple_of(col_tap * channels + core[0] * half, LANES)
            own = dot_pixels(taps[row_tap, :, pl.ds(start, half)], strided_grad[...])
            other = dot_pixels(
                taps_other[row_tap, :, col_tap * half : (col_tap + 1) * half], strided_grad_other[...]
            )
            place_row = (3 * row_tap + col_tap) * half
            full[place_row : place_row + half, :] = (own + other).astype(BF16)
    full[9 * half :, :] = chip_grad(core, block, block_other, widen_grad, widen_grad_other).astype(BF16)
    deal(place, full, (kept_a, kept_b), (sent_a, sent_b))


def third_wave_kernel(
    dims, core, place, triple, triple_other, middle_grad, middle_grad_other, act, act_other, closing_grad, closing_grad_other,
    kept_a, kept_b, sent_a, sent_b, full,
):
    batch, height, width = dims
    pixels = height * width
    half = triple_other.shape[2] // 3
    channels = 2 * half
    for row_tap in range(3):
        lines = slice(row_tap * width, row_tap * width + pixels)
        for col_tap in range(3):
            start = pl.multiple_of(col_tap * channels + core[0] * half, LANES)
            own = triple[:, lines, pl.ds(start, half)].reshape(batch * pixels, half)
            other = triple_other[:, lines, col_tap * half : (col_tap + 1) * half].reshape(batch * pixels, half)
            value = dot_pixels(own, middle_grad[...]) + dot_pixels(other, middle_grad_other[...])
            place_row = (3 * row_tap + col_tap) * half
            full[place_row : place_row + half, :] = value.astype(BF16)
    step = full.shape[1]
    for block in range(closing_grad.shape[1] // step):
        columns = slice(block * step, (block + 1) * step)
        start = (9 + block) * half
        full[start : start + half, :] = chip_grad(
            core, act, act_other, closing_grad, closing_grad_other, columns
        ).astype(BF16)
    used = (9 + closing_grad.shape[1] // step) * half
    if used < full.shape[0]:
        full[used:, :] = jnp.zeros((full.shape[0] - used, step), BF16)
    deal(place, full, (kept_a, kept_b), (sent_a, sent_b))


def last_wave_kernel(core, entry_in, entry_in_other, grad, grad_other, out):
    out[...] = chip_grad(core, entry_in, entry_in_other, grad, grad_other).astype(BF16)


def add_halves(first, second):
    return (first.astype(F32) + second.astype(F32)).astype(BF16)


def fold_kernel(groups, place, *refs):
    kept, got, keep, pass_on = (refs[i * groups : (i + 1) * groups] for i in range(4))
    for group in range(groups):
        rows = keep[group].shape[-2]
        for mine, out in ((1 - place[group], pass_on[group]), (place[group], keep[group])):
            here = pl.ds(pl.multiple_of(mine * rows, 16), rows)
            if kept[group].ndim == 3:
                out[...] = add_halves(kept[group][:, here, :], got[group][:, here, :])
            else:
                out[...] = add_halves(kept[group][here, :], got[group][here, :])
            send(out)


def add_kernel(kept, got, out):
    out[...] = add_halves(kept[...], got[...])


def merge_kernel(groups, place, *refs):
    own, got, out = (refs[i * groups : (i + 1) * groups] for i in range(3))
    for group in range(groups):
        rows = own[group].shape[-2]
        for mine, value in ((place[group], own[group]), (1 - place[group], got[group])):
            here = pl.ds(pl.multiple_of(mine * rows, 16), rows)
            if own[group].ndim == 3:
                out[group][:, here, :] = value[...]
            else:
                out[group][here, :] = value[...]


def fill(place, own, got, full):
    width = full.shape[1] // len(own)
    for group in range(len(own)):
        columns = slice(group * width, (group + 1) * width)
        rows = own[group].shape[0]
        for mine, value in ((place[group], own[group]), (1 - place[group], got[group])):
            full[pl.ds(pl.multiple_of(mine * rows, 16), rows), columns] = value[...]


def first_out_kernel(place, own_a, own_b, got_a, got_b, short, expand, full):
    fill(place, (own_a, own_b), (got_a, got_b), full)
    rows = short.shape[0]
    short[...] = full[:rows, :].astype(F32)
    send(short)
    expand[...] = full[rows:, :].astype(F32)


def second_out_kernel(place, own_a, own_b, got_a, got_b, strided, widen, full):
    fill(place, (own_a, own_b), (got_a, got_b), full)
    rows = strided.shape[1]
    for tap in range(9):
        strided[tap] = full[tap * rows : (tap + 1) * rows, :].astype(F32)
    send(strided)
    widen[...] = full[9 * rows :, :].astype(F32)


def third_out_kernel(place, own_a, own_b, got_a, got_b, middle, closing, full):
    fill(place, (own_a, own_b), (got_a, got_b), full)
    rows = middle.shape[1]
    for tap in range(9):
        middle[tap] = full[tap * rows : (tap + 1) * rows, :].astype(F32)
    step = full.shape[1]
    for block in range(closing.shape[1] // step):
        start = (9 + block) * rows
        closing[:, block * step : (block + 1) * step] = full[start : start + rows, :].astype(F32)


def place_of(bits):
    here = lax.axis_index("img")
    return jnp.stack([(here >> bit) & 1 for bit in bits]).astype(jnp.int32)


def stack_pair(pair):
    return [jnp.stack(pair)]


def sum_over_chips(kept, sent, out_kernel, outs, full):
    steps = list(zip(*orders()))
    halvings = 1
    while halvings < len(steps) and kept[0].shape[0] % (16 << halvings) == 0:
        halvings += 1
    merged = False
    for number, bits in enumerate(steps):
        got = [permute_bit(value, bit) for value, bit in zip(sent, bits)]
        following = steps[number + 1] if number + 1 < len(steps) else None
        if following is not None and following[0] == following[1] and not merged:
            kept, got, merged = stack_pair(kept), stack_pair(got), True
        groups = len(kept)
        if number + 1 >= halvings:
            kept = sent = [
                call(add_kernel, [(one.shape, BF16)], one, other, late=None)[0] for one, other in zip(kept, got)
            ]
            continue
        shapes = [value.shape[:-2] + (value.shape[-2] // 2, value.shape[-1]) for value in kept]
        results = call(
            functools.partial(fold_kernel, groups),
            [(shape, BF16) for shape in shapes] * 2,
            place_of(following[:groups]),
            *kept,
            *got,
            smem=(0,),
            late=None,
        )
        kept, sent = results[:groups], results[groups:]
    own = kept
    for number, bits in reversed(list(enumerate(steps[:halvings]))):
        if bits[0] != bits[1] and merged:
            own, merged = [own[0][0], own[0][1]], False
        got = [permute_bit(value, bit) for value, bit in zip(own, bits)]
        groups = len(own)
        if number == 0:
            return call(
                out_kernel, outs, place_of(bits), *own, *got, smem=(0,), scratch=[(full, BF16)], late=None
            )
        shapes = [value.shape[:-2] + (value.shape[-2] * 2, value.shape[-1]) for value in own]
        own = call(
            functools.partial(merge_kernel, groups),
            [(shape, BF16) for shape in shapes],
            place_of(bits[:groups]),
            *own,
            *got,
            smem=(0,),
            late=None,
        )


def sum_over_chips_short(parts):
    members = lax.axis_size("img")
    moved = lax.all_to_all(parts, "img", 0, 0, tiled=True)
    share = jnp.sum(moved.astype(F32), axis=0).astype(BF16)
    spread = jnp.broadcast_to(share[None], (members,) + share.shape)
    return lax.all_to_all(spread, "img", 0, 0, tiled=True).reshape(-1, parts.shape[-1])


def per_device(
    images,
    extents,
    entry_weight,
    middle_weight,
    closing_weight,
    widen_weight,
    strided_weight,
    expand_weight,
    shortcut_weight,
    entry_affine,
    middle_affine,
    closing_affine,
    widen_affine,
    strided_affine,
    expand_affine,
    shortcut_affine,
    cotangent,
):
    batch, height, width, wide_in = images.shape
    dims = (batch, height, width)
    pixels = batch * height * width
    small_pixels = pixels // 4
    chips = lax.axis_size("img")
    devices = chips * lax.axis_size("row")
    row = lax.axis_index("row")
    upper = row == 0
    flag = jnp.where(upper, 1.0, 0.0).astype(F32).reshape(1)
    core = row.astype(jnp.int32).reshape(1)
    local = extents - jnp.stack([row * height, 0]).astype(jnp.int32)
    mid, wider, last = entry_weight.shape[1], widen_weight.shape[1], expand_weight.shape[1]

    def message_rows(channels):
        return max(8, 2 * channels // LANES)

    def message(channels):
        return ((devices, message_rows(channels), LANES), F32)

    def rows(channels):
        return ((message_rows(channels), LANES), F32)

    def stat(channels):
        return ((8, channels), F32)

    def level(count, channels):
        return [((count, channels), BF16), ((count, channels), F32), ((count, channels), F32), stat(channels)]

    def ops(count, *sizes):
        total = 2 * count
        for size in sizes:
            total *= size
        return total

    entry_in, mask, small, above, below, small_below, entry_raw, edge, sent, give = call(
        functools.partial(entry_kernel, dims),
        [
            ((pixels, wide_in), BF16),
            ((pixels, LANES), F32),
            ((small_pixels, LANES), F32),
            ((batch * width, LANES), F32),
            ((batch * width, LANES), F32),
            ((batch * width // 2, LANES), F32),
            ((pixels, mid), F32),
            ((batch * width, mid), F32),
            message(mid),
            ((pixels, wide_in // 2), BF16),
        ],
        local,
        flag,
        core,
        images.reshape(pixels, wide_in),
        entry_weight,
        scratch=[rows(mid)],
        smem=(0, 1, 2),
        late=(3, 4),
        keep=(6, 7, 8),
        flops=ops(pixels, wide_in, mid),
    )
    halo = swap_rows(edge)
    entry_in_other = swap_rows(give)
    counts = gather_all(sent)
    padded_rows = batch * (height + 2) * width
    entry_unit, entry_slope, entry_stats, middle_raw, sent, triple, give = call(
        functools.partial(middle_kernel, dims),
        level(pixels, mid)[1:]
        + [
            ((pixels, mid), F32),
            message(mid),
            ((batch, (height + 2) * width, 3 * mid), BF16),
            ((batch, (height + 2) * width, 3 * mid // 2), BF16),
        ],
        core,
        counts,
        entry_raw,
        halo,
        mask,
        above,
        below,
        entry_affine,
        middle_weight.reshape(3, 3 * mid, mid),
        scratch=[rows(mid), ((padded_rows + 16, mid), F32)],
        smem=(0,),
        late=(8,),
        keep=(3, 4),
        flops=ops(pixels, 9, mid, mid),
    )
    triple_other = swap_rows(give)
    gathered = gather_all(sent)
    middle_act, middle_unit, middle_slope, middle_stats, closing_raw, sent, give = call(
        closing_kernel,
        level(pixels, mid) + [((pixels, wide_in), F32), message(wide_in), ((pixels, mid // 2), BF16)],
        core,
        gathered,
        counts,
        middle_raw,
        mask,
        middle_affine,
        closing_weight,
        scratch=[rows(wide_in)],
        smem=(0,),
        late=(6,),
        keep=(4, 5),
        flops=ops(pixels, mid, wide_in),
    )
    middle_act_other = swap_rows(give)
    gathered = gather_all(sent)
    block_out, closing_unit, block_slope, closing_stats, shortcut_in, widen_raw, edge, sent, give, give_short = call(
        functools.partial(widen_kernel, dims),
        level(pixels, wide_in)
        + [
            ((small_pixels, wide_in), BF16),
            ((pixels, wider), F32),
            ((batch * width, wider), F32),
            message(wider),
            ((pixels, wide_in // 2), BF16),
            ((small_pixels, wide_in // 2), BF16),
        ],
        core,
        gathered,
        counts,
        closing_raw,
        entry_in,
        mask,
        closing_affine,
        widen_weight,
        scratch=[rows(wider), ((wide_in // LANES, pixels, LANES), F32)],
        smem=(0,),
        late=(4, 7),
        keep=(5, 6, 7),
        flops=ops(pixels, wide_in, wider),
    )
    halo = swap_rows(edge)
    block_other, short_other = swap_rows(give), swap_rows(give_short)
    gathered = gather_all(sent)
    shortcut_raw, shortcut_rows = call(
        shortcut_kernel,
        [((small_pixels, last), F32), rows(last)],
        shortcut_in,
        small,
        shortcut_weight,
        late=(0, 2),
        keep=(),
        flops=ops(small_pixels, wide_in, last),
    )
    widen_unit, widen_slope, widen_stats, strided_raw, sent, taps, give = call(
        functools.partial(strided_kernel, dims),
        level(pixels, wider)[1:]
        + [
            ((small_pixels, wider), F32),
            message(wider),
            ((3, small_pixels, 3 * wider), BF16),
            ((3, small_pixels, 3 * wider // 2), BF16),
        ],
        core,
        gathered,
        counts,
        widen_raw,
        halo,
        mask,
        small,
        above,
        widen_affine,
        strided_weight.reshape(3, 3 * wider, wider),
        scratch=[rows(wider), ((wider // LANES, batch * (height + 1) * width + 16, LANES), F32)],
        smem=(0,),
        late=(9,),
        keep=(3, 4),
        flops=ops(small_pixels, 9, wider, wider),
    )
    taps_other = swap_rows(give)
    gathered = gather_all(sent)
    pair_rows = message_rows(last) + 8
    strided_act, strided_unit, strided_slope, strided_stats, expand_raw, mine, theirs, give = call(
        expand_kernel,
        level(small_pixels, wider)
        + [
            ((small_pixels, last), F32),
            ((pair_rows, LANES), F32),
            ((pair_rows, LANES), F32),
            ((small_pixels, wider // 2), BF16),
        ],
        gathered,
        counts,
        strided_raw,
        small,
        strided_affine,
        expand_weight,
        shortcut_rows,
        flag,
        core,
        scratch=[rows(last)],
        smem=(7, 8),
        late=(5, 6),
        keep=(4, 5, 6),
        flops=ops(small_pixels, wider, last),
    )
    strided_act_other = swap_rows(give)
    (sent,) = call(pair_kernel, [((chips, pair_rows, LANES), F32)], mine, swap_rows(theirs), keep=(0,))
    (own_stats,) = call(join_kernel, [stat(last)], gather_img(sent), keep=(0,))
    half_rows = 3 * last // (2 * LANES)
    features, final_grad, expand_unit, shortcut_unit, expand_stats, shortcut_stats, mine, theirs = call(
        final_kernel,
        [
            ((small_pixels, last), BF16),
            ((small_pixels, last), F32),
            ((small_pixels, last), F32),
            ((small_pixels, last), F32),
            stat(last),
            stat(last),
            ((half_rows, LANES), F32),
            ((half_rows, LANES), F32),
        ],
        own_stats,
        swap_rows(own_stats),
        flag,
        expand_raw,
        shortcut_raw,
        small,
        expand_affine,
        shortcut_affine,
        cotangent.reshape(small_pixels, last),
        late=(4, 8),
        keep=(1, 2, 3, 4, 5, 6, 7),
        scratch=[((3 * last // LANES, LANES), F32)],
        smem=(2,),
    )

    joined = mine + swap_rows(theirs)
    own_sums = jnp.sum(gather_img(jnp.broadcast_to(joined[None], (chips,) + joined.shape)), axis=0)
    affine_expand, affine_shortcut, expand_grad, shortcut_grad, strided_back, edge, sent = call(
        functools.partial(last_grads_kernel, batch),
        [
            ((2, last), F32),
            ((2, last), F32),
            ((small_pixels, last), BF16),
            ((small_pixels, last), BF16),
            ((small_pixels, wider), F32),
            ((batch * width, wider), F32),
            message(wider),
        ],
        own_sums,
        swap_rows(own_sums),
        flag,
        counts,
        final_grad,
        expand_unit,
        shortcut_unit,
        expand_stats,
        shortcut_stats,
        expand_affine,
        shortcut_affine,
        small,
        expand_weight,
        strided_slope,
        strided_unit,
        scratch=[rows(wider)],
        smem=(2,),
        late=(12, 13, 14),
        keep=(4, 5, 6),
        flops=ops(small_pixels, wider, last),
    )
    halo = swap_rows(edge)
    gathered = gather_all(sent)

    def small_image(value):
        return value.reshape(batch, height // 2, width // 2, value.shape[-1])

    def image(value):
        return value.reshape(batch, height, width, value.shape[-1])

    (short_back,) = call(
        functools.partial(short_back_kernel, dims),
        [((wide_in // LANES, pixels, LANES), F32)],
        shortcut_grad,
        shortcut_weight,
        late=(0, 1),
        keep=(),
        flops=ops(small_pixels, wide_in, last),
    )
    two = place_of([bits[0] for bits in orders()])

    def wave(kernel, shape, *operands, flops):
        half = (shape[0] // 2, shape[1] // 2)
        results = call(
            kernel,
            [(half, BF16)] * 4,
            core,
            two,
            *operands,
            scratch=[(shape, BF16)],
            smem=(0, 1),
            flops=flops,
            late=None,
        )
        return results[:2], results[2:]

    first_shape = ((wide_in + wider) // 2, last)
    kept, sent_on = wave(
        first_wave_kernel,
        first_shape,
        shortcut_in,
        short_other,
        strided_act,
        strided_act_other,
        shortcut_grad,
        swap_rows(shortcut_grad),
        expand_grad,
        swap_rows(expand_grad),
        flops=ops(2 * small_pixels, *first_shape),
    )
    shortcut_total, expand_total = sum_over_chips(
        kept, sent_on, first_out_kernel, [((wide_in // 2, last), F32), ((wider // 2, last), F32)], first_shape
    )

    affine_strided, strided_grad, widen_back, sent = call(
        functools.partial(widen_back_kernel, dims),
        [((2, wider), F32), ((small_pixels, wider), BF16), ((pixels, wider), F32), message(wider)],
        gathered,
        counts,
        strided_back,
        strided_unit,
        halo,
        small,
        small_below,
        strided_stats,
        strided_affine,
        strided_weight,
        widen_unit,
        widen_slope,
        scratch=[
            rows(wider),
            ((batch * (height // 2 + 1) * width // 2 + 8, wider), F32),
            ((wider // LANES, pixels, LANES), F32),
        ],
        late=(3, 9, 10, 11),
        keep=(2, 3),
        flops=ops(small_pixels, 9, wider, wider),
    )
    gathered = gather_all(sent)
    affine_widen, widen_grad, block_back, sent, block_back_saved = call(
        block_back_kernel,
        [
            ((2, wider), F32),
            ((pixels, wider), BF16),
            ((pixels, wide_in), F32),
            message(wide_in),
            ((pixels, wide_in), F32),
        ],
        gathered,
        counts,
        widen_back,
        widen_unit,
        mask,
        widen_stats,
        widen_affine,
        widen_weight,
        short_back,
        closing_unit,
        block_slope,
        scratch=[rows(wide_in)],
        late=(3, 7, 8, 9, 10),
        keep=(2, 3),
        flops=ops(pixels, wide_in, wider),
    )
    gathered = gather_all(sent)

    second_shape = ((9 * wider + wide_in) // 2, wider)
    kept, sent_on = wave(
        second_wave_kernel,
        second_shape,
        taps,
        taps_other,
        strided_grad,
        swap_rows(strided_grad),
        block_out,
        block_other,
        widen_grad,
        swap_rows(widen_grad),
        flops=ops(2 * small_pixels, *second_shape),
    )
    strided_total, widen_total = sum_over_chips(
        kept, sent_on, second_out_kernel, [((9, wider // 2, wider), F32), ((wide_in // 2, wider), F32)], second_shape
    )

    affine_closing, closing_grad, middle_back, edge, sent = call(
        functools.partial(middle_back_kernel, dims),
        [
            ((2, wide_in), F32),
            ((pixels, wide_in), BF16),
            ((pixels, mid), F32),
            ((2 * batch * width, mid), F32),
            message(mid),
        ],
        flag,
        gathered,
        counts,
        block_back,
        closing_unit,
        mask,
        closing_stats,
        closing_affine,
        closing_weight,
        middle_unit,
        middle_slope,
        scratch=[rows(mid)],
        smem=(0,),
        late=(4, 8, 9, 10),
        keep=(2, 3, 4),
        flops=ops(pixels, wide_in, mid),
    )
    halo = swap_rows(edge)
    gathered = gather_all(sent)
    affine_middle, middle_grad, entry_back, sent = call(
        functools.partial(entry_back_kernel, dims),
        [((2, mid), F32), ((pixels, mid), BF16), ((pixels, mid), F32), message(mid)],
        gathered,
        counts,
        middle_back,
        middle_unit,
        halo,
        mask,
        above,
        below,
        middle_stats,
        middle_affine,
        middle_weight,
        entry_unit,
        entry_slope,
        scratch=[rows(mid), ((padded_rows + 16, mid), F32), ((batch, (height + 2) * width, 3 * mid), BF16)],
        late=(3, 10, 11, 12),
        keep=(2, 3),
        flops=ops(pixels, 9, mid, mid),
    )
    gathered = gather_all(sent)
    affine_entry, entry_grad, image_grads = call(
        images_kernel,
        [((2, mid), F32), ((pixels, mid), BF16), ((pixels, wide_in), BF16)],
        gathered,
        counts,
        entry_back,
        entry_unit,
        mask,
        entry_stats,
        entry_affine,
        entry_weight,
        block_back_saved,
        late=(3, 7, 8),
        keep=(),
        flops=ops(pixels, mid, wide_in),
    )

    third_rows = 9 * mid // 2 + wide_in // 2
    third_shape = (-(-third_rows // 256) * 256, mid)
    kept, sent_on = wave(
        functools.partial(third_wave_kernel, dims),
        third_shape,
        triple,
        triple_other,
        middle_grad,
        swap_rows(middle_grad),
        middle_act,
        middle_act_other,
        closing_grad,
        swap_rows(closing_grad),
        flops=ops(2 * pixels, *third_shape),
    )
    middle_total, closing_total = sum_over_chips(
        kept, sent_on, third_out_kernel, [((9, mid // 2, mid), F32), ((mid // 2, wide_in), F32)], third_shape
    )
    (parts,) = call(
        last_wave_kernel,
        [((wide_in // 2, mid), BF16)],
        core,
        entry_in,
        entry_in_other,
        entry_grad,
        swap_rows(entry_grad),
        smem=(0,),
        flops=ops(2 * pixels, wide_in // 2, mid),
        late=None,
    )
    entry_total = sum_over_chips_short(parts.reshape(chips, -1, mid))
    middle_total = middle_total.reshape(3, 3, mid // 2, mid)
    strided_total = strided_total.reshape(3, 3, wider // 2, wider)
    return (
        small_image(features),
        image(image_grads),
        entry_total.astype(F32),
        middle_total,
        closing_total,
        widen_total,
        strided_total,
        expand_total,
        shortcut_total,
        affine_entry,
        affine_middle,
        affine_closing,
        affine_widen,
        affine_strided,
        affine_expand,
        affine_shortcut,
    )


def solution(mesh):
    image = P("img", "row", None, None)
    return jax.shard_map(
        per_device,
        mesh=mesh,
        in_specs=(image, P("img", None)) + (P(),) * 14 + (image,),
        out_specs=(
            image,
            image,
            P("row", None),
            P(None, None, "row", None),
            P("row", None),
            P("row", None),
            P(None, None, "row", None),
            P("row", None),
            P("row", None),
        )
        + (P(),) * 7,
        check_vma=False,
    )
```

```python
import functools
import math

import jax
import jax.numpy as jnp
from jax import lax
from jax.experimental import pallas as pl
from jax.experimental.pallas import tpu as pltpu
from jax.sharding import PartitionSpec as P

EPS = 1e-05
BOTH = ("img", "row")
F32 = jnp.float32
BF16 = jnp.bfloat16
LANES = 128
MIB = 1 << 20


def swap_rows(value):
    count = lax.axis_size("row")
    return lax.ppermute(value, "row", [(i, (i + 1) % count) for i in range(count)])


def gather_all(message):
    return lax.all_to_all(message, BOTH, 0, 0, tiled=True)


def gather_img(message):
    return lax.all_to_all(message, "img", 0, 0, tiled=True)


class Late:
    def __init__(self, source, buffer, semaphores):
        self.buffer = buffer
        self.shape, self.ndim, self.dtype = buffer.shape, len(buffer.shape), buffer.dtype
        parts = parts_of(self.shape)
        if parts == 1:
            self.copies = [pltpu.make_async_copy(source, buffer, semaphores.at[0])]
        else:
            self.copies = [
                pltpu.make_async_copy(source.at[i], buffer.at[i], semaphores.at[i]) for i in range(parts)
            ]
        for copy in self.copies:
            copy.start()
        self.waiting = set(range(parts))

    def ready(self, part=None):
        for i in sorted(self.waiting):
            if part is None or i == part:
                self.copies[i].wait()
                self.waiting.remove(i)
        return self.buffer

    def __getitem__(self, index):
        first = index[0] if isinstance(index, tuple) else index
        part = first if isinstance(first, int) and len(self.copies) > 1 else None
        return self.ready(part)[index]


def parts_of(shape):
    return shape[0] if len(shape) >= 3 and shape[0] == 3 else 1


class Saved:
    def __init__(self, target, buffer, semaphore):
        self.target, self.buffer, self.semaphore, self.copy = target, buffer, semaphore, None
        self.shape, self.ndim, self.dtype = buffer.shape, len(buffer.shape), buffer.dtype

    def send(self):
        if self.copy is None:
            self.copy = pltpu.make_async_copy(self.buffer, self.target, self.semaphore)
            self.copy.start()

    def __getitem__(self, index):
        return self.buffer[index]

    def __setitem__(self, index, value):
        self.buffer[index] = value


def send(*results):
    for result in results:
        if isinstance(result, Saved):
            result.send()


def call(kernel, outs, *operands, scratch=(), smem=(), late=(), flops=0, keep=(), limit=24, after=(), free=False):
    late = [place for place in (range(len(operands)) if late is None else late) if place not in smem]
    used = len(operands)
    operands += tuple(after)
    saved = [place for place in range(len(outs)) if place not in keep and not free]
    moved = sum(x.size * x.dtype.itemsize for x in operands) + sum(
        math.prod(shape) * jnp.dtype(dtype).itemsize for shape, dtype in outs
    )

    def place_of_operand(place):
        if place in smem:
            return pltpu.SMEM
        return pl.ANY if place in late or place >= used else pltpu.VMEM

    operands = [
        pltpu.with_memory_space_constraint(x, pltpu.HBM) if place in late or place >= used else x
        for place, x in enumerate(operands)
    ]
    buffers = [pltpu.VMEM(operands[place].shape, operands[place].dtype) for place in late]
    buffers += [pltpu.VMEM(*outs[place]) for place in saved]
    semaphores = [pltpu.SemaphoreType.DMA((parts_of(operands[place].shape),)) for place in late]
    semaphores += [pltpu.SemaphoreType.DMA] * len(saved)

    def body(*refs):
        refs = list(refs)
        inputs, refs = refs[: len(operands)], refs[len(operands) :]
        results, refs = refs[: len(outs)], refs[len(outs) :]
        own, refs = refs[: len(scratch)], refs[len(scratch) :]
        space, marks = refs[: len(buffers)], refs[len(buffers) :]
        for number, place in enumerate(late):
            inputs[place] = Late(inputs[place], space[number], marks[number])
        for number, place in enumerate(saved):
            number += len(late)
            results[place] = Saved(results[place], space[number], marks[number])
        kernel(*inputs[:used], *results, *own)
        for place in late:
            inputs[place].ready()
        for place in saved:
            results[place].send()
        for place in saved:
            results[place].copy.wait()

    return pl.pallas_call(
        body,
        out_shape=[
            jax.ShapeDtypeStruct(shape, dtype)
            if free
            else (pltpu.VMEM if place in keep else pltpu.HBM)(shape, dtype)
            for place, (shape, dtype) in enumerate(outs)
        ],
        in_specs=[pl.BlockSpec(memory_space=place_of_operand(place)) for place in range(len(operands))],
        out_specs=[
            pl.BlockSpec(memory_space=pl.ANY if place in saved else pltpu.VMEM) for place in range(len(outs))
        ],
        scratch_shapes=[pltpu.VMEM(shape, dtype) for shape, dtype in scratch] + buffers + semaphores,
        compiler_params=pltpu.CompilerParams(vmem_limit_bytes=limit * MIB),
        cost_estimate=pl.CostEstimate(flops=flops, bytes_accessed=moved, transcendentals=0),
    )(*operands)


def dot(left, right):
    return jnp.dot(left, right, preferred_element_type=F32)


def dot_back(grad, weight):
    return lax.dot_general(grad, weight, (((1,), (1,)), ((), ())), preferred_element_type=F32)


def wide(mask, width):
    return mask if width == LANES else jnp.concatenate([mask] * (width // LANES), axis=1)


def column_sum(value):
    return jnp.sum(value, axis=0, keepdims=True)


def spread_message(message, rows):
    tile = rows[...]
    for device in range(message.shape[0]):
        message[device] = tile


def put_row(rows, place, vector):
    for block in range(vector.shape[1] // LANES):
        rows[place + block : place + block + 1, :] = vector[:, block * LANES : (block + 1) * LANES]


def local_stats(raw, mask, rows, place=0):
    blocks = raw.shape[1] // LANES
    number = jnp.maximum(column_sum(mask[...]), 1.0)
    for block in range(blocks):
        columns = slice(block * LANES, (block + 1) * LANES)
        total = column_sum(raw[:, columns] * mask[...])
        centred = (raw[:, columns] - total / number) * mask[...]
        rows[place + block : place + block + 1, :] = total
        rows[place + blocks + block : place + blocks + block + 1, :] = column_sum(centred * centred)


def total_count(counts, place):
    return functools.reduce(
        jnp.add, [counts[i, place : place + 1, :] for i in range(counts.shape[0])]
    )


def join_stats(gathered, counts, place, stats, blocks):
    devices = gathered.shape[0]
    count = total_count(counts, place)
    mean = functools.reduce(jnp.add, [gathered[i, :blocks, :] for i in range(devices)]) / count
    spread = functools.reduce(jnp.add, [gathered[i, blocks : 2 * blocks, :] for i in range(devices)])
    for i in range(devices):
        number = counts[i, place : place + 1, :]
        shift = gathered[i, :blocks, :] / jnp.maximum(number, 1.0) - mean
        spread = spread + number * (shift * shift)
    scale = lax.rsqrt(spread / count + EPS)
    for block in range(blocks):
        columns = slice(block * LANES, (block + 1) * LANES)
        stats[0:1, columns] = mean[block : block + 1, :]
        stats[1:2, columns] = scale[block : block + 1, :]


def join_sums(gathered, affine):
    total = functools.reduce(jnp.add, [gathered[i] for i in range(gathered.shape[0])])
    blocks = affine.shape[1] // LANES
    for block in range(blocks):
        columns = slice(block * LANES, (block + 1) * LANES)
        affine[0:1, columns] = total[block : block + 1, :]
        affine[1:2, columns] = total[blocks + block : blocks + block + 1, :]


def chunks(rows, width, chunk=32, block=256):
    for start in range(0, width, block):
        for row in range(0, rows, chunk):
            yield slice(row, row + min(chunk, rows - row)), slice(start, start + min(block, width - start))


def silu_parts(value):
    gate = jax.nn.sigmoid(value)
    return value * gate, gate * (1.0 + value * (1.0 - gate))


def normed(raw, stats, params, columns):
    unit = (raw - stats[0:1, columns]) * stats[1:2, columns]
    return unit, unit * params[0:1, columns] + params[1:2, columns]


def act_pass(raw, mask, stats, params, unit, slope, act, skip=None, keep=None):
    rows, width = raw.shape
    for here, columns in chunks(rows, width):
        u, value = normed(raw[here, columns], stats, params, columns)
        if skip is not None:
            value = value + skip[here, columns].astype(F32)
        m = wide(mask[here, :], columns.stop - columns.start)
        out, rise = silu_parts(value)
        out = out * m
        unit[here, columns] = u
        slope[here, columns] = rise * m
        if act is not None:
            act[here, columns] = out.astype(BF16)
        if keep is not None:
            keep(here, columns, out)


def back_pass(back, unit, slope, rows):
    blocks = back.shape[1] // LANES
    for block in range(blocks):
        columns = slice(block * LANES, (block + 1) * LANES)
        value = back[:, columns] * slope[:, columns]
        back[:, columns] = value
        rows[block : block + 1, :] = column_sum(value * unit[:, columns])
        rows[blocks + block : blocks + block + 1, :] = column_sum(value)


def raw_grad(back, unit, mask, sums, stats, params, count, columns):
    width = columns.stop - columns.start
    n = wide(count, width)
    factor = params[0:1, columns] * stats[1:2, columns]
    centred = back - sums[1:2, columns] / n - unit * (sums[0:1, columns] / n)
    return factor * centred * wide(mask, width)


def grad_pass(back, unit, mask, sums, stats, params, count, grad, keep=None):
    for here, columns in chunks(*back.shape):
        value = raw_grad(
            back[here, columns], unit[here, columns], mask[here, :], sums, stats, params, count, columns
        )
        grad[here, columns] = value.astype(BF16)
        if keep is not None:
            keep(here, columns, value)


def valid(extents, image, first_row, columns, shape, step):
    place = lax.broadcasted_iota(jnp.int32, shape, 0)
    row = first_row + step * (place // columns)
    column = step * (place % columns)
    return jnp.where((row < extents[image, 0]) & (column < extents[image, 1]), 1.0, 0.0).astype(F32)


def core_number():
    return lax.axis_index("row").astype(jnp.int32)


def is_upper():
    return jnp.where(core_number() == 0, 1.0, 0.0).astype(F32)


def own_half(size):
    return pl.ds(pl.multiple_of(core_number() * size, LANES), size)


def other_half(size):
    return pl.ds(pl.multiple_of((1 - core_number()) * size, LANES), size)


def give_half(value, give):
    give[...] = value[:, other_half(give.shape[1])]
    send(give)


def entry_kernel(
    dims, extents, images, weight,
    entry_in, mask, small, above, below, small_below, raw, edge, message, give, rows,
):
    batch, height, width = dims
    pixels = height * width
    upper = is_upper()
    for b in range(batch):
        mask[b * pixels : (b + 1) * pixels, :] = valid(extents, b, 0, width, (pixels, LANES), 1)
        small[b * pixels // 4 : (b + 1) * pixels // 4, :] = valid(
            extents, b, 0, width // 2, (pixels // 4, LANES), 2
        )
        line = slice(b * width, (b + 1) * width)
        above[line, :] = valid(extents, b, -1, width, (width, LANES), 1) * (1.0 - upper)
        below[line, :] = valid(extents, b, height, width, (width, LANES), 1) * upper
        small_below[b * width // 2 : (b + 1) * width // 2, :] = (
            valid(extents, b, height, width // 2, (width // 2, LANES), 2) * upper
        )
    for here, columns in chunks(*images.shape):
        m = wide(mask[here, :], columns.stop - columns.start)
        entry_in[here, columns] = (images[here, columns].astype(F32) * m).astype(BF16)
    send(entry_in, mask, small, above, below, small_below)
    give_half(entry_in, give)
    raw[...] = dot(entry_in[...], weight[...])
    for b in range(batch):
        first = raw[b * pixels : b * pixels + width, :]
        last = raw[(b + 1) * pixels - width : (b + 1) * pixels, :]
        edge[b * width : (b + 1) * width, :] = last * upper + first * (1.0 - upper)
    rows[...] = jnp.zeros_like(rows)
    local_stats(raw, mask, rows)
    blocks = raw.shape[1] // LANES
    rows[2 * blocks : 2 * blocks + 1, :] = column_sum(mask[...])
    rows[2 * blocks + 1 : 2 * blocks + 2, :] = column_sum(small[...])
    spread_message(message, rows)


def put_blocks(target, here, columns, value):
    for start in range(columns.start, columns.stop, LANES):
        offset = start - columns.start
        target[start // LANES, here, :] = value[:, offset : offset + LANES]


def column_masks(rows, width):
    place = lax.broadcasted_iota(jnp.int32, (rows, LANES), 0) % width
    return (
        jnp.where(place == 0, 0.0, 1.0).astype(F32),
        jnp.where(place == width - 1, 0.0, 1.0).astype(F32),
    )


def fill_triple(padded, triple, batch, lines, width):
    size = lines * width
    channels = padded.shape[1]
    left_ok, right_ok = column_masks(size, width)
    for b in range(batch):
        start = 8 + b * size
        for c in range(0, channels, LANES):
            columns = slice(c, c + LANES)
            triple[b, :, c : c + LANES] = (padded[start - 1 : start - 1 + size, columns] * left_ok).astype(BF16)
            triple[b, :, channels + c : channels + c + LANES] = padded[start : start + size, columns].astype(BF16)
            triple[b, :, 2 * channels + c : 2 * channels + c + LANES] = (
                padded[start + 1 : start + 1 + size, columns] * right_ok
            ).astype(BF16)


def middle_kernel(
    dims, gathered, raw, halo, mask, above, below, params, weight,
    unit, slope, stats, out, message, triple, give, rows, padded,
):
    batch, height, width = dims
    pixels = height * width
    size = pixels + 2 * width
    blocks = raw.shape[1] // LANES
    join_stats(gathered, gathered, 2 * blocks, stats, blocks)
    everything = slice(0, raw.shape[1])
    _, value = normed(halo[...], stats, params, everything)
    rim, _ = silu_parts(value)
    padded[0:8, :] = jnp.zeros((8, raw.shape[1]), F32)
    padded[8 + batch * size :, :] = jnp.zeros((8, raw.shape[1]), F32)
    for b in range(batch):
        line = slice(b * width, (b + 1) * width)
        top = 8 + b * size
        padded[top : top + width, :] = rim[line] * wide(above[line, :], raw.shape[1])
        padded[top + size - width : top + size, :] = rim[line] * wide(below[line, :], raw.shape[1])

    def keep(here, columns, value):
        b = here.start // pixels
        start = 8 + b * size + width + here.start - b * pixels
        padded[start : start + here.stop - here.start, columns] = value

    act_pass(raw, mask, stats, params, unit, slope, None, keep=keep)
    send(unit, slope, stats)
    fill_triple(padded, triple, batch, height + 2, width)
    send(triple)
    give_taps(triple, give)
    total = None
    for tap in range(3):
        left = triple[:, tap * width : tap * width + pixels, :].reshape(batch * pixels, -1)
        part = dot(left, weight[tap])
        total = part if total is None else total + part
    out[...] = total
    local_stats(out, mask, rows)
    spread_message(message, rows)


def give_taps(taps, give):
    full, half = taps.shape[2] // 3, give.shape[2] // 3
    for tap in range(3):
        start = pl.multiple_of(tap * full + (1 - core_number()) * half, LANES)
        give[:, :, tap * half : (tap + 1) * half] = taps[:, :, pl.ds(start, half)]
    send(give)


def closing_kernel(
    gathered, counts, raw, mask, params, weight, act, unit, slope, stats, out, message, give, rows
):
    blocks = raw.shape[1] // LANES
    join_stats(gathered, counts, 4, stats, blocks)
    act_pass(raw, mask, stats, params, unit, slope, act)
    send(unit, slope, act, stats)
    give_half(act, give)
    out[...] = dot(act[...], weight[...])
    local_stats(out, mask, rows)
    spread_message(message, rows)


def widen_kernel(
    dims, gathered, counts, raw, entry_in, mask, params, weight,
    act, unit, slope, stats, short, out, edge, message, give, give_short, rows, even,
):
    batch, height, width = dims
    pixels = height * width
    blocks = raw.shape[1] // LANES
    join_stats(gathered, counts, 4, stats, blocks)

    def keep(here, columns, value):
        put_blocks(even, here, columns, value)

    act_pass(raw, mask, stats, params, unit, slope, act, skip=entry_in, keep=keep)
    send(unit, slope, act, stats)
    give_half(act, give)
    out[...] = dot(act[...], weight[...])
    for b in range(batch):
        edge[b * width : (b + 1) * width, :] = out[(b + 1) * pixels - width : (b + 1) * pixels, :]
    local_stats(out, mask, rows)
    spread_message(message, rows)
    for c in range(0, raw.shape[1], LANES):
        columns = slice(c, c + LANES)
        lines = []
        for b in range(batch):
            for i in range(height // 2):
                lines.append(even[c // LANES, pl.ds(b * pixels + 2 * i * width, width // 2, stride=2), :])
        short[:, columns] = jnp.concatenate(lines, axis=0).astype(BF16)
    send(short)
    give_half(short, give_short)


def shortcut_kernel(short, small, weight, out, rows):
    out[...] = dot(short[...], weight[...])
    send(out)
    local_stats(out, small, rows)


def strided_kernel(
    dims, gathered, counts, raw, halo, mask, small, above, params, weight,
    unit, slope, stats, out, message, taps, give, rows, padded,
):
    batch, height, width = dims
    pixels = height * width
    size = pixels + width
    half, half_width = height // 2, width // 2
    blocks = raw.shape[1] // LANES
    join_stats(gathered, counts, 4, stats, blocks)
    everything = slice(0, raw.shape[1])
    _, value = normed(halo[...], stats, params, everything)
    rim, _ = silu_parts(value)
    for block in range(padded.shape[0]):
        padded[block, 0:8, :] = jnp.zeros((8, LANES), F32)
    for b in range(batch):
        line = slice(b * width, (b + 1) * width)
        start = 8 + b * size
        put_blocks(padded, slice(start, start + width), everything, rim[line] * wide(above[line, :], raw.shape[1]))

    def keep(here, columns, value):
        b = here.start // pixels
        start = 8 + b * size + width + here.start - b * pixels
        put_blocks(padded, slice(start, start + here.stop - here.start), columns, value)

    act_pass(raw, mask, stats, params, unit, slope, None, keep=keep)
    send(unit, slope, stats)
    lines = height + 1
    not_first, _ = column_masks(lines * half_width, half_width)
    channels = raw.shape[1]
    for block in range(channels // LANES):
        for b in range(batch):
            start = 8 + b * size
            before = padded[block, pl.ds(start - 1, lines * half_width, stride=2), :] * not_first
            at = padded[block, pl.ds(start, lines * half_width, stride=2), :]
            after = padded[block, pl.ds(start + 1, lines * half_width, stride=2), :]
            for k, value in enumerate((before, at, after)):
                value = value.reshape(lines, half_width, LANES)
                place = k * channels + block * LANES
                for tap in range(3):
                    pieces = [value[tap + 2 * i] for i in range(half)]
                    taps[tap, b * half * half_width : (b + 1) * half * half_width, place : place + LANES] = (
                        jnp.concatenate(pieces, axis=0).astype(BF16)
                    )
    send(taps)
    give_taps(taps, give)
    total = None
    for tap in range(3):
        part = dot(taps[tap], weight[tap])
        total = part if total is None else total + part
    out[...] = total
    local_stats(out, small, rows)
    spread_message(message, rows)


def expand_kernel(
    gathered, counts, raw, small, params, weight, short_rows,
    act, unit, slope, stats, out, mine, theirs, give, rows,
):
    blocks = raw.shape[1] // LANES
    join_stats(gathered, counts, 5, stats, blocks)
    act_pass(raw, small, stats, params, unit, slope, act)
    send(unit, slope, act, stats)
    give_half(act, give)
    out[...] = dot(act[...], weight[...])
    local_stats(out, small, rows)
    upper = is_upper()
    size = rows.shape[0]
    number = jnp.broadcast_to(column_sum(small[...]), (8, LANES))
    mine[:size, :] = rows[...] * upper + short_rows[...] * (1.0 - upper)
    theirs[:size, :] = rows[...] * (1.0 - upper) + short_rows[...] * upper
    mine[size:, :] = number
    theirs[size:, :] = number


def pair_kernel(mine, other, message):
    size = mine.shape[0] - 8
    blocks = size // 2
    first, second = mine[size : size + 1, :], other[size : size + 1, :]
    both = first + second
    gap = mine[:blocks, :] / jnp.maximum(first, 1.0) - other[:blocks, :] / jnp.maximum(second, 1.0)
    weight = first * second / jnp.maximum(both, 1.0)
    total = mine[:blocks, :] + other[:blocks, :]
    square = mine[blocks:size, :] + other[blocks:size, :] + gap * gap * weight
    number = jnp.broadcast_to(both, (8, LANES))
    for i in range(message.shape[0]):
        message[i, :blocks, :] = total
        message[i, blocks:size, :] = square
        message[i, size:, :] = number


def join_kernel(gathered, stats):
    size = gathered.shape[1] - 8
    stats[...] = jnp.zeros_like(stats)
    join_stats(gathered, gathered, size, stats, size // 2)


def final_kernel(
    own, other, expand_raw, short_raw, small, expand_params, short_params, cotangent,
    features, grad, expand_unit, short_unit, expand_stats, short_stats, mine, theirs, rows,
):
    upper = is_upper()
    expand_stats[...] = own[...] * upper + other[...] * (1.0 - upper)
    short_stats[...] = own[...] * (1.0 - upper) + other[...] * upper
    height, width = expand_raw.shape
    blocks = width // LANES
    for block in range(blocks):
        columns = slice(block * LANES, (block + 1) * LANES)
        first, first_value = normed(expand_raw[:, columns], expand_stats, expand_params, columns)
        second, second_value = normed(short_raw[:, columns], short_stats, short_params, columns)
        out, rise = silu_parts(first_value + second_value)
        features[:, columns] = (out * small[...]).astype(BF16)
        value = cotangent[:, columns].astype(F32) * (rise * small[...])
        grad[:, columns] = value
        expand_unit[:, columns] = first
        short_unit[:, columns] = second
        rows[block : block + 1, :] = column_sum(value * first)
        rows[blocks + block : blocks + block + 1, :] = column_sum(value * second)
        rows[2 * blocks + block : 2 * blocks + block + 1, :] = column_sum(value)
    half = blocks // 2
    for stat in range(3):
        low = rows[stat * blocks : stat * blocks + half, :]
        high = rows[stat * blocks + half : (stat + 1) * blocks, :]
        mine[stat * half : (stat + 1) * half, :] = low * upper + high * (1.0 - upper)
        theirs[stat * half : (stat + 1) * half, :] = low * (1.0 - upper) + high * upper


def last_grads_kernel(
    batch, own, other, counts, grad, expand_unit, short_unit, expand_stats, short_stats,
    expand_params, short_params, small, weight, slope, unit,
    expand_affine, short_affine, expand_grad, short_grad, back, edge, message, rows,
):
    upper = is_upper()
    half = own.shape[0] // 3
    for stat in range(3):
        part = slice(stat * half, (stat + 1) * half)
        low = own[part, :] * upper + other[part, :] * (1.0 - upper)
        high = own[part, :] * (1.0 - upper) + other[part, :] * upper
        for block in range(2 * half):
            value = low[block : block + 1, :] if block < half else high[block - half : block - half + 1, :]
            columns = slice(block * LANES, (block + 1) * LANES)
            if stat == 0:
                expand_affine[0:1, columns] = value
            elif stat == 1:
                short_affine[0:1, columns] = value
            else:
                expand_affine[1:2, columns] = value
                short_affine[1:2, columns] = value
    count = total_count(counts, 5)
    for here, columns in chunks(*grad.shape):
        expand_grad[here, columns] = raw_grad(
            grad[here, columns], expand_unit[here, columns], small[here, :], expand_affine, expand_stats,
            expand_params, count, columns,
        ).astype(BF16)
        short_grad[here, columns] = raw_grad(
            grad[here, columns], short_unit[here, columns], small[here, :], short_affine, short_stats,
            short_params, count, columns,
        ).astype(BF16)
    send(expand_grad, short_grad, expand_affine, short_affine)
    back[...] = dot_back(expand_grad[...], weight[...])
    back_pass(back, unit, slope, rows)
    spread_message(message, rows)
    pixels = back.shape[0] // batch
    line = edge.shape[0] // (2 * batch)
    for b in range(batch):
        edge[b * line : (b + 1) * line, :] = back[b * pixels : b * pixels + line, :]
        edge[(batch + b) * line : (batch + b + 1) * line, :] = unit[b * pixels : b * pixels + line, :]


def short_back_kernel(dims, grad, weight, out):
    batch, height, width = dims
    pixels = height * width
    small = dot_back(grad[...], weight[...])
    out[...] = jnp.zeros(out.shape, out.dtype)
    half = width // 2
    for block in range(out.shape[0]):
        columns = slice(block * LANES, (block + 1) * LANES)
        for b in range(batch):
            for i in range(height // 2):
                place = b * pixels // 4 + i * half
                start = b * pixels + 2 * i * width
                out[block, pl.ds(start, half, stride=2), :] = small[place : place + half, columns]


def widen_back_kernel(
    dims, gathered, counts, back, unit, halo, small, small_below, stats, params, weight, out_unit, out_slope,
    affine, grad, out, message, rows, padded, full,
):
    batch, height, width = dims
    pixels = height * width
    half, half_width = height // 2, width // 2
    size = (half + 1) * half_width
    join_sums(gathered, affine)
    count = total_count(counts, 5)
    channels = back.shape[1]
    everything = slice(0, channels)
    line = batch * half_width
    rim = raw_grad(
        halo[:line, :], halo[line:, :], small_below[...], affine, stats, params, count, everything
    ).astype(BF16).astype(F32)
    for b in range(batch):
        stop = (b + 1) * size
        padded[stop - half_width : stop, :] = rim[b * half_width : (b + 1) * half_width]
    padded[batch * size :, :] = jnp.zeros((8, channels), F32)
    small_pixels = half * half_width
    for here, columns in chunks(back.shape[0], channels, chunk=small_pixels):
        value = raw_grad(
            back[here, columns], unit[here, columns], small[here, :], affine, stats, params, count, columns
        ).astype(BF16)
        grad[here, columns] = value
        b = here.start // small_pixels
        padded[b * size : b * size + small_pixels, columns] = value.astype(F32)
    send(grad, affine)
    _, not_last = column_masks(small_pixels, half_width)
    not_last = wide(not_last, channels)

    def moved(down, right):
        pieces = []
        for b in range(batch):
            start = b * size + down * half_width + right
            piece = padded[start : start + small_pixels, :]
            pieces.append(piece * not_last if right else piece)
        return jnp.concatenate(pieces, axis=0).astype(BF16)

    here, right, down, across = moved(0, 0), moved(0, 1), moved(1, 0), moved(1, 1)
    phases = {
        (0, 0): dot_back(here, weight[1, 1]),
        (0, 1): dot_back(here, weight[1, 2]) + dot_back(right, weight[1, 0]),
        (1, 0): dot_back(here, weight[2, 1]) + dot_back(down, weight[0, 1]),
        (1, 1): dot_back(here, weight[2, 2])
        + dot_back(right, weight[2, 0])
        + dot_back(down, weight[0, 2])
        + dot_back(across, weight[0, 0]),
    }
    for (a, e), value in phases.items():
        for b in range(batch):
            for i in range(half):
                place = b * small_pixels + i * half_width
                start = b * pixels + (2 * i + a) * width + e
                for block in range(full.shape[0]):
                    full[block, pl.ds(start, half_width, stride=2), :] = value[
                        place : place + half_width, block * LANES : (block + 1) * LANES
                    ]
    for block in range(full.shape[0]):
        out[:, block * LANES : (block + 1) * LANES] = full[block]
    back_pass(out, out_unit, out_slope, rows)
    spread_message(message, rows)


def block_back_kernel(
    gathered, counts, back, unit, mask, stats, params, weight, short_back, out_unit, out_slope,
    affine, grad, out, message, again, rows,
):
    join_sums(gathered, affine)
    grad_pass(back, unit, mask, affine, stats, params, total_count(counts, 4), grad)
    send(grad, affine)
    short = jnp.concatenate([short_back[block] for block in range(short_back.shape[0])], axis=1)
    out[...] = dot_back(grad[...], weight[...]) + short
    back_pass(out, out_unit, out_slope, rows)
    again[...] = out[...]
    send(again)
    spread_message(message, rows)


def middle_back_kernel(
    dims, gathered, counts, back, unit, mask, stats, params, weight, out_unit, out_slope,
    affine, grad, out, edge, message, rows,
):
    batch, height, width = dims
    pixels = height * width
    upper = is_upper()
    join_sums(gathered, affine)
    grad_pass(back, unit, mask, affine, stats, params, total_count(counts, 4), grad)
    send(grad, affine)
    out[...] = dot_back(grad[...], weight[...])
    back_pass(out, out_unit, out_slope, rows)
    spread_message(message, rows)
    for place, source in ((0, out), (batch, out_unit)):
        for b in range(batch):
            first = source[b * pixels : b * pixels + width, :]
            last = source[(b + 1) * pixels - width : (b + 1) * pixels, :]
            edge[(place + b) * width : (place + b + 1) * width, :] = last * upper + first * (1.0 - upper)


def entry_back_kernel(
    dims, gathered, counts, back, unit, halo, mask, above, below, stats, params, weight, out_unit, out_slope,
    affine, grad, out, message, rows, padded, triple,
):
    batch, height, width = dims
    pixels = height * width
    size = pixels + 2 * width
    join_sums(gathered, affine)
    count = total_count(counts, 4)
    channels = back.shape[1]
    everything = slice(0, channels)
    line = batch * width
    padded[0:8, :] = jnp.zeros((8, channels), F32)
    padded[8 + batch * size :, :] = jnp.zeros((8, channels), F32)
    up = raw_grad(halo[:line, :], halo[line:, :], above[...], affine, stats, params, count, everything)
    down = raw_grad(halo[:line, :], halo[line:, :], below[...], affine, stats, params, count, everything)
    for b in range(batch):
        here = slice(b * width, (b + 1) * width)
        top = 8 + b * size
        padded[top : top + width, :] = up[here]
        padded[top + size - width : top + size, :] = down[here]

    def keep(here, columns, value):
        b = here.start // pixels
        start = 8 + b * size + width + here.start - b * pixels
        padded[start : start + here.stop - here.start, columns] = value

    grad_pass(back, unit, mask, affine, stats, params, count, grad, keep=keep)
    send(grad, affine)
    fill_triple(padded, triple, batch, height + 2, width)
    total = None
    for row_tap in range(3):
        shift = (2 - row_tap) * width
        for col_tap in range(3):
            side = (2 - col_tap) * channels
            left = triple[:, shift : shift + pixels, side : side + channels].reshape(batch * pixels, channels)
            part = dot_back(left, weight[row_tap, col_tap])
            total = part if total is None else total + part
    out[...] = total
    back_pass(out, out_unit, out_slope, rows)
    spread_message(message, rows)


def images_kernel(gathered, counts, back, unit, mask, stats, params, weight, block_back, affine, grad, out):
    join_sums(gathered, affine)
    grad_pass(back, unit, mask, affine, stats, params, total_count(counts, 4), grad)
    send(grad, affine)
    step = 256
    for start in range(0, out.shape[1], step):
        columns = slice(start, start + step)
        value = dot_back(grad[...], weight[columns, :]) + block_back[:, columns]
        out[:, columns] = (value * wide(mask[...], step)).astype(BF16)


def dot_pixels(left, grad):
    return lax.dot_general(left, grad, (((0,), (0,)), ((), ())), preferred_element_type=F32)


def chip_grad(left, left_other, grad, grad_other, columns=slice(None)):
    half = left_other.shape[1]
    return dot_pixels(left[:, own_half(half)], grad[:, columns]) + dot_pixels(
        left_other[...], grad_other[:, columns]
    )


def bit_half(bit, flip, rows):
    mine = (lax.axis_index("img").astype(jnp.int32) >> bit) & 1
    return pl.ds(pl.multiple_of((1 - mine if flip else mine) * rows, 16), rows)


def round_part(low, bits, flip, rows):
    mine = (lax.axis_index("img").astype(jnp.int32) >> low) & ((1 << bits) - 1)
    return pl.ds(pl.multiple_of((mine ^ flip) * rows, 16), rows)


def deal(full, parts):
    rows, width = parts[0].shape
    for outs, flip in ((parts[2:], True), (parts[:2], False)):
        for group, out in enumerate(outs):
            out[...] = full[bit_half((0, 1)[group], flip, rows), group * width : (group + 1) * width]


def first_wave_kernel(
    short, short_other, strided, strided_other,
    short_grad, short_grad_other, expand_grad, expand_grad_other, full
):
    rows = short_other.shape[1]
    step = 512
    for start in range(0, full.shape[1], step):
        columns = slice(start, start + step)
        full[:rows, columns] = chip_grad(
            short, short_other, short_grad, short_grad_other, columns
        ).astype(BF16)
        full[rows:, columns] = chip_grad(
            strided, strided_other, expand_grad, expand_grad_other, columns
        ).astype(BF16)


def second_wave_kernel(
    taps, taps_other, strided_grad, strided_grad_other, *results
):
    *parts, full = results
    half = taps_other.shape[2] // 3
    channels = 2 * half
    for row_tap in range(3):
        for col_tap in range(3):
            start = pl.multiple_of(col_tap * channels + core_number() * half, LANES)
            own = dot_pixels(taps[row_tap, :, pl.ds(start, half)], strided_grad[...])
            other = dot_pixels(
                taps_other[row_tap, :, col_tap * half : (col_tap + 1) * half], strided_grad_other[...]
            )
            place_row = (3 * row_tap + col_tap) * half
            full[place_row : place_row + half, :] = (own + other).astype(BF16)
    deal(full, parts)


def fill_rest(full, row):
    if row < full.shape[0]:
        full[row:, :] = jnp.zeros((full.shape[0] - row, full.shape[1]), full.dtype)


def third_wave_kernel(
    dims, block, block_other, widen_grad, widen_grad_other, act, act_other, closing_grad,
    closing_grad_other, triple, triple_other, middle_grad, middle_grad_other, entry_in, entry_in_other, entry_grad,
    entry_grad_other, *results,
):
    *parts, full = results
    batch, height, width = dims
    pixels = height * width
    step = full.shape[1]
    row = 0
    for left, left_other, grad, grad_other in (
        (block, block_other, widen_grad, widen_grad_other),
        (act, act_other, closing_grad, closing_grad_other),
    ):
        rows = left_other.shape[1]
        for start in range(0, grad.shape[1], step):
            full[row : row + rows, :] = chip_grad(
                left, left_other, grad, grad_other, slice(start, start + step)
            ).astype(BF16)
            row += rows
    half = triple_other.shape[2] // 3
    channels = 2 * half
    for row_tap in range(3):
        lines = slice(row_tap * width, row_tap * width + pixels)
        for col_tap in range(3):
            start = pl.multiple_of(col_tap * channels + core_number() * half, LANES)
            own = triple[:, lines, pl.ds(start, half)].reshape(batch * pixels, half)
            other = triple_other[:, lines, col_tap * half : (col_tap + 1) * half].reshape(batch * pixels, half)
            value = dot_pixels(own, middle_grad[...]) + dot_pixels(other, middle_grad_other[...])
            full[row : row + half, :] = value.astype(BF16)
            row += half
    rows = entry_in_other.shape[1]
    full[row : row + rows, :] = chip_grad(entry_in, entry_in_other, entry_grad, entry_grad_other).astype(BF16)
    fill_rest(full, row + rows)
    deal(full, parts)


def added(parts, *index):
    total = parts[0][index].astype(F32)
    for part in parts[1:]:
        total = total + part[index].astype(F32)
    return total.astype(BF16)


def halve_kernel(kept_a, kept_b, got_a, got_b, *outs):
    rows = outs[0].shape[0]
    for targets, flip in ((outs[2:], True), (outs[:2], False)):
        for group, (out, parts) in enumerate(zip(targets, ((kept_a, got_a), (kept_b, got_b)))):
            out[...] = added(parts, bit_half((1, 0)[group], flip, rows), slice(None))


def part_order(count):
    return list(range(1, count)) + [0]


def quarter_kernel(step, kept_a, kept_b, got_a, got_b, *outs):
    rows = outs[0].shape[1]
    for flip in part_order(len(outs)):
        here = round_part(*step, flip, rows)
        for group, parts in enumerate(((kept_a, got_a), (kept_b, got_b))):
            outs[flip][group] = added(parts, here, slice(None))


def fold_kernel(count, step, *refs):
    parts, outs = refs[:count], refs[count:]
    rows = outs[0].shape[1]
    for flip in part_order(len(outs)):
        outs[flip][...] = added(parts, slice(None), round_part(*step, flip, rows), slice(None))


def add_kernel(*refs):
    *parts, out = refs
    out[...] = added(parts, slice(None))


def merge_kernel(count, step, *refs):
    parts, outs = refs[:count], refs[count:]
    rows = parts[0].shape[1]
    for flip, part in enumerate(parts):
        here = round_part(*step, flip, rows)
        if len(outs) == 1:
            outs[0][:, here, :] = part[...]
        else:
            for group, out in enumerate(outs):
                out[here, :] = part[group]


def double_kernel(own_a, own_b, got_a, got_b, *outs):
    rows = own_a.shape[0]
    for group, (out, own, got) in enumerate(zip(outs, (own_a, own_b), (got_a, got_b))):
        out[bit_half((1, 0)[group], False, rows), :] = own[...]
        out[bit_half((1, 0)[group], True, rows), :] = got[...]


def first_out(full, short, expand):
    rows = short.shape[0]
    short[...] = full[:rows, :].astype(F32)
    send(short)
    expand[...] = full[rows:, :].astype(F32)


def second_out(full, strided):
    rows = strided.shape[1]
    for tap in range(9):
        strided[tap] = full[tap * rows : (tap + 1) * rows, :].astype(F32)


def third_out(full, widen, closing, middle, entry):
    step = full.shape[1]
    row = 0
    for out in (widen, closing):
        rows = out.shape[0]
        for start in range(0, out.shape[1], step):
            out[:, start : start + step] = full[row : row + rows, :].astype(F32)
            row += rows
        send(out)
    rows = middle.shape[1]
    for tap in range(9):
        middle[tap] = full[row : row + rows, :].astype(F32)
        row += rows
    send(middle)
    entry[...] = full[row : row + entry.shape[0], :].astype(F32)


def out_kernel(finish, own_a, own_b, got_a, got_b, *refs):
    outs, full = refs[:-1], refs[-1]
    rows, width = own_a.shape
    for group, (own, got) in enumerate(((own_a, got_a), (own_b, got_b))):
        columns = slice(group * width, (group + 1) * width)
        full[bit_half((0, 1)[group], False, rows), columns] = own[...]
        full[bit_half((0, 1)[group], True, rows), columns] = got[...]
    finish(full, *outs)


def rounds():
    bits = lax.axis_size("img").bit_length() - 1
    return [(low, min(2, bits - low)) for low in range(2, bits, 2)]


def to_chip(value, flip):
    count = lax.axis_size("img")
    return lax.ppermute(value, "img", [(i, i ^ flip) for i in range(count)])


def sum_over_chips(order, parts, finish, outs, shape):
    steps = rounds()

    def run(kernel, shapes, *operands, scratch=(), free=True):
        results = call(kernel, shapes, *operands, free=free, after=(order[0],), scratch=scratch)
        order[0] = results[0]
        return results

    def exchange(values, low):
        return [to_chip(value, number << low) for number, value in enumerate(values, 1)]

    rows, width = shape[0] // 2, shape[1] // 2
    kept, sent = parts[:2], parts[2:]
    got = [to_chip(sent[0], 1), to_chip(sent[1], 2)]
    yield None
    rows //= 2
    results = run(halve_kernel, [((rows, width), BF16)] * 4, *kept, *got)
    kept, sent = results[:2], results[2:]
    got = [to_chip(sent[0], 2), to_chip(sent[1], 1)]
    yield None
    low, bits = steps[0]
    rows >>= bits
    parts = run(functools.partial(quarter_kernel, steps[0]), [((2, rows, width), BF16)] * (1 << bits), *kept, *got)
    dealt = 1
    for number, (low, bits) in enumerate(steps):
        if number < dealt:
            got = exchange(parts[1:], low)
        else:
            got = exchange([parts[0]] * ((1 << bits) - 1), low)
        yield None
        parts = [parts[0]] + got
        following = steps[number + 1] if number + 1 < len(steps) else None
        if following is not None and number + 1 == dealt and rows % (16 << following[1]) == 0:
            rows >>= following[1]
            dealt += 1
            parts = run(
                functools.partial(fold_kernel, len(parts), following),
                [((2, rows, width), BF16)] * (1 << following[1]),
                *parts,
            )
        else:
            parts = run(add_kernel, [((2, rows, width), BF16)], *parts)
    (share,) = parts
    for number in reversed(range(dealt)):
        low, bits = steps[number]
        got = exchange([share] * ((1 << bits) - 1), low)
        yield None
        rows <<= bits
        shapes = [((2, rows, width), BF16)] if number > 0 else [((rows, width), BF16)] * 2
        own = run(functools.partial(merge_kernel, 1 + len(got), steps[number]), shapes, share, *got)
        share = own[0]
    got = [to_chip(own[0], 2), to_chip(own[1], 1)]
    yield None
    rows *= 2
    own = run(double_kernel, [((rows, width), BF16)] * 2, *own, *got)
    got = [to_chip(own[0], 1), to_chip(own[1], 2)]
    yield None
    yield run(functools.partial(out_kernel, finish), outs, *own, *got, scratch=[(shape, BF16)], free=False)


def per_device(
    images,
    extents,
    entry_weight,
    middle_weight,
    closing_weight,
    widen_weight,
    strided_weight,
    expand_weight,
    shortcut_weight,
    entry_affine,
    middle_affine,
    closing_affine,
    widen_affine,
    strided_affine,
    expand_affine,
    shortcut_affine,
    cotangent,
):
    batch, height, width, wide_in = images.shape
    dims = (batch, height, width)
    pixels = batch * height * width
    small_pixels = pixels // 4
    chips = lax.axis_size("img")
    devices = chips * lax.axis_size("row")
    row = lax.axis_index("row")
    local = extents - jnp.stack([row * height, 0]).astype(jnp.int32)
    mid, wider, last = entry_weight.shape[1], widen_weight.shape[1], expand_weight.shape[1]

    def message_rows(channels):
        return max(8, 2 * channels // LANES)

    def message(channels):
        return ((devices, message_rows(channels), LANES), F32)

    def rows(channels):
        return ((message_rows(channels), LANES), F32)

    def stat(channels):
        return ((8, channels), F32)

    def level(count, channels):
        return [((count, channels), BF16), ((count, channels), F32), ((count, channels), F32), stat(channels)]

    def ops(count, *sizes):
        total = 2 * count
        for size in sizes:
            total *= size
        return total

    entry_in, mask, small, above, below, small_below, entry_raw, edge, sent, give = call(
        functools.partial(entry_kernel, dims),
        [
            ((pixels, wide_in), BF16),
            ((pixels, LANES), F32),
            ((small_pixels, LANES), F32),
            ((batch * width, LANES), F32),
            ((batch * width, LANES), F32),
            ((batch * width // 2, LANES), F32),
            ((pixels, mid), F32),
            ((batch * width, mid), F32),
            message(mid),
            ((pixels, wide_in // 2), BF16),
        ],
        local,
        images.reshape(pixels, wide_in),
        entry_weight,
        scratch=[rows(mid)],
        smem=(0,),
        late=(1, 2,),
        keep=(6, 7, 8),
        flops=ops(pixels, wide_in, mid),
    )
    halo = swap_rows(edge)
    entry_in_other = swap_rows(give)
    counts = gather_all(sent)
    padded_rows = batch * (height + 2) * width
    entry_unit, entry_slope, entry_stats, middle_raw, sent, triple, give = call(
        functools.partial(middle_kernel, dims),
        level(pixels, mid)[1:]
        + [
            ((pixels, mid), F32),
            message(mid),
            ((batch, (height + 2) * width, 3 * mid), BF16),
            ((batch, (height + 2) * width, 3 * mid // 2), BF16),
        ],
        counts,
        entry_raw,
        halo,
        mask,
        above,
        below,
        entry_affine,
        middle_weight.reshape(3, 3 * mid, mid),
        scratch=[rows(mid), ((padded_rows + 16, mid), F32)],

        late=(7,),
        keep=(3, 4),
        flops=ops(pixels, 9, mid, mid),
    )
    triple_other = swap_rows(give)
    gathered = gather_all(sent)
    middle_act, middle_unit, middle_slope, middle_stats, closing_raw, sent, give = call(
        closing_kernel,
        level(pixels, mid) + [((pixels, wide_in), F32), message(wide_in), ((pixels, mid // 2), BF16)],
        gathered,
        counts,
        middle_raw,
        mask,
        middle_affine,
        closing_weight,
        scratch=[rows(wide_in)],

        late=(5,),
        keep=(4, 5),
        flops=ops(pixels, mid, wide_in),
    )
    middle_act_other = swap_rows(give)
    gathered = gather_all(sent)
    block_out, closing_unit, block_slope, closing_stats, shortcut_in, widen_raw, edge, sent, give, give_short = call(
        functools.partial(widen_kernel, dims),
        level(pixels, wide_in)
        + [
            ((small_pixels, wide_in), BF16),
            ((pixels, wider), F32),
            ((batch * width, wider), F32),
            message(wider),
            ((pixels, wide_in // 2), BF16),
            ((small_pixels, wide_in // 2), BF16),
        ],
        gathered,
        counts,
        closing_raw,
        entry_in,
        mask,
        closing_affine,
        widen_weight,
        scratch=[rows(wider), ((wide_in // LANES, pixels, LANES), F32)],

        late=(3, 6,),
        keep=(5, 6, 7),
        flops=ops(pixels, wide_in, wider),
    )
    halo = swap_rows(edge)
    block_other, short_other = swap_rows(give), swap_rows(give_short)
    gathered = gather_all(sent)
    shortcut_raw, shortcut_rows = call(
        shortcut_kernel,
        [((small_pixels, last), F32), rows(last)],
        shortcut_in,
        small,
        shortcut_weight,
        late=(0, 2),
        keep=(),
        flops=ops(small_pixels, wide_in, last),
    )
    widen_unit, widen_slope, widen_stats, strided_raw, sent, taps, give = call(
        functools.partial(strided_kernel, dims),
        level(pixels, wider)[1:]
        + [
            ((small_pixels, wider), F32),
            message(wider),
            ((3, small_pixels, 3 * wider), BF16),
            ((3, small_pixels, 3 * wider // 2), BF16),
        ],
        gathered,
        counts,
        widen_raw,
        halo,
        mask,
        small,
        above,
        widen_affine,
        strided_weight.reshape(3, 3 * wider, wider),
        scratch=[rows(wider), ((wider // LANES, batch * (height + 1) * width + 16, LANES), F32)],

        late=(8,),
        keep=(3, 4),
        flops=ops(small_pixels, 9, wider, wider),
    )
    taps_other = swap_rows(give)
    gathered = gather_all(sent)
    pair_rows = message_rows(last) + 8
    strided_act, strided_unit, strided_slope, strided_stats, expand_raw, mine, theirs, give = call(
        expand_kernel,
        level(small_pixels, wider)
        + [
            ((small_pixels, last), F32),
            ((pair_rows, LANES), F32),
            ((pair_rows, LANES), F32),
            ((small_pixels, wider // 2), BF16),
        ],
        gathered,
        counts,
        strided_raw,
        small,
        strided_affine,
        expand_weight,
        shortcut_rows,
        scratch=[rows(last)],

        late=(5, 6,),
        keep=(4, 5, 6),
        flops=ops(small_pixels, wider, last),
    )
    strided_act_other = swap_rows(give)
    (sent,) = call(pair_kernel, [((chips, pair_rows, LANES), F32)], mine, swap_rows(theirs), keep=(0,))
    (own_stats,) = call(join_kernel, [stat(last)], gather_img(sent), keep=(0,))
    half_rows = 3 * last // (2 * LANES)
    features, final_grad, expand_unit, shortcut_unit, expand_stats, shortcut_stats, mine, theirs = call(
        final_kernel,
        [
            ((small_pixels, last), BF16),
            ((small_pixels, last), F32),
            ((small_pixels, last), F32),
            ((small_pixels, last), F32),
            stat(last),
            stat(last),
            ((half_rows, LANES), F32),
            ((half_rows, LANES), F32),
        ],
        own_stats,
        swap_rows(own_stats),
        expand_raw,
        shortcut_raw,
        small,
        expand_affine,
        shortcut_affine,
        cotangent.reshape(small_pixels, last),
        late=(3, 7,),
        keep=(1, 2, 3, 4, 5, 6, 7),
        scratch=[((3 * last // LANES, LANES), F32)],

    )

    joined = mine + swap_rows(theirs)
    own_sums = jnp.sum(gather_img(jnp.broadcast_to(joined[None], (chips,) + joined.shape)), axis=0)
    affine_expand, affine_shortcut, expand_grad, shortcut_grad, strided_back, edge, sent = call(
        functools.partial(last_grads_kernel, batch),
        [
            ((2, last), F32),
            ((2, last), F32),
            ((small_pixels, last), BF16),
            ((small_pixels, last), BF16),
            ((small_pixels, wider), F32),
            ((batch * width, wider), F32),
            message(wider),
        ],
        own_sums,
        swap_rows(own_sums),
        counts,
        final_grad,
        expand_unit,
        shortcut_unit,
        expand_stats,
        shortcut_stats,
        expand_affine,
        shortcut_affine,
        small,
        expand_weight,
        strided_slope,
        strided_unit,
        scratch=[rows(wider)],

        late=(11, 12, 13,),
        keep=(4, 5, 6),
        flops=ops(small_pixels, wider, last),
    )
    halo = swap_rows(edge)
    gathered = gather_all(sent)

    def small_image(value):
        return value.reshape(batch, height // 2, width // 2, value.shape[-1])

    def image(value):
        return value.reshape(batch, height, width, value.shape[-1])

    order = [affine_expand]

    def move(wave, times=1):
        for _ in range(times):
            result = next(wave)
        return result


    def wave_parts(kernel, shape, *operands, flops):
        parts = call(
            kernel,
            [((shape[0] // 2, shape[1] // 2), BF16)] * 4,
            *operands,
            scratch=[(shape, BF16)],
            flops=flops,
            late=None,
            free=True,
            after=(order[0],),
        )
        order[0] = parts[0]
        return parts

    def moving_sum(parts, shape, finish, outs):
        moving = sum_over_chips(order, parts, finish, outs, shape)
        move(moving)
        return moving

    first_shape = ((wide_in + wider) // 2, last)
    (first,) = call(
        first_wave_kernel,
        [(first_shape, BF16)],
        shortcut_in,
        short_other,
        strided_act,
        strided_act_other,
        shortcut_grad,
        swap_rows(shortcut_grad),
        expand_grad,
        swap_rows(expand_grad),

        flops=ops(2 * small_pixels, *first_shape),
        late=None,
        after=(order[0],),
    )
    order[0] = first
    first = lax.psum(first, "img")

    affine_strided, strided_grad, widen_back, sent = call(
        functools.partial(widen_back_kernel, dims),
        [((2, wider), F32), ((small_pixels, wider), BF16), ((pixels, wider), F32), message(wider)],
        gathered,
        counts,
        strided_back,
        strided_unit,
        halo,
        small,
        small_below,
        strided_stats,
        strided_affine,
        strided_weight,
        widen_unit,
        widen_slope,
        scratch=[
            rows(wider),
            ((batch * (height // 2 + 1) * width // 2 + 8, wider), F32),
            ((wider // LANES, pixels, LANES), F32),
        ],
        late=(3, 9, 10, 11),
        keep=(2, 3),
        after=(order[0],),
        flops=ops(small_pixels, 9, wider, wider),
    )
    gathered = gather_all(sent)
    order[0] = affine_strided
    strided_grad_other = swap_rows(strided_grad)
    (short_back,) = call(
        functools.partial(short_back_kernel, dims),
        [((wide_in // LANES, pixels, LANES), F32)],
        shortcut_grad,
        shortcut_weight,
        late=(0, 1),
        keep=(),
        after=(order[0],),
        flops=ops(small_pixels, wide_in, last),
    )
    order[0] = short_back
    affine_widen, widen_grad, block_back, sent, block_back_saved = call(
        block_back_kernel,
        [
            ((2, wider), F32),
            ((pixels, wider), BF16),
            ((pixels, wide_in), F32),
            message(wide_in),
            ((pixels, wide_in), F32),
        ],
        gathered,
        counts,
        widen_back,
        widen_unit,
        mask,
        widen_stats,
        widen_affine,
        widen_weight,
        short_back,
        closing_unit,
        block_slope,
        scratch=[rows(wide_in)],
        late=(3, 7, 8, 9, 10),
        keep=(2, 3),
        after=(order[0],),
        flops=ops(pixels, wide_in, wider),
    )
    gathered = gather_all(sent)

    order[0] = affine_widen
    widen_grad_other = swap_rows(widen_grad)
    second_shape = (9 * wider // 2, wider)
    second_parts = wave_parts(
        second_wave_kernel,
        second_shape,
        taps,
        taps_other,
        strided_grad,
        strided_grad_other,
        flops=ops(2 * small_pixels, *second_shape),
    )
    second = moving_sum(second_parts, second_shape, second_out, [((9, wider // 2, wider), F32)])

    affine_closing, closing_grad, middle_back, edge, sent = call(
        functools.partial(middle_back_kernel, dims),
        [
            ((2, wide_in), F32),
            ((pixels, wide_in), BF16),
            ((pixels, mid), F32),
            ((2 * batch * width, mid), F32),
            message(mid),
        ],
        gathered,
        counts,
        block_back,
        closing_unit,
        mask,
        closing_stats,
        closing_affine,
        closing_weight,
        middle_unit,
        middle_slope,
        scratch=[rows(mid)],

        late=(3, 7, 8, 9,),
        keep=(2, 3, 4),
        after=(order[0],),
        flops=ops(pixels, wide_in, mid),
    )
    halo = swap_rows(edge)
    gathered = gather_all(sent)
    order[0] = affine_closing
    closing_grad_other = swap_rows(closing_grad)
    affine_middle, middle_grad, entry_back, sent = call(
        functools.partial(entry_back_kernel, dims),
        [((2, mid), F32), ((pixels, mid), BF16), ((pixels, mid), F32), message(mid)],
        gathered,
        counts,
        middle_back,
        middle_unit,
        halo,
        mask,
        above,
        below,
        middle_stats,
        middle_affine,
        middle_weight,
        entry_unit,
        entry_slope,
        scratch=[rows(mid), ((padded_rows + 16, mid), F32), ((batch, (height + 2) * width, 3 * mid), BF16)],
        late=(3, 10, 11, 12),
        keep=(2, 3),
        after=(order[0],),
        flops=ops(pixels, 9, mid, mid),
    )
    gathered = gather_all(sent)
    order[0] = affine_middle
    middle_grad_other = swap_rows(middle_grad)
    move(second)
    affine_entry, entry_grad, image_grads = call(
        images_kernel,
        [((2, mid), F32), ((pixels, mid), BF16), ((pixels, wide_in), BF16)],
        gathered,
        counts,
        entry_back,
        entry_unit,
        mask,
        entry_stats,
        entry_affine,
        entry_weight,
        block_back_saved,
        late=(3, 7, 8),
        keep=(),
        after=(order[0],),
        flops=ops(pixels, mid, wide_in),
    )

    order[0] = affine_entry
    third_sizes = (wide_in // 2 * wider // mid, wide_in // 2, 9 * mid // 2, wide_in // 2)
    third_shape = (-(-sum(third_sizes) // 256) * 256, mid)
    third_parts = wave_parts(
        functools.partial(third_wave_kernel, dims),
        third_shape,
        block_out,
        block_other,
        widen_grad,
        widen_grad_other,
        middle_act,
        middle_act_other,
        closing_grad,
        closing_grad_other,
        triple,
        triple_other,
        middle_grad,
        middle_grad_other,
        entry_in,
        entry_in_other,
        entry_grad,
        swap_rows(entry_grad),
        flops=ops(2 * pixels, *third_shape),
    )
    third = moving_sum(
        third_parts,
        third_shape,
        third_out,
        [
            ((wide_in // 2, wider), F32),
            ((mid // 2, wide_in), F32),
            ((9, mid // 2, mid), F32),
            ((wide_in // 2, mid), F32),
        ],
    )
    totals = {}
    for name in "bcbcbcbcbcbac":
        if name == "a":
            totals["a"] = call(
                first_out,
                [((wide_in // 2, last), F32), ((wider // 2, last), F32)],
                first,
                late=None,
                after=(order[0],),
            )
            order[0] = totals["a"][0]
        elif name not in totals:
            result = move(second if name == "b" else third)
            if result is not None:
                totals[name] = result
    for name, moving in (("b", second), ("c", third)):
        while name not in totals:
            result = move(moving)
            if result is not None:
                totals[name] = result
    shortcut_total, expand_total = totals["a"]
    (strided_total,) = totals["b"]
    widen_total, closing_total, middle_total, entry_total = totals["c"]
    middle_total = middle_total.reshape(3, 3, mid // 2, mid)
    strided_total = strided_total.reshape(3, 3, wider // 2, wider)
    return (
        small_image(features),
        image(image_grads),
        entry_total,
        middle_total,
        closing_total,
        widen_total,
        strided_total,
        expand_total,
        shortcut_total,
        affine_entry,
        affine_middle,
        affine_closing,
        affine_widen,
        affine_strided,
        affine_expand,
        affine_shortcut,
    )


def solution(mesh):
    image = P("img", "row", None, None)
    return jax.shard_map(
        per_device,
        mesh=mesh,
        in_specs=(image, P("img", None)) + (P(),) * 14 + (image,),
        out_specs=(
            image,
            image,
            P("row", None),
            P(None, None, "row", None),
            P("row", None),
            P("row", None),
            P(None, None, "row", None),
            P("row", None),
            P("row", None),
        )
        + (P(),) * 7,
        check_vma=False,
    )
```

```python
import functools
import math

import jax
import jax.numpy as jnp
from jax import lax
from jax.experimental import pallas as pl
from jax.experimental.pallas import tpu as pltpu
from jax.sharding import PartitionSpec as P

EPS = 1e-05
BOTH = ("img", "row")
F32 = jnp.float32
BF16 = jnp.bfloat16
LANES = 128
MIB = 1 << 20


def swap_rows(value):
    count = lax.axis_size("row")
    return lax.ppermute(value, "row", [(i, (i + 1) % count) for i in range(count)])


def gather_all(message):
    return lax.all_to_all(message, BOTH, 0, 0, tiled=True)


def gather_img(message):
    return lax.all_to_all(message, "img", 0, 0, tiled=True)


class Late:
    def __init__(self, source, buffer, semaphores):
        self.buffer = buffer
        self.shape, self.ndim, self.dtype = buffer.shape, len(buffer.shape), buffer.dtype
        parts = parts_of(self.shape)
        if parts == 1:
            self.copies = [pltpu.make_async_copy(source, buffer, semaphores.at[0])]
        else:
            self.copies = [
                pltpu.make_async_copy(source.at[i], buffer.at[i], semaphores.at[i]) for i in range(parts)
            ]
        for copy in self.copies:
            copy.start()
        self.waiting = set(range(parts))

    def ready(self, part=None):
        for i in sorted(self.waiting):
            if part is None or i == part:
                self.copies[i].wait()
                self.waiting.remove(i)
        return self.buffer

    def __getitem__(self, index):
        first = index[0] if isinstance(index, tuple) else index
        part = first if isinstance(first, int) and len(self.copies) > 1 else None
        return self.ready(part)[index]


def parts_of(shape):
    return shape[0] if len(shape) >= 3 and shape[0] == 3 else 1


class Saved:
    def __init__(self, target, buffer, semaphore):
        self.target, self.buffer, self.semaphore, self.copy = target, buffer, semaphore, None
        self.shape, self.ndim, self.dtype = buffer.shape, len(buffer.shape), buffer.dtype

    def send(self):
        if self.copy is None:
            self.copy = pltpu.make_async_copy(self.buffer, self.target, self.semaphore)
            self.copy.start()

    def __getitem__(self, index):
        return self.buffer[index]

    def __setitem__(self, index, value):
        self.buffer[index] = value


def send(*results):
    for result in results:
        if isinstance(result, Saved):
            result.send()


def call(kernel, outs, *operands, scratch=(), smem=(), late=(), flops=0, keep=(), limit=24, after=(), free=False):
    late = [place for place in (range(len(operands)) if late is None else late) if place not in smem]
    used = len(operands)
    operands += tuple(after)
    saved = [place for place in range(len(outs)) if place not in keep and not free]
    moved = sum(x.size * x.dtype.itemsize for x in operands) + sum(
        math.prod(shape) * jnp.dtype(dtype).itemsize for shape, dtype in outs
    )

    def place_of_operand(place):
        if place in smem:
            return pltpu.SMEM
        return pl.ANY if place in late or place >= used else pltpu.VMEM

    operands = [
        pltpu.with_memory_space_constraint(x, pltpu.HBM) if place in late or (place >= used and in_hbm(x)) else x
        for place, x in enumerate(operands)
    ]
    buffers = [pltpu.VMEM(operands[place].shape, operands[place].dtype) for place in late]
    buffers += [pltpu.VMEM(*outs[place]) for place in saved]
    semaphores = [pltpu.SemaphoreType.DMA((parts_of(operands[place].shape),)) for place in late]
    semaphores += [pltpu.SemaphoreType.DMA] * len(saved)

    def body(*refs):
        refs = list(refs)
        inputs, refs = refs[: len(operands)], refs[len(operands) :]
        results, refs = refs[: len(outs)], refs[len(outs) :]
        own, refs = refs[: len(scratch)], refs[len(scratch) :]
        space, marks = refs[: len(buffers)], refs[len(buffers) :]
        for number, place in enumerate(late):
            inputs[place] = Late(inputs[place], space[number], marks[number])
        for number, place in enumerate(saved):
            number += len(late)
            results[place] = Saved(results[place], space[number], marks[number])
        kernel(*inputs[:used], *results, *own)
        for place in late:
            inputs[place].ready()
        for place in saved:
            results[place].send()
        for place in saved:
            results[place].copy.wait()

    results = pl.pallas_call(
        body,
        out_shape=[
            jax.ShapeDtypeStruct(shape, dtype)
            if free
            else (pltpu.VMEM if place in keep else pltpu.HBM)(shape, dtype)
            for place, (shape, dtype) in enumerate(outs)
        ],
        in_specs=[pl.BlockSpec(memory_space=place_of_operand(place)) for place in range(len(operands))],
        out_specs=[
            pl.BlockSpec(memory_space=pl.ANY if place in saved else pltpu.VMEM) for place in range(len(outs))
        ],
        scratch_shapes=[pltpu.VMEM(shape, dtype) for shape, dtype in scratch] + buffers + semaphores,
        compiler_params=pltpu.CompilerParams(vmem_limit_bytes=limit * MIB),
        cost_estimate=pl.CostEstimate(flops=flops, bytes_accessed=moved, transcendentals=0),
    )(*operands)
    HELD.extend(results[place] for place in saved)
    return results


HELD = []


def in_hbm(value):
    return any(value is held for held in HELD)


def dot(left, right):
    return jnp.dot(left, right, preferred_element_type=F32)


def dot_back(grad, weight):
    return lax.dot_general(grad, weight, (((1,), (1,)), ((), ())), preferred_element_type=F32)


def wide(mask, width):
    return mask if width == LANES else jnp.concatenate([mask] * (width // LANES), axis=1)


def column_sum(value):
    return jnp.sum(value, axis=0, keepdims=True)


def spread_message(message, rows):
    tile = rows[...]
    for device in range(message.shape[0]):
        message[device] = tile


def put_row(rows, place, vector):
    for block in range(vector.shape[1] // LANES):
        rows[place + block : place + block + 1, :] = vector[:, block * LANES : (block + 1) * LANES]


def local_stats(raw, mask, rows, place=0):
    blocks = raw.shape[1] // LANES
    number = jnp.maximum(column_sum(mask[...]), 1.0)
    for block in range(blocks):
        columns = slice(block * LANES, (block + 1) * LANES)
        total = column_sum(raw[:, columns] * mask[...])
        centred = (raw[:, columns] - total / number) * mask[...]
        rows[place + block : place + block + 1, :] = total
        rows[place + blocks + block : place + blocks + block + 1, :] = column_sum(centred * centred)


def total_count(counts, place):
    return functools.reduce(
        jnp.add, [counts[i, place : place + 1, :] for i in range(counts.shape[0])]
    )


def join_stats(gathered, counts, place, stats, blocks):
    devices = gathered.shape[0]
    count = total_count(counts, place)
    mean = functools.reduce(jnp.add, [gathered[i, :blocks, :] for i in range(devices)]) / count
    spread = functools.reduce(jnp.add, [gathered[i, blocks : 2 * blocks, :] for i in range(devices)])
    for i in range(devices):
        number = counts[i, place : place + 1, :]
        shift = gathered[i, :blocks, :] / jnp.maximum(number, 1.0) - mean
        spread = spread + number * (shift * shift)
    scale = lax.rsqrt(spread / count + EPS)
    for block in range(blocks):
        columns = slice(block * LANES, (block + 1) * LANES)
        stats[0:1, columns] = mean[block : block + 1, :]
        stats[1:2, columns] = scale[block : block + 1, :]


def join_sums(gathered, affine):
    total = functools.reduce(jnp.add, [gathered[i] for i in range(gathered.shape[0])])
    blocks = affine.shape[1] // LANES
    for block in range(blocks):
        columns = slice(block * LANES, (block + 1) * LANES)
        affine[0:1, columns] = total[block : block + 1, :]
        affine[1:2, columns] = total[blocks + block : blocks + block + 1, :]


def chunks(rows, width, chunk=32, block=256):
    for start in range(0, width, block):
        for row in range(0, rows, chunk):
            yield slice(row, row + min(chunk, rows - row)), slice(start, start + min(block, width - start))


def silu_parts(value):
    gate = jax.nn.sigmoid(value)
    return value * gate, gate * (1.0 + value * (1.0 - gate))


def normed(raw, stats, params, columns):
    unit = (raw - stats[0:1, columns]) * stats[1:2, columns]
    return unit, unit * params[0:1, columns] + params[1:2, columns]


def act_pass(raw, mask, stats, params, unit, slope, act, skip=None, keep=None):
    rows, width = raw.shape
    for here, columns in chunks(rows, width):
        u, value = normed(raw[here, columns], stats, params, columns)
        if skip is not None:
            value = value + skip[here, columns].astype(F32)
        m = wide(mask[here, :], columns.stop - columns.start)
        out, rise = silu_parts(value)
        out = out * m
        unit[here, columns] = u
        slope[here, columns] = rise * m
        if act is not None:
            act[here, columns] = out.astype(BF16)
        if keep is not None:
            keep(here, columns, out)


def back_pass(back, unit, slope, rows):
    blocks = back.shape[1] // LANES
    for block in range(blocks):
        columns = slice(block * LANES, (block + 1) * LANES)
        value = back[:, columns] * slope[:, columns]
        back[:, columns] = value
        rows[block : block + 1, :] = column_sum(value * unit[:, columns])
        rows[blocks + block : blocks + block + 1, :] = column_sum(value)


def raw_grad(back, unit, mask, sums, stats, params, count, columns):
    width = columns.stop - columns.start
    n = wide(count, width)
    factor = params[0:1, columns] * stats[1:2, columns]
    centred = back - sums[1:2, columns] / n - unit * (sums[0:1, columns] / n)
    return factor * centred * wide(mask, width)


def grad_pass(back, unit, mask, sums, stats, params, count, grad, keep=None):
    for here, columns in chunks(*back.shape):
        value = raw_grad(
            back[here, columns], unit[here, columns], mask[here, :], sums, stats, params, count, columns
        )
        grad[here, columns] = value.astype(BF16)
        if keep is not None:
            keep(here, columns, value)


def valid(extents, image, first_row, columns, shape, step):
    place = lax.broadcasted_iota(jnp.int32, shape, 0)
    row = first_row + step * (place // columns)
    column = step * (place % columns)
    return jnp.where((row < extents[image, 0]) & (column < extents[image, 1]), 1.0, 0.0).astype(F32)


def core_number():
    return lax.axis_index("row").astype(jnp.int32)


def is_upper():
    return jnp.where(core_number() == 0, 1.0, 0.0).astype(F32)


def own_half(size):
    return pl.ds(pl.multiple_of(core_number() * size, LANES), size)


def other_half(size):
    return pl.ds(pl.multiple_of((1 - core_number()) * size, LANES), size)


def give_half(value, give):
    give[...] = value[:, other_half(give.shape[1])]
    send(give)


def entry_kernel(
    dims, extents, images, weight,
    entry_in, mask, small, above, below, small_below, raw, edge, message, give, rows,
):
    batch, height, width = dims
    pixels = height * width
    upper = is_upper()
    for b in range(batch):
        mask[b * pixels : (b + 1) * pixels, :] = valid(extents, b, 0, width, (pixels, LANES), 1)
        small[b * pixels // 4 : (b + 1) * pixels // 4, :] = valid(
            extents, b, 0, width // 2, (pixels // 4, LANES), 2
        )
        line = slice(b * width, (b + 1) * width)
        above[line, :] = valid(extents, b, -1, width, (width, LANES), 1) * (1.0 - upper)
        below[line, :] = valid(extents, b, height, width, (width, LANES), 1) * upper
        small_below[b * width // 2 : (b + 1) * width // 2, :] = (
            valid(extents, b, height, width // 2, (width // 2, LANES), 2) * upper
        )
    for here, columns in chunks(*images.shape):
        m = wide(mask[here, :], columns.stop - columns.start)
        entry_in[here, columns] = (images[here, columns].astype(F32) * m).astype(BF16)
    send(entry_in, mask, small, above, below, small_below)
    give_half(entry_in, give)
    raw[...] = dot(entry_in[...], weight[...])
    for b in range(batch):
        first = raw[b * pixels : b * pixels + width, :]
        last = raw[(b + 1) * pixels - width : (b + 1) * pixels, :]
        edge[b * width : (b + 1) * width, :] = last * upper + first * (1.0 - upper)
    rows[...] = jnp.zeros_like(rows)
    local_stats(raw, mask, rows)
    blocks = raw.shape[1] // LANES
    rows[2 * blocks : 2 * blocks + 1, :] = column_sum(mask[...])
    rows[2 * blocks + 1 : 2 * blocks + 2, :] = column_sum(small[...])
    spread_message(message, rows)


def put_blocks(target, here, columns, value):
    for start in range(columns.start, columns.stop, LANES):
        offset = start - columns.start
        target[start // LANES, here, :] = value[:, offset : offset + LANES]


def column_masks(rows, width):
    place = lax.broadcasted_iota(jnp.int32, (rows, LANES), 0) % width
    return (
        jnp.where(place == 0, 0.0, 1.0).astype(F32),
        jnp.where(place == width - 1, 0.0, 1.0).astype(F32),
    )


def fill_triple(padded, triple, batch, lines, width):
    size = lines * width
    channels = padded.shape[1]
    left_ok, right_ok = column_masks(size, width)
    for b in range(batch):
        start = 8 + b * size
        for c in range(0, channels, LANES):
            columns = slice(c, c + LANES)
            triple[b, :, c : c + LANES] = (padded[start - 1 : start - 1 + size, columns] * left_ok).astype(BF16)
            triple[b, :, channels + c : channels + c + LANES] = padded[start : start + size, columns].astype(BF16)
            triple[b, :, 2 * channels + c : 2 * channels + c + LANES] = (
                padded[start + 1 : start + 1 + size, columns] * right_ok
            ).astype(BF16)


def middle_kernel(
    dims, gathered, raw, halo, mask, above, below, params, weight,
    unit, slope, stats, out, message, triple, give, rows, padded,
):
    batch, height, width = dims
    pixels = height * width
    size = pixels + 2 * width
    blocks = raw.shape[1] // LANES
    join_stats(gathered, gathered, 2 * blocks, stats, blocks)
    everything = slice(0, raw.shape[1])
    _, value = normed(halo[...], stats, params, everything)
    rim, _ = silu_parts(value)
    padded[0:8, :] = jnp.zeros((8, raw.shape[1]), F32)
    padded[8 + batch * size :, :] = jnp.zeros((8, raw.shape[1]), F32)
    for b in range(batch):
        line = slice(b * width, (b + 1) * width)
        top = 8 + b * size
        padded[top : top + width, :] = rim[line] * wide(above[line, :], raw.shape[1])
        padded[top + size - width : top + size, :] = rim[line] * wide(below[line, :], raw.shape[1])

    def keep(here, columns, value):
        b = here.start // pixels
        start = 8 + b * size + width + here.start - b * pixels
        padded[start : start + here.stop - here.start, columns] = value

    act_pass(raw, mask, stats, params, unit, slope, None, keep=keep)
    send(unit, slope, stats)
    fill_triple(padded, triple, batch, height + 2, width)
    send(triple)
    give_taps(triple, give)
    total = None
    for tap in range(3):
        left = triple[:, tap * width : tap * width + pixels, :].reshape(batch * pixels, -1)
        part = dot(left, weight[tap])
        total = part if total is None else total + part
    out[...] = total
    local_stats(out, mask, rows)
    spread_message(message, rows)


def give_taps(taps, give):
    full, half = taps.shape[2] // 3, give.shape[2] // 3
    for tap in range(3):
        start = pl.multiple_of(tap * full + (1 - core_number()) * half, LANES)
        give[:, :, tap * half : (tap + 1) * half] = taps[:, :, pl.ds(start, half)]
    send(give)


def closing_kernel(
    gathered, counts, raw, mask, params, weight, act, unit, slope, stats, out, message, give, rows
):
    blocks = raw.shape[1] // LANES
    join_stats(gathered, counts, 4, stats, blocks)
    act_pass(raw, mask, stats, params, unit, slope, act)
    send(unit, slope, act, stats)
    give_half(act, give)
    out[...] = dot(act[...], weight[...])
    local_stats(out, mask, rows)
    spread_message(message, rows)


def widen_kernel(
    dims, gathered, counts, raw, entry_in, mask, params, weight,
    act, unit, slope, stats, short, out, edge, message, give, give_short, rows, even,
):
    batch, height, width = dims
    pixels = height * width
    blocks = raw.shape[1] // LANES
    join_stats(gathered, counts, 4, stats, blocks)

    def keep(here, columns, value):
        put_blocks(even, here, columns, value)

    act_pass(raw, mask, stats, params, unit, slope, act, skip=entry_in, keep=keep)
    send(unit, slope, act, stats)
    give_half(act, give)
    out[...] = dot(act[...], weight[...])
    for b in range(batch):
        edge[b * width : (b + 1) * width, :] = out[(b + 1) * pixels - width : (b + 1) * pixels, :]
    local_stats(out, mask, rows)
    spread_message(message, rows)
    for c in range(0, raw.shape[1], LANES):
        columns = slice(c, c + LANES)
        lines = []
        for b in range(batch):
            for i in range(height // 2):
                lines.append(even[c // LANES, pl.ds(b * pixels + 2 * i * width, width // 2, stride=2), :])
        short[:, columns] = jnp.concatenate(lines, axis=0).astype(BF16)
    send(short)
    give_half(short, give_short)


def shortcut_kernel(short, small, weight, out, rows):
    out[...] = dot(short[...], weight[...])
    send(out)
    local_stats(out, small, rows)


def strided_kernel(
    dims, gathered, counts, raw, halo, mask, small, above, params, weight,
    unit, slope, stats, out, message, taps, give, rows, padded,
):
    batch, height, width = dims
    pixels = height * width
    size = pixels + width
    half, half_width = height // 2, width // 2
    blocks = raw.shape[1] // LANES
    join_stats(gathered, counts, 4, stats, blocks)
    everything = slice(0, raw.shape[1])
    _, value = normed(halo[...], stats, params, everything)
    rim, _ = silu_parts(value)
    for block in range(padded.shape[0]):
        padded[block, 0:8, :] = jnp.zeros((8, LANES), F32)
    for b in range(batch):
        line = slice(b * width, (b + 1) * width)
        start = 8 + b * size
        put_blocks(padded, slice(start, start + width), everything, rim[line] * wide(above[line, :], raw.shape[1]))

    def keep(here, columns, value):
        b = here.start // pixels
        start = 8 + b * size + width + here.start - b * pixels
        put_blocks(padded, slice(start, start + here.stop - here.start), columns, value)

    act_pass(raw, mask, stats, params, unit, slope, None, keep=keep)
    send(unit, slope, stats)
    lines = height + 1
    not_first, _ = column_masks(lines * half_width, half_width)
    channels = raw.shape[1]
    for block in range(channels // LANES):
        for b in range(batch):
            start = 8 + b * size
            before = padded[block, pl.ds(start - 1, lines * half_width, stride=2), :] * not_first
            at = padded[block, pl.ds(start, lines * half_width, stride=2), :]
            after = padded[block, pl.ds(start + 1, lines * half_width, stride=2), :]
            for k, value in enumerate((before, at, after)):
                value = value.reshape(lines, half_width, LANES)
                place = k * channels + block * LANES
                for tap in range(3):
                    pieces = [value[tap + 2 * i] for i in range(half)]
                    taps[tap, b * half * half_width : (b + 1) * half * half_width, place : place + LANES] = (
                        jnp.concatenate(pieces, axis=0).astype(BF16)
                    )
    send(taps)
    give_taps(taps, give)
    total = None
    for tap in range(3):
        part = dot(taps[tap], weight[tap])
        total = part if total is None else total + part
    out[...] = total
    local_stats(out, small, rows)
    spread_message(message, rows)


def expand_kernel(
    gathered, counts, raw, small, params, weight, short_rows,
    act, unit, slope, stats, out, mine, theirs, give, rows,
):
    blocks = raw.shape[1] // LANES
    join_stats(gathered, counts, 5, stats, blocks)
    act_pass(raw, small, stats, params, unit, slope, act)
    send(unit, slope, act, stats)
    give_half(act, give)
    out[...] = dot(act[...], weight[...])
    local_stats(out, small, rows)
    upper = is_upper()
    size = rows.shape[0]
    number = jnp.broadcast_to(column_sum(small[...]), (8, LANES))
    mine[:size, :] = rows[...] * upper + short_rows[...] * (1.0 - upper)
    theirs[:size, :] = rows[...] * (1.0 - upper) + short_rows[...] * upper
    mine[size:, :] = number
    theirs[size:, :] = number


def pair_kernel(mine, other, message):
    size = mine.shape[0] - 8
    blocks = size // 2
    first, second = mine[size : size + 1, :], other[size : size + 1, :]
    both = first + second
    gap = mine[:blocks, :] / jnp.maximum(first, 1.0) - other[:blocks, :] / jnp.maximum(second, 1.0)
    weight = first * second / jnp.maximum(both, 1.0)
    total = mine[:blocks, :] + other[:blocks, :]
    square = mine[blocks:size, :] + other[blocks:size, :] + gap * gap * weight
    number = jnp.broadcast_to(both, (8, LANES))
    for i in range(message.shape[0]):
        message[i, :blocks, :] = total
        message[i, blocks:size, :] = square
        message[i, size:, :] = number


def join_kernel(gathered, stats):
    size = gathered.shape[1] - 8
    stats[...] = jnp.zeros_like(stats)
    join_stats(gathered, gathered, size, stats, size // 2)


def final_kernel(
    own, other, expand_raw, short_raw, small, expand_params, short_params, cotangent,
    features, grad, expand_unit, short_unit, expand_stats, short_stats, mine, theirs, rows,
):
    upper = is_upper()
    expand_stats[...] = own[...] * upper + other[...] * (1.0 - upper)
    short_stats[...] = own[...] * (1.0 - upper) + other[...] * upper
    height, width = expand_raw.shape
    blocks = width // LANES
    for block in range(blocks):
        columns = slice(block * LANES, (block + 1) * LANES)
        first, first_value = normed(expand_raw[:, columns], expand_stats, expand_params, columns)
        second, second_value = normed(short_raw[:, columns], short_stats, short_params, columns)
        out, rise = silu_parts(first_value + second_value)
        features[:, columns] = (out * small[...]).astype(BF16)
        value = cotangent[:, columns].astype(F32) * (rise * small[...])
        grad[:, columns] = value
        expand_unit[:, columns] = first
        short_unit[:, columns] = second
        rows[block : block + 1, :] = column_sum(value * first)
        rows[blocks + block : blocks + block + 1, :] = column_sum(value * second)
        rows[2 * blocks + block : 2 * blocks + block + 1, :] = column_sum(value)
    half = blocks // 2
    for stat in range(3):
        low = rows[stat * blocks : stat * blocks + half, :]
        high = rows[stat * blocks + half : (stat + 1) * blocks, :]
        mine[stat * half : (stat + 1) * half, :] = low * upper + high * (1.0 - upper)
        theirs[stat * half : (stat + 1) * half, :] = low * (1.0 - upper) + high * upper


def last_grads_kernel(
    batch, own, other, counts, grad, expand_unit, short_unit, expand_stats, short_stats,
    expand_params, short_params, small, weight, slope, unit,
    expand_affine, short_affine, expand_grad, short_grad, back, edge, message, rows,
):
    upper = is_upper()
    half = own.shape[0] // 3
    for stat in range(3):
        part = slice(stat * half, (stat + 1) * half)
        low = own[part, :] * upper + other[part, :] * (1.0 - upper)
        high = own[part, :] * (1.0 - upper) + other[part, :] * upper
        for block in range(2 * half):
            value = low[block : block + 1, :] if block < half else high[block - half : block - half + 1, :]
            columns = slice(block * LANES, (block + 1) * LANES)
            if stat == 0:
                expand_affine[0:1, columns] = value
            elif stat == 1:
                short_affine[0:1, columns] = value
            else:
                expand_affine[1:2, columns] = value
                short_affine[1:2, columns] = value
    count = total_count(counts, 5)
    for here, columns in chunks(*grad.shape):
        expand_grad[here, columns] = raw_grad(
            grad[here, columns], expand_unit[here, columns], small[here, :], expand_affine, expand_stats,
            expand_params, count, columns,
        ).astype(BF16)
        short_grad[here, columns] = raw_grad(
            grad[here, columns], short_unit[here, columns], small[here, :], short_affine, short_stats,
            short_params, count, columns,
        ).astype(BF16)
    send(expand_grad, short_grad, expand_affine, short_affine)
    back[...] = dot_back(expand_grad[...], weight[...])
    back_pass(back, unit, slope, rows)
    spread_message(message, rows)
    pixels = back.shape[0] // batch
    line = edge.shape[0] // (2 * batch)
    for b in range(batch):
        edge[b * line : (b + 1) * line, :] = back[b * pixels : b * pixels + line, :]
        edge[(batch + b) * line : (batch + b + 1) * line, :] = unit[b * pixels : b * pixels + line, :]


def short_back_kernel(dims, grad, weight, out):
    batch, height, width = dims
    pixels = height * width
    small = dot_back(grad[...], weight[...])
    out[...] = jnp.zeros(out.shape, out.dtype)
    half = width // 2
    for block in range(out.shape[0]):
        columns = slice(block * LANES, (block + 1) * LANES)
        for b in range(batch):
            for i in range(height // 2):
                place = b * pixels // 4 + i * half
                start = b * pixels + 2 * i * width
                out[block, pl.ds(start, half, stride=2), :] = small[place : place + half, columns]


def widen_back_kernel(
    dims, gathered, counts, back, unit, halo, small, small_below, stats, params, weight, out_unit, out_slope,
    affine, grad, out, message, rows, padded, full,
):
    batch, height, width = dims
    pixels = height * width
    half, half_width = height // 2, width // 2
    size = (half + 1) * half_width
    join_sums(gathered, affine)
    count = total_count(counts, 5)
    channels = back.shape[1]
    everything = slice(0, channels)
    line = batch * half_width
    rim = raw_grad(
        halo[:line, :], halo[line:, :], small_below[...], affine, stats, params, count, everything
    ).astype(BF16).astype(F32)
    for b in range(batch):
        stop = (b + 1) * size
        padded[stop - half_width : stop, :] = rim[b * half_width : (b + 1) * half_width]
    padded[batch * size :, :] = jnp.zeros((8, channels), F32)
    small_pixels = half * half_width
    for here, columns in chunks(back.shape[0], channels, chunk=small_pixels):
        value = raw_grad(
            back[here, columns], unit[here, columns], small[here, :], affine, stats, params, count, columns
        ).astype(BF16)
        grad[here, columns] = value
        b = here.start // small_pixels
        padded[b * size : b * size + small_pixels, columns] = value.astype(F32)
    send(grad, affine)
    _, not_last = column_masks(small_pixels, half_width)
    not_last = wide(not_last, channels)

    def moved(down, right):
        pieces = []
        for b in range(batch):
            start = b * size + down * half_width + right
            piece = padded[start : start + small_pixels, :]
            pieces.append(piece * not_last if right else piece)
        return jnp.concatenate(pieces, axis=0).astype(BF16)

    here, right, down, across = moved(0, 0), moved(0, 1), moved(1, 0), moved(1, 1)
    phases = {
        (0, 0): dot_back(here, weight[1, 1]),
        (0, 1): dot_back(here, weight[1, 2]) + dot_back(right, weight[1, 0]),
        (1, 0): dot_back(here, weight[2, 1]) + dot_back(down, weight[0, 1]),
        (1, 1): dot_back(here, weight[2, 2])
        + dot_back(right, weight[2, 0])
        + dot_back(down, weight[0, 2])
        + dot_back(across, weight[0, 0]),
    }
    for (a, e), value in phases.items():
        for b in range(batch):
            for i in range(half):
                place = b * small_pixels + i * half_width
                start = b * pixels + (2 * i + a) * width + e
                for block in range(full.shape[0]):
                    full[block, pl.ds(start, half_width, stride=2), :] = value[
                        place : place + half_width, block * LANES : (block + 1) * LANES
                    ]
    for block in range(full.shape[0]):
        out[:, block * LANES : (block + 1) * LANES] = full[block]
    back_pass(out, out_unit, out_slope, rows)
    spread_message(message, rows)


def block_back_kernel(
    gathered, counts, back, unit, mask, stats, params, weight, short_back, out_unit, out_slope,
    affine, grad, out, message, again, rows,
):
    join_sums(gathered, affine)
    grad_pass(back, unit, mask, affine, stats, params, total_count(counts, 4), grad)
    send(grad, affine)
    short = jnp.concatenate([short_back[block] for block in range(short_back.shape[0])], axis=1)
    out[...] = dot_back(grad[...], weight[...]) + short
    back_pass(out, out_unit, out_slope, rows)
    again[...] = out[...]
    send(again)
    spread_message(message, rows)


def middle_back_kernel(
    dims, gathered, counts, back, unit, mask, stats, params, weight, out_unit, out_slope,
    affine, grad, out, edge, message, rows,
):
    batch, height, width = dims
    pixels = height * width
    upper = is_upper()
    join_sums(gathered, affine)
    grad_pass(back, unit, mask, affine, stats, params, total_count(counts, 4), grad)
    send(grad, affine)
    out[...] = dot_back(grad[...], weight[...])
    back_pass(out, out_unit, out_slope, rows)
    spread_message(message, rows)
    for place, source in ((0, out), (batch, out_unit)):
        for b in range(batch):
            first = source[b * pixels : b * pixels + width, :]
            last = source[(b + 1) * pixels - width : (b + 1) * pixels, :]
            edge[(place + b) * width : (place + b + 1) * width, :] = last * upper + first * (1.0 - upper)


def entry_back_kernel(
    dims, gathered, counts, back, unit, halo, mask, above, below, stats, params, weight, out_unit, out_slope,
    affine, grad, out, message, rows, padded, triple,
):
    batch, height, width = dims
    pixels = height * width
    size = pixels + 2 * width
    join_sums(gathered, affine)
    count = total_count(counts, 4)
    channels = back.shape[1]
    everything = slice(0, channels)
    line = batch * width
    padded[0:8, :] = jnp.zeros((8, channels), F32)
    padded[8 + batch * size :, :] = jnp.zeros((8, channels), F32)
    up = raw_grad(halo[:line, :], halo[line:, :], above[...], affine, stats, params, count, everything)
    down = raw_grad(halo[:line, :], halo[line:, :], below[...], affine, stats, params, count, everything)
    for b in range(batch):
        here = slice(b * width, (b + 1) * width)
        top = 8 + b * size
        padded[top : top + width, :] = up[here]
        padded[top + size - width : top + size, :] = down[here]

    def keep(here, columns, value):
        b = here.start // pixels
        start = 8 + b * size + width + here.start - b * pixels
        padded[start : start + here.stop - here.start, columns] = value

    grad_pass(back, unit, mask, affine, stats, params, count, grad, keep=keep)
    send(grad, affine)
    fill_triple(padded, triple, batch, height + 2, width)
    total = None
    for row_tap in range(3):
        shift = (2 - row_tap) * width
        for col_tap in range(3):
            side = (2 - col_tap) * channels
            left = triple[:, shift : shift + pixels, side : side + channels].reshape(batch * pixels, channels)
            part = dot_back(left, weight[row_tap, col_tap])
            total = part if total is None else total + part
    out[...] = total
    back_pass(out, out_unit, out_slope, rows)
    spread_message(message, rows)


def images_kernel(gathered, counts, back, unit, mask, stats, params, weight, block_back, affine, grad, out):
    join_sums(gathered, affine)
    grad_pass(back, unit, mask, affine, stats, params, total_count(counts, 4), grad)
    send(grad, affine)
    step = 256
    for start in range(0, out.shape[1], step):
        columns = slice(start, start + step)
        value = dot_back(grad[...], weight[columns, :]) + block_back[:, columns]
        out[:, columns] = (value * wide(mask[...], step)).astype(BF16)


def dot_pixels(left, grad):
    return lax.dot_general(left, grad, (((0,), (0,)), ((), ())), preferred_element_type=F32)


def chip_grad(left, left_other, grad, grad_other, columns=slice(None)):
    half = left_other.shape[1]
    return dot_pixels(left[:, own_half(half)], grad[:, columns]) + dot_pixels(
        left_other[...], grad_other[:, columns]
    )


class View:
    def __init__(self, refs, group):
        self.ref = refs[group] if len(refs) > 1 else refs[0]
        self.lead = () if len(refs) > 1 else (group,)
        self.rows = self.ref.shape[-2]

    def __getitem__(self, here):
        return self.ref[self.lead + (here, slice(None))]

    def __setitem__(self, here, value):
        self.ref[self.lead + (here, slice(None))] = value


def half_rows(bit, flip, rows):
    mine = (lax.axis_index("img").astype(jnp.int32) >> bit) & 1
    return pl.ds(pl.multiple_of((1 - mine if flip else mine) * rows, 16), rows)


def deal(full, parts):
    rows, width = parts[0].shape
    for outs, flip in ((parts[2:], True), (parts[:2], False)):
        for group, (out, bit) in enumerate(zip(outs, steps()[0])):
            out[...] = full[half_rows(bit, flip, rows), group * width : (group + 1) * width]


def first_wave_kernel(
    short, short_other, strided, strided_other,
    short_grad, short_grad_other, expand_grad, expand_grad_other, full
):
    rows = short_other.shape[1]
    step = 512
    for start in range(0, full.shape[1], step):
        columns = slice(start, start + step)
        full[:rows, columns] = chip_grad(
            short, short_other, short_grad, short_grad_other, columns
        ).astype(BF16)
        full[rows:, columns] = chip_grad(
            strided, strided_other, expand_grad, expand_grad_other, columns
        ).astype(BF16)


def second_wave_kernel(
    taps, taps_other, strided_grad, strided_grad_other, *results
):
    *parts, full = results
    half = taps_other.shape[2] // 3
    channels = 2 * half
    for row_tap in range(3):
        for col_tap in range(3):
            start = pl.multiple_of(col_tap * channels + core_number() * half, LANES)
            own = dot_pixels(taps[row_tap, :, pl.ds(start, half)], strided_grad[...])
            other = dot_pixels(
                taps_other[row_tap, :, col_tap * half : (col_tap + 1) * half], strided_grad_other[...]
            )
            place_row = (3 * row_tap + col_tap) * half
            full[place_row : place_row + half, :] = (own + other).astype(BF16)
    deal(full, parts)


def fill_rest(full, row):
    if row < full.shape[0]:
        full[row:, :] = jnp.zeros((full.shape[0] - row, full.shape[1]), full.dtype)


def third_early_kernel(
    dims, block, block_other, widen_grad, widen_grad_other, act, act_other, closing_grad,
    closing_grad_other, triple, triple_other, middle_grad, middle_grad_other, full,
):
    batch, height, width = dims
    pixels = height * width
    step = full.shape[1]
    row = 0
    for left, left_other, grad, grad_other in (
        (block, block_other, widen_grad, widen_grad_other),
        (act, act_other, closing_grad, closing_grad_other),
    ):
        rows = left_other.shape[1]
        for start in range(0, grad.shape[1], step):
            full[row : row + rows, :] = chip_grad(
                left, left_other, grad, grad_other, slice(start, start + step)
            ).astype(BF16)
            row += rows
    half = triple_other.shape[2] // 3
    channels = 2 * half
    for row_tap in range(3):
        lines = slice(row_tap * width, row_tap * width + pixels)
        for col_tap in range(3):
            start = pl.multiple_of(col_tap * channels + core_number() * half, LANES)
            own = triple[:, lines, pl.ds(start, half)].reshape(batch * pixels, half)
            other = triple_other[:, lines, col_tap * half : (col_tap + 1) * half].reshape(batch * pixels, half)
            value = dot_pixels(own, middle_grad[...]) + dot_pixels(other, middle_grad_other[...])
            full[row : row + half, :] = value.astype(BF16)
            row += half


def third_wave_kernel(early, entry_in, entry_in_other, entry_grad, entry_grad_other, *results):
    *parts, full = results
    row, rows = early.shape[0], entry_in_other.shape[1]
    full[row : row + rows, :] = chip_grad(entry_in, entry_in_other, entry_grad, entry_grad_other).astype(BF16)
    fill_rest(full, row + rows)
    full[:row, :] = early[...]
    deal(full, parts)


def split_refs(refs, sizes):
    parts, start = [], 0
    for size in sizes:
        parts.append(refs[start : start + size])
        start += size
    return parts


def added(first, second):
    return (first.astype(F32) + second.astype(F32)).astype(BF16)


def halve_kernel(sizes, bits, *refs):
    kept, got, keep, pass_on = split_refs(refs, sizes)
    for outs, flip in ((pass_on, True), (keep, False)):
        for group, bit in enumerate(bits):
            out, first, second = View(outs, group), View(kept, group), View(got, group)
            here = half_rows(bit, flip, out.rows)
            out[:] = added(first[here], second[here])


def add_kernel(kept, got, out):
    out[...] = added(kept[...], got[...])


def double_kernel(sizes, bits, *refs):
    own, got, outs = split_refs(refs, sizes)
    for group, bit in enumerate(bits):
        out, first, second = View(outs, group), View(own, group), View(got, group)
        out[half_rows(bit, False, first.rows)] = first[:]
        out[half_rows(bit, True, first.rows)] = second[:]


def first_out(full, short, expand):
    rows = short.shape[0]
    short[...] = full[:rows, :].astype(F32)
    send(short)
    expand[...] = full[rows:, :].astype(F32)


def second_out(full, strided):
    rows = strided.shape[1]
    for tap in range(9):
        strided[tap] = full[tap * rows : (tap + 1) * rows, :].astype(F32)


def third_out(full, widen, closing, middle, entry):
    step = full.shape[1]
    row = 0
    for out in (widen, closing):
        rows = out.shape[0]
        for start in range(0, out.shape[1], step):
            out[:, start : start + step] = full[row : row + rows, :].astype(F32)
            row += rows
        send(out)
    rows = middle.shape[1]
    for tap in range(9):
        middle[tap] = full[row : row + rows, :].astype(F32)
        row += rows
    send(middle)
    entry[...] = full[row : row + entry.shape[0], :].astype(F32)


def out_kernel(finish, bits, own_a, own_b, got_a, got_b, *refs):
    outs, full = refs[:-1], refs[-1]
    rows, width = own_a.shape
    for group, (bit, own, got) in enumerate(zip(bits, (own_a, own_b), (got_a, got_b))):
        columns = slice(group * width, (group + 1) * width)
        full[half_rows(bit, False, rows), columns] = own[...]
        full[half_rows(bit, True, rows), columns] = got[...]
    finish(full, *outs)


def steps():
    bits = lax.axis_size("img").bit_length() - 1
    return [(0, 1), (1, 0)] + [(bit, bit) for bit in range(2, bits)]


def to_chip(value, bit):
    count = lax.axis_size("img")
    return lax.ppermute(value, "img", [(i, i ^ (1 << bit)) for i in range(count)])


def exchange(values, bits):
    return [to_chip(value, bit) for value, bit in zip(values, bits)]


def run_after(order, kernel, shapes, *operands, scratch=(), free=True):
    results = call(kernel, shapes, *operands, free=free, after=(order[0],), scratch=scratch)
    order[0] = results[0]
    return results


def group_shapes(bits, rows, width):
    return [((2, rows, width), BF16)] if bits[0] == bits[1] else [((rows, width), BF16)] * 2


def halve(order, kept, got, bits, rows, width):
    shapes = group_shapes(bits, rows, width)
    sizes = (len(kept), len(got), len(shapes), len(shapes))
    results = run_after(order, functools.partial(halve_kernel, sizes, bits), shapes * 2, *kept, *got)
    return results[: len(shapes)], results[len(shapes) :]


def sum_over_chips(order, kept, sent, number, shape, finish=None):
    todo = steps()
    rows, width = shape[0] >> (number + 1), shape[1] // 2
    halvings = number + 1
    for number in range(number, len(todo)):
        got = exchange(sent, todo[number])
        yield None
        following = todo[number + 1] if number + 1 < len(todo) else None
        if following is not None and number + 1 == halvings and (number == 0 or rows % 32 == 0):
            halvings += 1
            rows //= 2
            kept, sent = halve(order, kept, got, following, rows, width)
        else:
            kept = sent = run_after(order, add_kernel, [((2, rows, width), BF16)], kept[0], got[0])
    own = kept
    for number in reversed(range(1, halvings)):
        got = exchange(own, todo[number])
        yield None
        rows *= 2
        shapes = group_shapes(todo[number - 1], rows, width)
        sizes = (len(own), len(got), len(shapes))
        own = run_after(order, functools.partial(double_kernel, sizes, todo[number]), shapes, *own, *got)
    if finish is not None:
        got = exchange(own, todo[0])
        yield None
        kernel, outs = finish
        own = run_after(
            order,
            functools.partial(out_kernel, kernel, todo[0]),
            outs,
            *own,
            *got,
            scratch=[(shape, BF16)],
            free=False,
        )
    yield own


def per_device(
    images,
    extents,
    entry_weight,
    middle_weight,
    closing_weight,
    widen_weight,
    strided_weight,
    expand_weight,
    shortcut_weight,
    entry_affine,
    middle_affine,
    closing_affine,
    widen_affine,
    strided_affine,
    expand_affine,
    shortcut_affine,
    cotangent,
):
    batch, height, width, wide_in = images.shape
    dims = (batch, height, width)
    pixels = batch * height * width
    small_pixels = pixels // 4
    chips = lax.axis_size("img")
    devices = chips * lax.axis_size("row")
    row = lax.axis_index("row")
    local = extents - jnp.stack([row * height, 0]).astype(jnp.int32)
    mid, wider, last = entry_weight.shape[1], widen_weight.shape[1], expand_weight.shape[1]

    def message_rows(channels):
        return max(8, 2 * channels // LANES)

    def message(channels):
        return ((devices, message_rows(channels), LANES), F32)

    def rows(channels):
        return ((message_rows(channels), LANES), F32)

    def stat(channels):
        return ((8, channels), F32)

    def level(count, channels):
        return [((count, channels), BF16), ((count, channels), F32), ((count, channels), F32), stat(channels)]

    def ops(count, *sizes):
        total = 2 * count
        for size in sizes:
            total *= size
        return total

    entry_in, mask, small, above, below, small_below, entry_raw, edge, sent, give = call(
        functools.partial(entry_kernel, dims),
        [
            ((pixels, wide_in), BF16),
            ((pixels, LANES), F32),
            ((small_pixels, LANES), F32),
            ((batch * width, LANES), F32),
            ((batch * width, LANES), F32),
            ((batch * width // 2, LANES), F32),
            ((pixels, mid), F32),
            ((batch * width, mid), F32),
            message(mid),
            ((pixels, wide_in // 2), BF16),
        ],
        local,
        images.reshape(pixels, wide_in),
        entry_weight,
        scratch=[rows(mid)],
        smem=(0,),
        late=(1, 2,),
        keep=(6, 7, 8),
        flops=ops(pixels, wide_in, mid),
    )
    halo = swap_rows(edge)
    entry_in_other = swap_rows(give)
    counts = gather_all(sent)
    padded_rows = batch * (height + 2) * width
    entry_unit, entry_slope, entry_stats, middle_raw, sent, triple, give = call(
        functools.partial(middle_kernel, dims),
        level(pixels, mid)[1:]
        + [
            ((pixels, mid), F32),
            message(mid),
            ((batch, (height + 2) * width, 3 * mid), BF16),
            ((batch, (height + 2) * width, 3 * mid // 2), BF16),
        ],
        counts,
        entry_raw,
        halo,
        mask,
        above,
        below,
        entry_affine,
        middle_weight.reshape(3, 3 * mid, mid),
        scratch=[rows(mid), ((padded_rows + 16, mid), F32)],

        late=(7,),
        keep=(3, 4),
        flops=ops(pixels, 9, mid, mid),
    )
    triple_other = swap_rows(give)
    gathered = gather_all(sent)
    middle_act, middle_unit, middle_slope, middle_stats, closing_raw, sent, give = call(
        closing_kernel,
        level(pixels, mid) + [((pixels, wide_in), F32), message(wide_in), ((pixels, mid // 2), BF16)],
        gathered,
        counts,
        middle_raw,
        mask,
        middle_affine,
        closing_weight,
        scratch=[rows(wide_in)],

        late=(5,),
        keep=(4, 5),
        flops=ops(pixels, mid, wide_in),
    )
    middle_act_other = swap_rows(give)
    gathered = gather_all(sent)
    block_out, closing_unit, block_slope, closing_stats, shortcut_in, widen_raw, edge, sent, give, give_short = call(
        functools.partial(widen_kernel, dims),
        level(pixels, wide_in)
        + [
            ((small_pixels, wide_in), BF16),
            ((pixels, wider), F32),
            ((batch * width, wider), F32),
            message(wider),
            ((pixels, wide_in // 2), BF16),
            ((small_pixels, wide_in // 2), BF16),
        ],
        gathered,
        counts,
        closing_raw,
        entry_in,
        mask,
        closing_affine,
        widen_weight,
        scratch=[rows(wider), ((wide_in // LANES, pixels, LANES), F32)],

        late=(3, 6,),
        keep=(5, 6, 7),
        flops=ops(pixels, wide_in, wider),
    )
    halo = swap_rows(edge)
    block_other, short_other = swap_rows(give), swap_rows(give_short)
    gathered = gather_all(sent)
    shortcut_raw, shortcut_rows = call(
        shortcut_kernel,
        [((small_pixels, last), F32), rows(last)],
        shortcut_in,
        small,
        shortcut_weight,
        late=(0, 2),
        keep=(),
        flops=ops(small_pixels, wide_in, last),
    )
    widen_unit, widen_slope, widen_stats, strided_raw, sent, taps, give = call(
        functools.partial(strided_kernel, dims),
        level(pixels, wider)[1:]
        + [
            ((small_pixels, wider), F32),
            message(wider),
            ((3, small_pixels, 3 * wider), BF16),
            ((3, small_pixels, 3 * wider // 2), BF16),
        ],
        gathered,
        counts,
        widen_raw,
        halo,
        mask,
        small,
        above,
        widen_affine,
        strided_weight.reshape(3, 3 * wider, wider),
        scratch=[rows(wider), ((wider // LANES, batch * (height + 1) * width + 16, LANES), F32)],

        late=(8,),
        keep=(3, 4),
        flops=ops(small_pixels, 9, wider, wider),
    )
    taps_other = swap_rows(give)
    gathered = gather_all(sent)
    pair_rows = message_rows(last) + 8
    strided_act, strided_unit, strided_slope, strided_stats, expand_raw, mine, theirs, give = call(
        expand_kernel,
        level(small_pixels, wider)
        + [
            ((small_pixels, last), F32),
            ((pair_rows, LANES), F32),
            ((pair_rows, LANES), F32),
            ((small_pixels, wider // 2), BF16),
        ],
        gathered,
        counts,
        strided_raw,
        small,
        strided_affine,
        expand_weight,
        shortcut_rows,
        scratch=[rows(last)],

        late=(5, 6,),
        keep=(4, 5, 6),
        flops=ops(small_pixels, wider, last),
    )
    strided_act_other = swap_rows(give)
    (sent,) = call(pair_kernel, [((chips, pair_rows, LANES), F32)], mine, swap_rows(theirs), keep=(0,))
    (own_stats,) = call(join_kernel, [stat(last)], gather_img(sent), keep=(0,))
    half_rows = 3 * last // (2 * LANES)
    features, final_grad, expand_unit, shortcut_unit, expand_stats, shortcut_stats, mine, theirs = call(
        final_kernel,
        [
            ((small_pixels, last), BF16),
            ((small_pixels, last), F32),
            ((small_pixels, last), F32),
            ((small_pixels, last), F32),
            stat(last),
            stat(last),
            ((half_rows, LANES), F32),
            ((half_rows, LANES), F32),
        ],
        own_stats,
        swap_rows(own_stats),
        expand_raw,
        shortcut_raw,
        small,
        expand_affine,
        shortcut_affine,
        cotangent.reshape(small_pixels, last),
        late=(3, 7,),
        keep=(1, 2, 3, 4, 5, 6, 7),
        scratch=[((3 * last // LANES, LANES), F32)],

    )

    joined = mine + swap_rows(theirs)
    own_sums = jnp.sum(gather_img(jnp.broadcast_to(joined[None], (chips,) + joined.shape)), axis=0)
    affine_expand, affine_shortcut, expand_grad, shortcut_grad, strided_back, edge, sent = call(
        functools.partial(last_grads_kernel, batch),
        [
            ((2, last), F32),
            ((2, last), F32),
            ((small_pixels, last), BF16),
            ((small_pixels, last), BF16),
            ((small_pixels, wider), F32),
            ((batch * width, wider), F32),
            message(wider),
        ],
        own_sums,
        swap_rows(own_sums),
        counts,
        final_grad,
        expand_unit,
        shortcut_unit,
        expand_stats,
        shortcut_stats,
        expand_affine,
        shortcut_affine,
        small,
        expand_weight,
        strided_slope,
        strided_unit,
        scratch=[rows(wider)],

        late=(11, 12, 13,),
        keep=(4, 5, 6),
        flops=ops(small_pixels, wider, last),
    )
    halo = swap_rows(edge)
    gathered = gather_all(sent)

    def small_image(value):
        return value.reshape(batch, height // 2, width // 2, value.shape[-1])

    def image(value):
        return value.reshape(batch, height, width, value.shape[-1])

    order = [affine_expand]

    def wave_parts(kernel, shape, *operands, flops):
        parts = call(
            kernel,
            [((shape[0] // 2, shape[1] // 2), BF16)] * 4,
            *operands,
            scratch=[(shape, BF16)],
            flops=flops,
            late=None,
            free=True,
            after=(order[0],),
        )
        order[0] = parts[0]
        return parts

    first_shape = ((wide_in + wider) // 2, last)
    (first,) = call(
        first_wave_kernel,
        [(first_shape, BF16)],
        shortcut_in,
        short_other,
        strided_act,
        strided_act_other,
        shortcut_grad,
        swap_rows(shortcut_grad),
        expand_grad,
        swap_rows(expand_grad),

        flops=ops(2 * small_pixels, *first_shape),
        late=None,
        after=(order[0],),
    )
    order[0] = first
    first = lax.psum(first, "img")

    affine_strided, strided_grad, widen_back, sent = call(
        functools.partial(widen_back_kernel, dims),
        [((2, wider), F32), ((small_pixels, wider), BF16), ((pixels, wider), F32), message(wider)],
        gathered,
        counts,
        strided_back,
        strided_unit,
        halo,
        small,
        small_below,
        strided_stats,
        strided_affine,
        strided_weight,
        widen_unit,
        widen_slope,
        scratch=[
            rows(wider),
            ((batch * (height // 2 + 1) * width // 2 + 8, wider), F32),
            ((wider // LANES, pixels, LANES), F32),
        ],
        late=(3, 9, 10, 11),
        keep=(2, 3),
        after=(order[0],),
        flops=ops(small_pixels, 9, wider, wider),
    )
    gathered = gather_all(sent)
    order[0] = affine_strided
    strided_grad_other = swap_rows(strided_grad)
    (short_back,) = call(
        functools.partial(short_back_kernel, dims),
        [((wide_in // LANES, pixels, LANES), F32)],
        shortcut_grad,
        shortcut_weight,
        late=(0, 1),
        keep=(),
        after=(order[0],),
        flops=ops(small_pixels, wide_in, last),
    )
    order[0] = short_back
    affine_widen, widen_grad, block_back, sent, block_back_saved = call(
        block_back_kernel,
        [
            ((2, wider), F32),
            ((pixels, wider), BF16),
            ((pixels, wide_in), F32),
            message(wide_in),
            ((pixels, wide_in), F32),
        ],
        gathered,
        counts,
        widen_back,
        widen_unit,
        mask,
        widen_stats,
        widen_affine,
        widen_weight,
        short_back,
        closing_unit,
        block_slope,
        scratch=[rows(wide_in)],
        late=(3, 7, 8, 9, 10),
        keep=(2, 3),
        after=(order[0],),
        flops=ops(pixels, wide_in, wider),
    )
    gathered = gather_all(sent)

    order[0] = affine_widen
    widen_grad_other = swap_rows(widen_grad)
    second_shape = (9 * wider // 2, wider)
    second_parts = wave_parts(
        second_wave_kernel,
        second_shape,
        taps,
        taps_other,
        strided_grad,
        strided_grad_other,
        flops=ops(2 * small_pixels, *second_shape),
    )
    second_got = exchange(second_parts[2:], steps()[0])

    affine_closing, closing_grad, middle_back, edge, sent = call(
        functools.partial(middle_back_kernel, dims),
        [
            ((2, wide_in), F32),
            ((pixels, wide_in), BF16),
            ((pixels, mid), F32),
            ((2 * batch * width, mid), F32),
            message(mid),
        ],
        gathered,
        counts,
        block_back,
        closing_unit,
        mask,
        closing_stats,
        closing_affine,
        closing_weight,
        middle_unit,
        middle_slope,
        scratch=[rows(mid)],

        late=(3, 7, 8, 9,),
        keep=(2, 3, 4),
        after=(order[0],),
        flops=ops(pixels, wide_in, mid),
    )
    halo = swap_rows(edge)
    gathered = gather_all(sent)
    order[0] = affine_closing
    closing_grad_other = swap_rows(closing_grad)
    affine_middle, middle_grad, entry_back, sent = call(
        functools.partial(entry_back_kernel, dims),
        [((2, mid), F32), ((pixels, mid), BF16), ((pixels, mid), F32), message(mid)],
        gathered,
        counts,
        middle_back,
        middle_unit,
        halo,
        mask,
        above,
        below,
        middle_stats,
        middle_affine,
        middle_weight,
        entry_unit,
        entry_slope,
        scratch=[rows(mid), ((padded_rows + 16, mid), F32), ((batch, (height + 2) * width, 3 * mid), BF16)],
        late=(3, 10, 11, 12),
        keep=(2, 3),
        after=(order[0],),
        flops=ops(pixels, 9, mid, mid),
    )
    gathered = gather_all(sent)
    order[0] = affine_middle
    middle_grad_other = swap_rows(middle_grad)
    third_sizes = (wide_in // 2 * wider // mid, wide_in // 2, 9 * mid // 2, wide_in // 2)
    third_shape = (-(-sum(third_sizes) // 256) * 256, mid)
    (third_early,) = call(
        functools.partial(third_early_kernel, dims),
        [((sum(third_sizes[:3]), mid), BF16)],
        block_out,
        block_other,
        widen_grad,
        widen_grad_other,
        middle_act,
        middle_act_other,
        closing_grad,
        closing_grad_other,
        triple,
        triple_other,
        middle_grad,
        middle_grad_other,
        flops=ops(2 * pixels, *third_shape),
        late=None,
        after=(order[0],),
    )
    order[0] = third_early
    second_kept, second_sent = halve(
        order, second_parts[:2], second_got, steps()[1], second_shape[0] // 4, second_shape[1] // 2
    )
    affine_entry, entry_grad, image_grads = call(
        images_kernel,
        [((2, mid), F32), ((pixels, mid), BF16), ((pixels, wide_in), BF16)],
        gathered,
        counts,
        entry_back,
        entry_unit,
        mask,
        entry_stats,
        entry_affine,
        entry_weight,
        block_back_saved,
        late=(3, 7, 8),
        keep=(),
        after=(order[0],),
        flops=ops(pixels, mid, wide_in),
    )

    order[0] = affine_entry
    third_parts = wave_parts(
        third_wave_kernel,
        third_shape,
        third_early,
        entry_in,
        entry_in_other,
        entry_grad,
        swap_rows(entry_grad),
        flops=ops(2 * pixels, wide_in // 2, mid),
    )

    second_result = ((9, wider // 2, wider), F32)

    def most(second_parts, third_parts):
        order = [third_parts[0]]
        waves = {
            "b": sum_over_chips(
                order, second_parts[:2], second_parts[2:], 1, second_shape, (second_out, [second_result])
            ),
            "c": sum_over_chips(order, third_parts[:2], third_parts[2:], 0, third_shape),
        }
        sums = {}
        for name in "bc" + 16 * "bc":
            if name not in sums:
                result = next(waves[name])
                if result is not None:
                    sums[name] = list(result)
        return sums["b"], sums["c"]

    def none(second_parts, third_parts):
        del second_parts, third_parts
        half = (third_shape[0] // 2, third_shape[1] // 2)
        return [jnp.zeros(*second_result)], [jnp.zeros(half, BF16)] * 2

    (strided_total,), third_own = lax.cond(local[0, 1] > 0, most, none, [*second_kept, *second_sent], list(third_parts))
    third_got = exchange(third_own, steps()[0])
    shortcut_total, expand_total = call(
        first_out,
        [((wide_in // 2, last), F32), ((wider // 2, last), F32)],
        first,
        late=None,
        after=(third_own[0],),
    )
    order[0] = shortcut_total
    widen_total, closing_total, middle_total, entry_total = run_after(
        order,
        functools.partial(out_kernel, third_out, steps()[0]),
        [
            ((wide_in // 2, wider), F32),
            ((mid // 2, wide_in), F32),
            ((9, mid // 2, mid), F32),
            ((wide_in // 2, mid), F32),
        ],
        *third_own,
        *third_got,
        scratch=[(third_shape, BF16)],
        free=False,
    )
    middle_total = middle_total.reshape(3, 3, mid // 2, mid)
    strided_total = strided_total.reshape(3, 3, wider // 2, wider)
    return (
        small_image(features),
        image(image_grads),
        entry_total,
        middle_total,
        closing_total,
        widen_total,
        strided_total,
        expand_total,
        shortcut_total,
        affine_entry,
        affine_middle,
        affine_closing,
        affine_widen,
        affine_strided,
        affine_expand,
        affine_shortcut,
    )


def solution(mesh):
    image = P("img", "row", None, None)
    return jax.shard_map(
        per_device,
        mesh=mesh,
        in_specs=(image, P("img", None)) + (P(),) * 14 + (image,),
        out_specs=(
            image,
            image,
            P("row", None),
            P(None, None, "row", None),
            P("row", None),
            P("row", None),
            P(None, None, "row", None),
            P("row", None),
            P("row", None),
        )
        + (P(),) * 7,
        check_vma=False,
    )
```

```python
import functools
import math

import jax
import jax.numpy as jnp
from jax import lax
from jax.experimental import pallas as pl
from jax.experimental.pallas import tpu as pltpu
from jax.sharding import PartitionSpec as P

EPS = 1e-05
BOTH = ("img", "row")
F32 = jnp.float32
BF16 = jnp.bfloat16
LANES = 128
MIB = 1 << 20


def swap_rows(value):
    count = lax.axis_size("row")
    return lax.ppermute(value, "row", [(i, (i + 1) % count) for i in range(count)])


def gather_all(message):
    return lax.all_to_all(message, BOTH, 0, 0, tiled=True)


def gather_img(message):
    return lax.all_to_all(message, "img", 0, 0, tiled=True)


class Late:
    def __init__(self, source, buffer, semaphores):
        self.buffer = buffer
        self.shape, self.ndim, self.dtype = buffer.shape, len(buffer.shape), buffer.dtype
        parts = parts_of(self.shape)
        if parts == 1:
            self.copies = [pltpu.make_async_copy(source, buffer, semaphores.at[0])]
        else:
            self.copies = [
                pltpu.make_async_copy(source.at[i], buffer.at[i], semaphores.at[i]) for i in range(parts)
            ]
        for copy in self.copies:
            copy.start()
        self.waiting = set(range(parts))

    def ready(self, part=None):
        for i in sorted(self.waiting):
            if part is None or i == part:
                self.copies[i].wait()
                self.waiting.remove(i)
        return self.buffer

    def __getitem__(self, index):
        first = index[0] if isinstance(index, tuple) else index
        part = first if isinstance(first, int) and len(self.copies) > 1 else None
        return self.ready(part)[index]


def parts_of(shape):
    return shape[0] if len(shape) >= 3 and shape[0] == 3 else 1


class Saved:
    def __init__(self, target, buffer, semaphore):
        self.target, self.buffer, self.semaphore, self.copy = target, buffer, semaphore, None
        self.shape, self.ndim, self.dtype = buffer.shape, len(buffer.shape), buffer.dtype

    def send(self):
        if self.copy is None:
            self.copy = pltpu.make_async_copy(self.buffer, self.target, self.semaphore)
            self.copy.start()

    def __getitem__(self, index):
        return self.buffer[index]

    def __setitem__(self, index, value):
        self.buffer[index] = value


def send(*results):
    for result in results:
        if isinstance(result, Saved):
            result.send()


def call(kernel, outs, *operands, scratch=(), smem=(), late=(), flops=0, keep=(), limit=24, after=(), free=False):
    late = [place for place in (range(len(operands)) if late is None else late) if place not in smem]
    used = len(operands)
    operands += tuple(after)
    saved = [place for place in range(len(outs)) if place not in keep and not free]
    moved = sum(x.size * x.dtype.itemsize for x in operands) + sum(
        math.prod(shape) * jnp.dtype(dtype).itemsize for shape, dtype in outs
    )

    def place_of_operand(place):
        if place in smem:
            return pltpu.SMEM
        return pl.ANY if place in late or place >= used else pltpu.VMEM

    operands = [
        pltpu.with_memory_space_constraint(x, pltpu.HBM) if place in late or (place >= used and in_hbm(x)) else x
        for place, x in enumerate(operands)
    ]
    buffers = [pltpu.VMEM(operands[place].shape, operands[place].dtype) for place in late]
    buffers += [pltpu.VMEM(*outs[place]) for place in saved]
    semaphores = [pltpu.SemaphoreType.DMA((parts_of(operands[place].shape),)) for place in late]
    semaphores += [pltpu.SemaphoreType.DMA] * len(saved)

    def body(*refs):
        refs = list(refs)
        inputs, refs = refs[: len(operands)], refs[len(operands) :]
        results, refs = refs[: len(outs)], refs[len(outs) :]
        own, refs = refs[: len(scratch)], refs[len(scratch) :]
        space, marks = refs[: len(buffers)], refs[len(buffers) :]
        for number, place in enumerate(late):
            inputs[place] = Late(inputs[place], space[number], marks[number])
        for number, place in enumerate(saved):
            number += len(late)
            results[place] = Saved(results[place], space[number], marks[number])
        kernel(*inputs[:used], *results, *own)
        for place in late:
            inputs[place].ready()
        for place in saved:
            results[place].send()
        for place in saved:
            results[place].copy.wait()

    results = pl.pallas_call(
        body,
        out_shape=[
            jax.ShapeDtypeStruct(shape, dtype)
            if free
            else (pltpu.VMEM if place in keep else pltpu.HBM)(shape, dtype)
            for place, (shape, dtype) in enumerate(outs)
        ],
        in_specs=[pl.BlockSpec(memory_space=place_of_operand(place)) for place in range(len(operands))],
        out_specs=[
            pl.BlockSpec(memory_space=pl.ANY if place in saved else pltpu.VMEM) for place in range(len(outs))
        ],
        scratch_shapes=[pltpu.VMEM(shape, dtype) for shape, dtype in scratch] + buffers + semaphores,
        compiler_params=pltpu.CompilerParams(vmem_limit_bytes=limit * MIB),
        cost_estimate=pl.CostEstimate(flops=flops, bytes_accessed=moved, transcendentals=0),
    )(*operands)
    HELD.extend(results[place] for place in saved)
    return results


HELD = []


def in_hbm(value):
    return any(value is held for held in HELD)


def dot(left, right):
    return jnp.dot(left, right, preferred_element_type=F32)


def dot_back(grad, weight):
    return lax.dot_general(grad, weight, (((1,), (1,)), ((), ())), preferred_element_type=F32)


def wide(mask, width):
    return mask if width == LANES else jnp.concatenate([mask] * (width // LANES), axis=1)


def column_sum(value):
    return jnp.sum(value, axis=0, keepdims=True)


def spread_message(message, rows):
    tile = rows[...]
    for device in range(message.shape[0]):
        message[device] = tile


def put_row(rows, place, vector):
    for block in range(vector.shape[1] // LANES):
        rows[place + block : place + block + 1, :] = vector[:, block * LANES : (block + 1) * LANES]


def local_stats(raw, mask, rows, place=0):
    blocks = raw.shape[1] // LANES
    number = jnp.maximum(column_sum(mask[...]), 1.0)
    for block in range(blocks):
        columns = slice(block * LANES, (block + 1) * LANES)
        total = column_sum(raw[:, columns] * mask[...])
        centred = (raw[:, columns] - total / number) * mask[...]
        rows[place + block : place + block + 1, :] = total
        rows[place + blocks + block : place + blocks + block + 1, :] = column_sum(centred * centred)


def total_count(counts, place):
    return functools.reduce(
        jnp.add, [counts[i, place : place + 1, :] for i in range(counts.shape[0])]
    )


def join_stats(gathered, counts, place, stats, blocks):
    devices = gathered.shape[0]
    count = total_count(counts, place)
    mean = functools.reduce(jnp.add, [gathered[i, :blocks, :] for i in range(devices)]) / count
    spread = functools.reduce(jnp.add, [gathered[i, blocks : 2 * blocks, :] for i in range(devices)])
    for i in range(devices):
        number = counts[i, place : place + 1, :]
        shift = gathered[i, :blocks, :] / jnp.maximum(number, 1.0) - mean
        spread = spread + number * (shift * shift)
    scale = lax.rsqrt(spread / count + EPS)
    for block in range(blocks):
        columns = slice(block * LANES, (block + 1) * LANES)
        stats[0:1, columns] = mean[block : block + 1, :]
        stats[1:2, columns] = scale[block : block + 1, :]


def join_sums(gathered, affine):
    total = functools.reduce(jnp.add, [gathered[i] for i in range(gathered.shape[0])])
    blocks = affine.shape[1] // LANES
    for block in range(blocks):
        columns = slice(block * LANES, (block + 1) * LANES)
        affine[0:1, columns] = total[block : block + 1, :]
        affine[1:2, columns] = total[blocks + block : blocks + block + 1, :]


def chunks(rows, width, chunk=32, block=256):
    for start in range(0, width, block):
        for row in range(0, rows, chunk):
            yield slice(row, row + min(chunk, rows - row)), slice(start, start + min(block, width - start))


def silu_parts(value):
    gate = jax.nn.sigmoid(value)
    return value * gate, gate * (1.0 + value * (1.0 - gate))


def normed(raw, stats, params, columns):
    unit = (raw - stats[0:1, columns]) * stats[1:2, columns]
    return unit, unit * params[0:1, columns] + params[1:2, columns]


def act_pass(raw, mask, stats, params, unit, slope, act, skip=None, keep=None):
    rows, width = raw.shape
    for here, columns in chunks(rows, width):
        u, value = normed(raw[here, columns], stats, params, columns)
        if skip is not None:
            value = value + skip[here, columns].astype(F32)
        m = wide(mask[here, :], columns.stop - columns.start)
        out, rise = silu_parts(value)
        out = out * m
        unit[here, columns] = u
        slope[here, columns] = rise * m
        if act is not None:
            act[here, columns] = out.astype(BF16)
        if keep is not None:
            keep(here, columns, out)


def back_pass(back, unit, slope, rows):
    blocks = back.shape[1] // LANES
    for block in range(blocks):
        columns = slice(block * LANES, (block + 1) * LANES)
        value = back[:, columns] * slope[:, columns]
        back[:, columns] = value
        rows[block : block + 1, :] = column_sum(value * unit[:, columns])
        rows[blocks + block : blocks + block + 1, :] = column_sum(value)


def raw_grad(back, unit, mask, sums, stats, params, count, columns):
    width = columns.stop - columns.start
    n = wide(count, width)
    factor = params[0:1, columns] * stats[1:2, columns]
    centred = back - sums[1:2, columns] / n - unit * (sums[0:1, columns] / n)
    return factor * centred * wide(mask, width)


def grad_pass(back, unit, mask, sums, stats, params, count, grad, keep=None):
    for here, columns in chunks(*back.shape):
        value = raw_grad(
            back[here, columns], unit[here, columns], mask[here, :], sums, stats, params, count, columns
        )
        grad[here, columns] = value.astype(BF16)
        if keep is not None:
            keep(here, columns, value)


def valid(extents, image, first_row, columns, shape, step):
    place = lax.broadcasted_iota(jnp.int32, shape, 0)
    row = first_row + step * (place // columns)
    column = step * (place % columns)
    return jnp.where((row < extents[image, 0]) & (column < extents[image, 1]), 1.0, 0.0).astype(F32)


def core_number():
    return lax.axis_index("row").astype(jnp.int32)


def is_upper():
    return jnp.where(core_number() == 0, 1.0, 0.0).astype(F32)


def own_half(size):
    return pl.ds(pl.multiple_of(core_number() * size, LANES), size)


def other_half(size):
    return pl.ds(pl.multiple_of((1 - core_number()) * size, LANES), size)


def give_half(value, give):
    give[...] = value[:, other_half(give.shape[1])]
    send(give)


def entry_kernel(
    dims, extents, images, weight,
    entry_in, mask, small, above, below, small_below, raw, edge, message, give, rows,
):
    batch, height, width = dims
    pixels = height * width
    upper = is_upper()
    for b in range(batch):
        mask[b * pixels : (b + 1) * pixels, :] = valid(extents, b, 0, width, (pixels, LANES), 1)
        small[b * pixels // 4 : (b + 1) * pixels // 4, :] = valid(
            extents, b, 0, width // 2, (pixels // 4, LANES), 2
        )
        line = slice(b * width, (b + 1) * width)
        above[line, :] = valid(extents, b, -1, width, (width, LANES), 1) * (1.0 - upper)
        below[line, :] = valid(extents, b, height, width, (width, LANES), 1) * upper
        small_below[b * width // 2 : (b + 1) * width // 2, :] = (
            valid(extents, b, height, width // 2, (width // 2, LANES), 2) * upper
        )
    for here, columns in chunks(*images.shape):
        m = wide(mask[here, :], columns.stop - columns.start)
        entry_in[here, columns] = (images[here, columns].astype(F32) * m).astype(BF16)
    send(entry_in, mask, small, above, below, small_below)
    give_half(entry_in, give)
    raw[...] = dot(entry_in[...], weight[...])
    for b in range(batch):
        first = raw[b * pixels : b * pixels + width, :]
        last = raw[(b + 1) * pixels - width : (b + 1) * pixels, :]
        edge[b * width : (b + 1) * width, :] = last * upper + first * (1.0 - upper)
    rows[...] = jnp.zeros_like(rows)
    local_stats(raw, mask, rows)
    blocks = raw.shape[1] // LANES
    rows[2 * blocks : 2 * blocks + 1, :] = column_sum(mask[...])
    rows[2 * blocks + 1 : 2 * blocks + 2, :] = column_sum(small[...])
    spread_message(message, rows)


def put_blocks(target, here, columns, value):
    for start in range(columns.start, columns.stop, LANES):
        offset = start - columns.start
        target[start // LANES, here, :] = value[:, offset : offset + LANES]


def column_masks(rows, width):
    place = lax.broadcasted_iota(jnp.int32, (rows, LANES), 0) % width
    return (
        jnp.where(place == 0, 0.0, 1.0).astype(F32),
        jnp.where(place == width - 1, 0.0, 1.0).astype(F32),
    )


def fill_triple(padded, triple, batch, lines, width):
    size = lines * width
    channels = padded.shape[1]
    left_ok, right_ok = column_masks(size, width)
    for b in range(batch):
        start = 8 + b * size
        for c in range(0, channels, LANES):
            columns = slice(c, c + LANES)
            triple[b, :, c : c + LANES] = (padded[start - 1 : start - 1 + size, columns] * left_ok).astype(BF16)
            triple[b, :, channels + c : channels + c + LANES] = padded[start : start + size, columns].astype(BF16)
            triple[b, :, 2 * channels + c : 2 * channels + c + LANES] = (
                padded[start + 1 : start + 1 + size, columns] * right_ok
            ).astype(BF16)


def middle_kernel(
    dims, gathered, raw, halo, mask, above, below, params, weight,
    unit, slope, stats, out, message, triple, give, rows, padded,
):
    batch, height, width = dims
    pixels = height * width
    size = pixels + 2 * width
    blocks = raw.shape[1] // LANES
    join_stats(gathered, gathered, 2 * blocks, stats, blocks)
    everything = slice(0, raw.shape[1])
    _, value = normed(halo[...], stats, params, everything)
    rim, _ = silu_parts(value)
    padded[0:8, :] = jnp.zeros((8, raw.shape[1]), F32)
    padded[8 + batch * size :, :] = jnp.zeros((8, raw.shape[1]), F32)
    for b in range(batch):
        line = slice(b * width, (b + 1) * width)
        top = 8 + b * size
        padded[top : top + width, :] = rim[line] * wide(above[line, :], raw.shape[1])
        padded[top + size - width : top + size, :] = rim[line] * wide(below[line, :], raw.shape[1])

    def keep(here, columns, value):
        b = here.start // pixels
        start = 8 + b * size + width + here.start - b * pixels
        padded[start : start + here.stop - here.start, columns] = value

    act_pass(raw, mask, stats, params, unit, slope, None, keep=keep)
    send(unit, slope, stats)
    fill_triple(padded, triple, batch, height + 2, width)
    send(triple)
    give_taps(triple, give)
    total = None
    for tap in range(3):
        left = triple[:, tap * width : tap * width + pixels, :].reshape(batch * pixels, -1)
        part = dot(left, weight[tap])
        total = part if total is None else total + part
    out[...] = total
    local_stats(out, mask, rows)
    spread_message(message, rows)


def give_taps(taps, give):
    full, half = taps.shape[2] // 3, give.shape[2] // 3
    for tap in range(3):
        start = pl.multiple_of(tap * full + (1 - core_number()) * half, LANES)
        give[:, :, tap * half : (tap + 1) * half] = taps[:, :, pl.ds(start, half)]
    send(give)


def closing_kernel(
    gathered, counts, raw, mask, params, weight, act, unit, slope, stats, out, message, give, rows
):
    blocks = raw.shape[1] // LANES
    join_stats(gathered, counts, 4, stats, blocks)
    act_pass(raw, mask, stats, params, unit, slope, act)
    send(unit, slope, act, stats)
    give_half(act, give)
    out[...] = dot(act[...], weight[...])
    local_stats(out, mask, rows)
    spread_message(message, rows)


def widen_kernel(
    dims, gathered, counts, raw, entry_in, mask, params, weight,
    act, unit, slope, stats, short, out, edge, message, give, give_short, rows, even,
):
    batch, height, width = dims
    pixels = height * width
    blocks = raw.shape[1] // LANES
    join_stats(gathered, counts, 4, stats, blocks)

    def keep(here, columns, value):
        put_blocks(even, here, columns, value)

    act_pass(raw, mask, stats, params, unit, slope, act, skip=entry_in, keep=keep)
    send(unit, slope, act, stats)
    give_half(act, give)
    out[...] = dot(act[...], weight[...])
    for b in range(batch):
        edge[b * width : (b + 1) * width, :] = out[(b + 1) * pixels - width : (b + 1) * pixels, :]
    local_stats(out, mask, rows)
    spread_message(message, rows)
    for c in range(0, raw.shape[1], LANES):
        columns = slice(c, c + LANES)
        lines = []
        for b in range(batch):
            for i in range(height // 2):
                lines.append(even[c // LANES, pl.ds(b * pixels + 2 * i * width, width // 2, stride=2), :])
        short[:, columns] = jnp.concatenate(lines, axis=0).astype(BF16)
    send(short)
    give_half(short, give_short)


def shortcut_kernel(short, small, weight, out, rows):
    out[...] = dot(short[...], weight[...])
    send(out)
    local_stats(out, small, rows)


def strided_kernel(
    dims, gathered, counts, raw, halo, mask, small, above, params, weight,
    unit, slope, stats, out, message, taps, give, rows, padded,
):
    batch, height, width = dims
    pixels = height * width
    size = pixels + width
    half, half_width = height // 2, width // 2
    blocks = raw.shape[1] // LANES
    join_stats(gathered, counts, 4, stats, blocks)
    everything = slice(0, raw.shape[1])
    _, value = normed(halo[...], stats, params, everything)
    rim, _ = silu_parts(value)
    for block in range(padded.shape[0]):
        padded[block, 0:8, :] = jnp.zeros((8, LANES), F32)
    for b in range(batch):
        line = slice(b * width, (b + 1) * width)
        start = 8 + b * size
        put_blocks(padded, slice(start, start + width), everything, rim[line] * wide(above[line, :], raw.shape[1]))

    def keep(here, columns, value):
        b = here.start // pixels
        start = 8 + b * size + width + here.start - b * pixels
        put_blocks(padded, slice(start, start + here.stop - here.start), columns, value)

    act_pass(raw, mask, stats, params, unit, slope, None, keep=keep)
    send(unit, slope, stats)
    lines = height + 1
    not_first, _ = column_masks(lines * half_width, half_width)
    channels = raw.shape[1]
    for block in range(channels // LANES):
        for b in range(batch):
            start = 8 + b * size
            before = padded[block, pl.ds(start - 1, lines * half_width, stride=2), :] * not_first
            at = padded[block, pl.ds(start, lines * half_width, stride=2), :]
            after = padded[block, pl.ds(start + 1, lines * half_width, stride=2), :]
            for k, value in enumerate((before, at, after)):
                value = value.reshape(lines, half_width, LANES)
                place = k * channels + block * LANES
                for tap in range(3):
                    pieces = [value[tap + 2 * i] for i in range(half)]
                    taps[tap, b * half * half_width : (b + 1) * half * half_width, place : place + LANES] = (
                        jnp.concatenate(pieces, axis=0).astype(BF16)
                    )
    send(taps)
    give_taps(taps, give)
    total = None
    for tap in range(3):
        part = dot(taps[tap], weight[tap])
        total = part if total is None else total + part
    out[...] = total
    local_stats(out, small, rows)
    spread_message(message, rows)


def expand_kernel(
    gathered, counts, raw, small, params, weight, short_rows,
    act, unit, slope, stats, out, mine, theirs, give, rows,
):
    blocks = raw.shape[1] // LANES
    join_stats(gathered, counts, 5, stats, blocks)
    act_pass(raw, small, stats, params, unit, slope, act)
    send(unit, slope, act, stats)
    give_half(act, give)
    out[...] = dot(act[...], weight[...])
    local_stats(out, small, rows)
    upper = is_upper()
    size = rows.shape[0]
    number = jnp.broadcast_to(column_sum(small[...]), (8, LANES))
    mine[:size, :] = rows[...] * upper + short_rows[...] * (1.0 - upper)
    theirs[:size, :] = rows[...] * (1.0 - upper) + short_rows[...] * upper
    mine[size:, :] = number
    theirs[size:, :] = number


def pair_kernel(mine, other, message):
    size = mine.shape[0] - 8
    blocks = size // 2
    first, second = mine[size : size + 1, :], other[size : size + 1, :]
    both = first + second
    gap = mine[:blocks, :] / jnp.maximum(first, 1.0) - other[:blocks, :] / jnp.maximum(second, 1.0)
    weight = first * second / jnp.maximum(both, 1.0)
    total = mine[:blocks, :] + other[:blocks, :]
    square = mine[blocks:size, :] + other[blocks:size, :] + gap * gap * weight
    number = jnp.broadcast_to(both, (8, LANES))
    for i in range(message.shape[0]):
        message[i, :blocks, :] = total
        message[i, blocks:size, :] = square
        message[i, size:, :] = number


def join_kernel(gathered, stats):
    size = gathered.shape[1] - 8
    stats[...] = jnp.zeros_like(stats)
    join_stats(gathered, gathered, size, stats, size // 2)


def final_kernel(
    own, other, expand_raw, short_raw, small, expand_params, short_params, cotangent,
    features, grad, expand_unit, short_unit, expand_stats, short_stats, mine, theirs, rows,
):
    upper = is_upper()
    expand_stats[...] = own[...] * upper + other[...] * (1.0 - upper)
    short_stats[...] = own[...] * (1.0 - upper) + other[...] * upper
    height, width = expand_raw.shape
    blocks = width // LANES
    for block in range(blocks):
        columns = slice(block * LANES, (block + 1) * LANES)
        first, first_value = normed(expand_raw[:, columns], expand_stats, expand_params, columns)
        second, second_value = normed(short_raw[:, columns], short_stats, short_params, columns)
        out, rise = silu_parts(first_value + second_value)
        features[:, columns] = (out * small[...]).astype(BF16)
        value = cotangent[:, columns].astype(F32) * (rise * small[...])
        grad[:, columns] = value
        expand_unit[:, columns] = first
        short_unit[:, columns] = second
        rows[block : block + 1, :] = column_sum(value * first)
        rows[blocks + block : blocks + block + 1, :] = column_sum(value * second)
        rows[2 * blocks + block : 2 * blocks + block + 1, :] = column_sum(value)
    half = blocks // 2
    for stat in range(3):
        low = rows[stat * blocks : stat * blocks + half, :]
        high = rows[stat * blocks + half : (stat + 1) * blocks, :]
        mine[stat * half : (stat + 1) * half, :] = low * upper + high * (1.0 - upper)
        theirs[stat * half : (stat + 1) * half, :] = low * (1.0 - upper) + high * upper


def last_grads_kernel(
    batch, own, other, counts, grad, expand_unit, short_unit, expand_stats, short_stats,
    expand_params, short_params, small, weight, slope, unit,
    expand_affine, short_affine, expand_grad, short_grad, back, edge, message, rows,
):
    upper = is_upper()
    half = own.shape[0] // 3
    for stat in range(3):
        part = slice(stat * half, (stat + 1) * half)
        low = own[part, :] * upper + other[part, :] * (1.0 - upper)
        high = own[part, :] * (1.0 - upper) + other[part, :] * upper
        for block in range(2 * half):
            value = low[block : block + 1, :] if block < half else high[block - half : block - half + 1, :]
            columns = slice(block * LANES, (block + 1) * LANES)
            if stat == 0:
                expand_affine[0:1, columns] = value
            elif stat == 1:
                short_affine[0:1, columns] = value
            else:
                expand_affine[1:2, columns] = value
                short_affine[1:2, columns] = value
    count = total_count(counts, 5)
    for here, columns in chunks(*grad.shape):
        expand_grad[here, columns] = raw_grad(
            grad[here, columns], expand_unit[here, columns], small[here, :], expand_affine, expand_stats,
            expand_params, count, columns,
        ).astype(BF16)
        short_grad[here, columns] = raw_grad(
            grad[here, columns], short_unit[here, columns], small[here, :], short_affine, short_stats,
            short_params, count, columns,
        ).astype(BF16)
    send(expand_grad, short_grad, expand_affine, short_affine)
    back[...] = dot_back(expand_grad[...], weight[...])
    back_pass(back, unit, slope, rows)
    spread_message(message, rows)
    pixels = back.shape[0] // batch
    line = edge.shape[0] // (2 * batch)
    for b in range(batch):
        edge[b * line : (b + 1) * line, :] = back[b * pixels : b * pixels + line, :]
        edge[(batch + b) * line : (batch + b + 1) * line, :] = unit[b * pixels : b * pixels + line, :]


def short_back_kernel(dims, grad, weight, out):
    batch, height, width = dims
    pixels = height * width
    small = dot_back(grad[...], weight[...])
    out[...] = jnp.zeros(out.shape, out.dtype)
    half = width // 2
    for block in range(out.shape[0]):
        columns = slice(block * LANES, (block + 1) * LANES)
        for b in range(batch):
            for i in range(height // 2):
                place = b * pixels // 4 + i * half
                start = b * pixels + 2 * i * width
                out[block, pl.ds(start, half, stride=2), :] = small[place : place + half, columns]


def widen_back_kernel(
    dims, gathered, counts, back, unit, halo, small, small_below, stats, params, weight, out_unit, out_slope,
    affine, grad, out, message, rows, padded, full,
):
    batch, height, width = dims
    pixels = height * width
    half, half_width = height // 2, width // 2
    size = (half + 1) * half_width
    join_sums(gathered, affine)
    count = total_count(counts, 5)
    channels = back.shape[1]
    everything = slice(0, channels)
    line = batch * half_width
    rim = raw_grad(
        halo[:line, :], halo[line:, :], small_below[...], affine, stats, params, count, everything
    ).astype(BF16).astype(F32)
    for b in range(batch):
        stop = (b + 1) * size
        padded[stop - half_width : stop, :] = rim[b * half_width : (b + 1) * half_width]
    padded[batch * size :, :] = jnp.zeros((8, channels), F32)
    small_pixels = half * half_width
    for here, columns in chunks(back.shape[0], channels, chunk=small_pixels):
        value = raw_grad(
            back[here, columns], unit[here, columns], small[here, :], affine, stats, params, count, columns
        ).astype(BF16)
        grad[here, columns] = value
        b = here.start // small_pixels
        padded[b * size : b * size + small_pixels, columns] = value.astype(F32)
    send(grad, affine)
    _, not_last = column_masks(small_pixels, half_width)
    not_last = wide(not_last, channels)

    def moved(down, right):
        pieces = []
        for b in range(batch):
            start = b * size + down * half_width + right
            piece = padded[start : start + small_pixels, :]
            pieces.append(piece * not_last if right else piece)
        return jnp.concatenate(pieces, axis=0).astype(BF16)

    here, right, down, across = moved(0, 0), moved(0, 1), moved(1, 0), moved(1, 1)
    phases = {
        (0, 0): dot_back(here, weight[1, 1]),
        (0, 1): dot_back(here, weight[1, 2]) + dot_back(right, weight[1, 0]),
        (1, 0): dot_back(here, weight[2, 1]) + dot_back(down, weight[0, 1]),
        (1, 1): dot_back(here, weight[2, 2])
        + dot_back(right, weight[2, 0])
        + dot_back(down, weight[0, 2])
        + dot_back(across, weight[0, 0]),
    }
    for (a, e), value in phases.items():
        for b in range(batch):
            for i in range(half):
                place = b * small_pixels + i * half_width
                start = b * pixels + (2 * i + a) * width + e
                for block in range(full.shape[0]):
                    full[block, pl.ds(start, half_width, stride=2), :] = value[
                        place : place + half_width, block * LANES : (block + 1) * LANES
                    ]
    for block in range(full.shape[0]):
        out[:, block * LANES : (block + 1) * LANES] = full[block]
    back_pass(out, out_unit, out_slope, rows)
    spread_message(message, rows)


def block_back_kernel(
    gathered, counts, back, unit, mask, stats, params, weight, short_back, out_unit, out_slope,
    affine, grad, out, message, again, rows,
):
    join_sums(gathered, affine)
    grad_pass(back, unit, mask, affine, stats, params, total_count(counts, 4), grad)
    send(grad, affine)
    short = jnp.concatenate([short_back[block] for block in range(short_back.shape[0])], axis=1)
    out[...] = dot_back(grad[...], weight[...]) + short
    back_pass(out, out_unit, out_slope, rows)
    again[...] = out[...]
    send(again)
    spread_message(message, rows)


def middle_back_kernel(
    dims, gathered, counts, back, unit, mask, stats, params, weight, out_unit, out_slope,
    affine, grad, out, edge, message, rows,
):
    batch, height, width = dims
    pixels = height * width
    upper = is_upper()
    join_sums(gathered, affine)
    grad_pass(back, unit, mask, affine, stats, params, total_count(counts, 4), grad)
    send(grad, affine)
    out[...] = dot_back(grad[...], weight[...])
    back_pass(out, out_unit, out_slope, rows)
    spread_message(message, rows)
    for place, source in ((0, out), (batch, out_unit)):
        for b in range(batch):
            first = source[b * pixels : b * pixels + width, :]
            last = source[(b + 1) * pixels - width : (b + 1) * pixels, :]
            edge[(place + b) * width : (place + b + 1) * width, :] = last * upper + first * (1.0 - upper)


def entry_back_kernel(
    dims, gathered, counts, back, unit, halo, mask, above, below, stats, params, weight, out_unit, out_slope,
    affine, grad, out, message, rows, padded, triple,
):
    batch, height, width = dims
    pixels = height * width
    size = pixels + 2 * width
    join_sums(gathered, affine)
    count = total_count(counts, 4)
    channels = back.shape[1]
    everything = slice(0, channels)
    line = batch * width
    padded[0:8, :] = jnp.zeros((8, channels), F32)
    padded[8 + batch * size :, :] = jnp.zeros((8, channels), F32)
    up = raw_grad(halo[:line, :], halo[line:, :], above[...], affine, stats, params, count, everything)
    down = raw_grad(halo[:line, :], halo[line:, :], below[...], affine, stats, params, count, everything)
    for b in range(batch):
        here = slice(b * width, (b + 1) * width)
        top = 8 + b * size
        padded[top : top + width, :] = up[here]
        padded[top + size - width : top + size, :] = down[here]

    def keep(here, columns, value):
        b = here.start // pixels
        start = 8 + b * size + width + here.start - b * pixels
        padded[start : start + here.stop - here.start, columns] = value

    grad_pass(back, unit, mask, affine, stats, params, count, grad, keep=keep)
    send(grad, affine)
    fill_triple(padded, triple, batch, height + 2, width)
    total = None
    for row_tap in range(3):
        shift = (2 - row_tap) * width
        for col_tap in range(3):
            side = (2 - col_tap) * channels
            left = triple[:, shift : shift + pixels, side : side + channels].reshape(batch * pixels, channels)
            part = dot_back(left, weight[row_tap, col_tap])
            total = part if total is None else total + part
    out[...] = total
    back_pass(out, out_unit, out_slope, rows)
    spread_message(message, rows)


def images_kernel(gathered, counts, back, unit, mask, stats, params, weight, block_back, affine, grad, out):
    join_sums(gathered, affine)
    grad_pass(back, unit, mask, affine, stats, params, total_count(counts, 4), grad)
    send(grad, affine)
    step = 256
    for start in range(0, out.shape[1], step):
        columns = slice(start, start + step)
        value = dot_back(grad[...], weight[columns, :]) + block_back[:, columns]
        out[:, columns] = (value * wide(mask[...], step)).astype(BF16)


def dot_pixels(left, grad):
    return lax.dot_general(left, grad, (((0,), (0,)), ((), ())), preferred_element_type=F32)


def chip_grad(left, left_other, grad, grad_other, columns=slice(None)):
    half = left_other.shape[1]
    return dot_pixels(left[:, own_half(half)], grad[:, columns]) + dot_pixels(
        left_other[...], grad_other[:, columns]
    )


class View:
    def __init__(self, refs, group):
        self.ref = refs[group] if len(refs) > 1 else refs[0]
        self.lead = () if len(refs) > 1 else (group,)
        self.rows = self.ref.shape[-2]

    def __getitem__(self, here):
        return self.ref[self.lead + (here, slice(None))]

    def __setitem__(self, here, value):
        self.ref[self.lead + (here, slice(None))] = value


def half_rows(bit, flip, rows):
    mine = (lax.axis_index("img").astype(jnp.int32) >> bit) & 1
    return pl.ds(pl.multiple_of((1 - mine if flip else mine) * rows, 16), rows)


def deal(full, parts):
    rows, width = parts[0].shape
    for outs, flip in ((parts[2:], True), (parts[:2], False)):
        for group, (out, bit) in enumerate(zip(outs, steps()[0])):
            out[...] = full[half_rows(bit, flip, rows), group * width : (group + 1) * width]


def first_wave_kernel(
    short, short_other, strided, strided_other,
    short_grad, short_grad_other, expand_grad, expand_grad_other, full
):
    rows = short_other.shape[1]
    step = 512
    for start in range(0, full.shape[1], step):
        columns = slice(start, start + step)
        full[:rows, columns] = chip_grad(
            short, short_other, short_grad, short_grad_other, columns
        ).astype(BF16)
        full[rows:, columns] = chip_grad(
            strided, strided_other, expand_grad, expand_grad_other, columns
        ).astype(BF16)


def second_wave_kernel(
    taps, taps_other, strided_grad, strided_grad_other, *results
):
    *parts, full = results
    half = taps_other.shape[2] // 3
    channels = 2 * half
    for row_tap in range(3):
        for col_tap in range(3):
            start = pl.multiple_of(col_tap * channels + core_number() * half, LANES)
            own = dot_pixels(taps[row_tap, :, pl.ds(start, half)], strided_grad[...])
            other = dot_pixels(
                taps_other[row_tap, :, col_tap * half : (col_tap + 1) * half], strided_grad_other[...]
            )
            place_row = (3 * row_tap + col_tap) * half
            full[place_row : place_row + half, :] = (own + other).astype(BF16)
    deal(full, parts)


def fill_rest(full, row):
    if row < full.shape[0]:
        full[row:, :] = jnp.zeros((full.shape[0] - row, full.shape[1]), full.dtype)


def third_early_kernel(
    dims, block, block_other, widen_grad, widen_grad_other, act, act_other, closing_grad,
    closing_grad_other, triple, triple_other, middle_grad, middle_grad_other, full,
):
    batch, height, width = dims
    pixels = height * width
    step = full.shape[1]
    row = 0
    for left, left_other, grad, grad_other in (
        (block, block_other, widen_grad, widen_grad_other),
        (act, act_other, closing_grad, closing_grad_other),
    ):
        rows = left_other.shape[1]
        for start in range(0, grad.shape[1], step):
            full[row : row + rows, :] = chip_grad(
                left, left_other, grad, grad_other, slice(start, start + step)
            ).astype(BF16)
            row += rows
    half = triple_other.shape[2] // 3
    channels = 2 * half
    for row_tap in range(3):
        lines = slice(row_tap * width, row_tap * width + pixels)
        for col_tap in range(3):
            start = pl.multiple_of(col_tap * channels + core_number() * half, LANES)
            own = triple[:, lines, pl.ds(start, half)].reshape(batch * pixels, half)
            other = triple_other[:, lines, col_tap * half : (col_tap + 1) * half].reshape(batch * pixels, half)
            value = dot_pixels(own, middle_grad[...]) + dot_pixels(other, middle_grad_other[...])
            full[row : row + half, :] = value.astype(BF16)
            row += half


def third_wave_kernel(early, entry_in, entry_in_other, entry_grad, entry_grad_other, *results):
    *parts, full = results
    row, rows = early.shape[0], entry_in_other.shape[1]
    full[row : row + rows, :] = chip_grad(entry_in, entry_in_other, entry_grad, entry_grad_other).astype(BF16)
    fill_rest(full, row + rows)
    full[:row, :] = early[...]
    deal(full, parts)


def split_refs(refs, sizes):
    parts, start = [], 0
    for size in sizes:
        parts.append(refs[start : start + size])
        start += size
    return parts


def added(first, second):
    return (first.astype(F32) + second.astype(F32)).astype(BF16)


def halve_kernel(sizes, bits, *refs):
    kept, got, keep, pass_on = split_refs(refs, sizes)
    for outs, flip in ((pass_on, True), (keep, False)):
        for group, bit in enumerate(bits):
            out, first, second = View(outs, group), View(kept, group), View(got, group)
            here = half_rows(bit, flip, out.rows)
            out[:] = added(first[here], second[here])


def add_kernel(kept, got, out):
    out[...] = added(kept[...], got[...])


def double_kernel(sizes, bits, *refs):
    own, got, outs = split_refs(refs, sizes)
    for group, bit in enumerate(bits):
        out, first, second = View(outs, group), View(own, group), View(got, group)
        out[half_rows(bit, False, first.rows)] = first[:]
        out[half_rows(bit, True, first.rows)] = second[:]


def first_out(full, short, expand):
    rows = short.shape[0]
    short[...] = full[:rows, :].astype(F32)
    send(short)
    expand[...] = full[rows:, :].astype(F32)


def second_out(full, strided):
    rows = strided.shape[1]
    for tap in range(9):
        strided[tap] = full[tap * rows : (tap + 1) * rows, :].astype(F32)


def third_out(full, widen, closing, middle, entry):
    step = full.shape[1]
    row = 0
    for out in (widen, closing):
        rows = out.shape[0]
        for start in range(0, out.shape[1], step):
            out[:, start : start + step] = full[row : row + rows, :].astype(F32)
            row += rows
        send(out)
    rows = middle.shape[1]
    for tap in range(9):
        middle[tap] = full[row : row + rows, :].astype(F32)
        row += rows
    send(middle)
    entry[...] = full[row : row + entry.shape[0], :].astype(F32)


def out_kernel(finish, bits, own_a, own_b, got_a, got_b, *refs):
    outs, full = refs[:-1], refs[-1]
    rows, width = own_a.shape
    for group, (bit, own, got) in enumerate(zip(bits, (own_a, own_b), (got_a, got_b))):
        columns = slice(group * width, (group + 1) * width)
        full[half_rows(bit, False, rows), columns] = own[...]
        full[half_rows(bit, True, rows), columns] = got[...]
    finish(full, *outs)


def steps():
    bits = lax.axis_size("img").bit_length() - 1
    return [(0, 1), (1, 0)] + [(bit, bit) for bit in range(2, bits)]


def to_chip(value, bit):
    count = lax.axis_size("img")
    return lax.ppermute(value, "img", [(i, i ^ (1 << bit)) for i in range(count)])


def exchange(values, bits):
    return [to_chip(value, bit) for value, bit in zip(values, bits)]


def run_after(order, kernel, shapes, *operands, scratch=(), free=True):
    results = call(kernel, shapes, *operands, free=free, after=(order[0],), scratch=scratch)
    order[0] = results[0]
    return results


def group_shapes(bits, rows, width):
    return [((2, rows, width), BF16)] if bits[0] == bits[1] else [((rows, width), BF16)] * 2


def halve(order, kept, got, bits, rows, width):
    shapes = group_shapes(bits, rows, width)
    sizes = (len(kept), len(got), len(shapes), len(shapes))
    results = run_after(order, functools.partial(halve_kernel, sizes, bits), shapes * 2, *kept, *got)
    return results[: len(shapes)], results[len(shapes) :]


def sum_over_chips(order, kept, sent, number, shape, finish=None):
    todo = steps()
    rows, width = shape[0] >> (number + 1), shape[1] // 2
    halvings = number + 1
    for number in range(number, len(todo)):
        got = exchange(sent, todo[number])
        yield None
        following = todo[number + 1] if number + 1 < len(todo) else None
        if following is not None and number + 1 == halvings and (number == 0 or rows % 32 == 0):
            halvings += 1
            rows //= 2
            kept, sent = halve(order, kept, got, following, rows, width)
        else:
            kept = sent = run_after(order, add_kernel, [((2, rows, width), BF16)], kept[0], got[0])
    own = kept
    for number in reversed(range(1, halvings)):
        got = exchange(own, todo[number])
        yield None
        rows *= 2
        shapes = group_shapes(todo[number - 1], rows, width)
        sizes = (len(own), len(got), len(shapes))
        own = run_after(order, functools.partial(double_kernel, sizes, todo[number]), shapes, *own, *got)
    if finish is not None:
        got = exchange(own, todo[0])
        yield None
        kernel, outs = finish
        own = run_after(
            order,
            functools.partial(out_kernel, kernel, todo[0]),
            outs,
            *own,
            *got,
            scratch=[(shape, BF16)],
            free=False,
        )
    yield own


def per_device(
    images,
    extents,
    entry_weight,
    middle_weight,
    closing_weight,
    widen_weight,
    strided_weight,
    expand_weight,
    shortcut_weight,
    entry_affine,
    middle_affine,
    closing_affine,
    widen_affine,
    strided_affine,
    expand_affine,
    shortcut_affine,
    cotangent,
):
    batch, height, width, wide_in = images.shape
    dims = (batch, height, width)
    pixels = batch * height * width
    small_pixels = pixels // 4
    chips = lax.axis_size("img")
    devices = chips * lax.axis_size("row")
    row = lax.axis_index("row")
    local = extents - jnp.stack([row * height, 0]).astype(jnp.int32)
    mid, wider, last = entry_weight.shape[1], widen_weight.shape[1], expand_weight.shape[1]

    def message_rows(channels):
        return max(8, 2 * channels // LANES)

    def message(channels):
        return ((devices, message_rows(channels), LANES), F32)

    def rows(channels):
        return ((message_rows(channels), LANES), F32)

    def stat(channels):
        return ((8, channels), F32)

    def level(count, channels):
        return [((count, channels), BF16), ((count, channels), F32), ((count, channels), F32), stat(channels)]

    def ops(count, *sizes):
        total = 2 * count
        for size in sizes:
            total *= size
        return total

    entry_in, mask, small, above, below, small_below, entry_raw, edge, sent, give = call(
        functools.partial(entry_kernel, dims),
        [
            ((pixels, wide_in), BF16),
            ((pixels, LANES), F32),
            ((small_pixels, LANES), F32),
            ((batch * width, LANES), F32),
            ((batch * width, LANES), F32),
            ((batch * width // 2, LANES), F32),
            ((pixels, mid), F32),
            ((batch * width, mid), F32),
            message(mid),
            ((pixels, wide_in // 2), BF16),
        ],
        local,
        images.reshape(pixels, wide_in),
        entry_weight,
        scratch=[rows(mid)],
        smem=(0,),
        late=(1, 2,),
        keep=(6, 7, 8),
        flops=ops(pixels, wide_in, mid),
    )
    halo = swap_rows(edge)
    entry_in_other = swap_rows(give)
    counts = gather_all(sent)
    padded_rows = batch * (height + 2) * width
    entry_unit, entry_slope, entry_stats, middle_raw, sent, triple, give = call(
        functools.partial(middle_kernel, dims),
        level(pixels, mid)[1:]
        + [
            ((pixels, mid), F32),
            message(mid),
            ((batch, (height + 2) * width, 3 * mid), BF16),
            ((batch, (height + 2) * width, 3 * mid // 2), BF16),
        ],
        counts,
        entry_raw,
        halo,
        mask,
        above,
        below,
        entry_affine,
        middle_weight.reshape(3, 3 * mid, mid),
        scratch=[rows(mid), ((padded_rows + 16, mid), F32)],

        late=(3, 4, 5, 6, 7),
        keep=(3, 4),
        flops=ops(pixels, 9, mid, mid),
    )
    triple_other = swap_rows(give)
    gathered = gather_all(sent)
    middle_act, middle_unit, middle_slope, middle_stats, closing_raw, sent, give = call(
        closing_kernel,
        level(pixels, mid) + [((pixels, wide_in), F32), message(wide_in), ((pixels, mid // 2), BF16)],
        gathered,
        counts,
        middle_raw,
        mask,
        middle_affine,
        closing_weight,
        scratch=[rows(wide_in)],

        late=(5,),
        keep=(4, 5),
        flops=ops(pixels, mid, wide_in),
    )
    middle_act_other = swap_rows(give)
    gathered = gather_all(sent)
    block_out, closing_unit, block_slope, closing_stats, shortcut_in, widen_raw, edge, sent, give, give_short = call(
        functools.partial(widen_kernel, dims),
        level(pixels, wide_in)
        + [
            ((small_pixels, wide_in), BF16),
            ((pixels, wider), F32),
            ((batch * width, wider), F32),
            message(wider),
            ((pixels, wide_in // 2), BF16),
            ((small_pixels, wide_in // 2), BF16),
        ],
        gathered,
        counts,
        closing_raw,
        entry_in,
        mask,
        closing_affine,
        widen_weight,
        scratch=[rows(wider), ((wide_in // LANES, pixels, LANES), F32)],

        late=(3, 6,),
        keep=(5, 6, 7),
        flops=ops(pixels, wide_in, wider),
    )
    halo = swap_rows(edge)
    block_other, short_other = swap_rows(give), swap_rows(give_short)
    gathered = gather_all(sent)
    shortcut_raw, shortcut_rows = call(
        shortcut_kernel,
        [((small_pixels, last), F32), rows(last)],
        shortcut_in,
        small,
        shortcut_weight,
        late=(0, 2),
        keep=(),
        flops=ops(small_pixels, wide_in, last),
    )
    widen_unit, widen_slope, widen_stats, strided_raw, sent, taps, give = call(
        functools.partial(strided_kernel, dims),
        level(pixels, wider)[1:]
        + [
            ((small_pixels, wider), F32),
            message(wider),
            ((3, small_pixels, 3 * wider), BF16),
            ((3, small_pixels, 3 * wider // 2), BF16),
        ],
        gathered,
        counts,
        widen_raw,
        halo,
        mask,
        small,
        above,
        widen_affine,
        strided_weight.reshape(3, 3 * wider, wider),
        scratch=[rows(wider), ((wider // LANES, batch * (height + 1) * width + 16, LANES), F32)],

        late=(8,),
        keep=(3, 4),
        flops=ops(small_pixels, 9, wider, wider),
    )
    taps_other = swap_rows(give)
    gathered = gather_all(sent)
    pair_rows = message_rows(last) + 8
    strided_act, strided_unit, strided_slope, strided_stats, expand_raw, mine, theirs, give = call(
        expand_kernel,
        level(small_pixels, wider)
        + [
            ((small_pixels, last), F32),
            ((pair_rows, LANES), F32),
            ((pair_rows, LANES), F32),
            ((small_pixels, wider // 2), BF16),
        ],
        gathered,
        counts,
        strided_raw,
        small,
        strided_affine,
        expand_weight,
        shortcut_rows,
        scratch=[rows(last)],

        late=(5, 6,),
        keep=(4, 5, 6),
        flops=ops(small_pixels, wider, last),
    )
    strided_act_other = swap_rows(give)
    (sent,) = call(pair_kernel, [((chips, pair_rows, LANES), F32)], mine, swap_rows(theirs), keep=(0,))
    (own_stats,) = call(join_kernel, [stat(last)], gather_img(sent), keep=(0,))
    half_rows = 3 * last // (2 * LANES)
    features, final_grad, expand_unit, shortcut_unit, expand_stats, shortcut_stats, mine, theirs = call(
        final_kernel,
        [
            ((small_pixels, last), BF16),
            ((small_pixels, last), F32),
            ((small_pixels, last), F32),
            ((small_pixels, last), F32),
            stat(last),
            stat(last),
            ((half_rows, LANES), F32),
            ((half_rows, LANES), F32),
        ],
        own_stats,
        swap_rows(own_stats),
        expand_raw,
        shortcut_raw,
        small,
        expand_affine,
        shortcut_affine,
        cotangent.reshape(small_pixels, last),
        late=(3, 7,),
        keep=(1, 2, 3, 4, 5, 6, 7),
        scratch=[((3 * last // LANES, LANES), F32)],

    )

    joined = mine + swap_rows(theirs)
    own_sums = jnp.sum(gather_img(jnp.broadcast_to(joined[None], (chips,) + joined.shape)), axis=0)
    affine_expand, affine_shortcut, expand_grad, shortcut_grad, strided_back, edge, sent = call(
        functools.partial(last_grads_kernel, batch),
        [
            ((2, last), F32),
            ((2, last), F32),
            ((small_pixels, last), BF16),
            ((small_pixels, last), BF16),
            ((small_pixels, wider), F32),
            ((batch * width, wider), F32),
            message(wider),
        ],
        own_sums,
        swap_rows(own_sums),
        counts,
        final_grad,
        expand_unit,
        shortcut_unit,
        expand_stats,
        shortcut_stats,
        expand_affine,
        shortcut_affine,
        small,
        expand_weight,
        strided_slope,
        strided_unit,
        scratch=[rows(wider)],

        late=(11, 12, 13,),
        keep=(4, 5, 6),
        flops=ops(small_pixels, wider, last),
    )
    halo = swap_rows(edge)
    gathered = gather_all(sent)

    def small_image(value):
        return value.reshape(batch, height // 2, width // 2, value.shape[-1])

    def image(value):
        return value.reshape(batch, height, width, value.shape[-1])

    order = [affine_expand]

    def wave_parts(kernel, shape, *operands, flops, free=True):
        parts = call(
            kernel,
            [((shape[0] // 2, shape[1] // 2), BF16)] * 4,
            *operands,
            scratch=[(shape, BF16)],
            flops=flops,
            late=None,
            free=free,
            after=(order[0],),
        )
        order[0] = parts[0]
        return parts

    first_shape = ((wide_in + wider) // 2, last)
    (first,) = call(
        first_wave_kernel,
        [(first_shape, BF16)],
        shortcut_in,
        short_other,
        strided_act,
        strided_act_other,
        shortcut_grad,
        swap_rows(shortcut_grad),
        expand_grad,
        swap_rows(expand_grad),

        flops=ops(2 * small_pixels, *first_shape),
        late=None,
        after=(order[0],),
    )
    order[0] = first
    first = lax.psum(first, "img")

    affine_strided, strided_grad, widen_back, sent = call(
        functools.partial(widen_back_kernel, dims),
        [((2, wider), F32), ((small_pixels, wider), BF16), ((pixels, wider), F32), message(wider)],
        gathered,
        counts,
        strided_back,
        strided_unit,
        halo,
        small,
        small_below,
        strided_stats,
        strided_affine,
        strided_weight,
        widen_unit,
        widen_slope,
        scratch=[
            rows(wider),
            ((batch * (height // 2 + 1) * width // 2 + 8, wider), F32),
            ((wider // LANES, pixels, LANES), F32),
        ],
        late=(3, 9, 10, 11),
        keep=(2, 3),
        after=(order[0],),
        flops=ops(small_pixels, 9, wider, wider),
    )
    gathered = gather_all(sent)
    order[0] = affine_strided
    strided_grad_other = swap_rows(strided_grad)
    (short_back,) = call(
        functools.partial(short_back_kernel, dims),
        [((wide_in // LANES, pixels, LANES), F32)],
        shortcut_grad,
        shortcut_weight,
        late=(0, 1),
        keep=(),
        after=(order[0],),
        flops=ops(small_pixels, wide_in, last),
    )
    order[0] = short_back
    affine_widen, widen_grad, block_back, sent, block_back_saved = call(
        block_back_kernel,
        [
            ((2, wider), F32),
            ((pixels, wider), BF16),
            ((pixels, wide_in), F32),
            message(wide_in),
            ((pixels, wide_in), F32),
        ],
        gathered,
        counts,
        widen_back,
        widen_unit,
        mask,
        widen_stats,
        widen_affine,
        widen_weight,
        short_back,
        closing_unit,
        block_slope,
        scratch=[rows(wide_in)],
        late=(3, 7, 8, 9, 10),
        keep=(2, 3),
        after=(order[0],),
        flops=ops(pixels, wide_in, wider),
    )
    gathered = gather_all(sent)

    order[0] = affine_widen
    widen_grad_other = swap_rows(widen_grad)
    second_shape = (9 * wider // 2, wider)
    second_parts = wave_parts(
        second_wave_kernel,
        second_shape,
        taps,
        taps_other,
        strided_grad,
        strided_grad_other,
        flops=ops(2 * small_pixels, *second_shape),
        free=False,
    )
    second_got = exchange(second_parts[2:], steps()[0])

    affine_closing, closing_grad, middle_back, edge, sent = call(
        functools.partial(middle_back_kernel, dims),
        [
            ((2, wide_in), F32),
            ((pixels, wide_in), BF16),
            ((pixels, mid), F32),
            ((2 * batch * width, mid), F32),
            message(mid),
        ],
        gathered,
        counts,
        block_back,
        closing_unit,
        mask,
        closing_stats,
        closing_affine,
        closing_weight,
        middle_unit,
        middle_slope,
        scratch=[rows(mid)],

        late=(3, 7, 8, 9,),
        keep=(2, 3, 4),
        after=(order[0],),
        flops=ops(pixels, wide_in, mid),
    )
    halo = swap_rows(edge)
    gathered = gather_all(sent)
    order[0] = affine_closing
    closing_grad_other = swap_rows(closing_grad)
    affine_middle, middle_grad, entry_back, sent = call(
        functools.partial(entry_back_kernel, dims),
        [((2, mid), F32), ((pixels, mid), BF16), ((pixels, mid), F32), message(mid)],
        gathered,
        counts,
        middle_back,
        middle_unit,
        halo,
        mask,
        above,
        below,
        middle_stats,
        middle_affine,
        middle_weight,
        entry_unit,
        entry_slope,
        scratch=[rows(mid), ((padded_rows + 16, mid), F32), ((batch, (height + 2) * width, 3 * mid), BF16)],
        late=(3, 10, 11, 12),
        keep=(2, 3),
        after=(order[0],),
        flops=ops(pixels, 9, mid, mid),
    )
    gathered = gather_all(sent)
    order[0] = affine_middle
    middle_grad_other = swap_rows(middle_grad)
    third_sizes = (wide_in // 2 * wider // mid, wide_in // 2, 9 * mid // 2, wide_in // 2)
    third_shape = (-(-sum(third_sizes) // 256) * 256, mid)
    (third_early,) = call(
        functools.partial(third_early_kernel, dims),
        [((sum(third_sizes[:3]), mid), BF16)],
        block_out,
        block_other,
        widen_grad,
        widen_grad_other,
        middle_act,
        middle_act_other,
        closing_grad,
        closing_grad_other,
        triple,
        triple_other,
        middle_grad,
        middle_grad_other,
        flops=ops(2 * pixels, *third_shape),
        late=None,
        after=(order[0],),
    )
    order[0] = third_early
    second_kept, second_sent = halve(
        order, second_parts[:2], second_got, steps()[1], second_shape[0] // 4, second_shape[1] // 2
    )
    affine_entry, entry_grad, image_grads = call(
        images_kernel,
        [((2, mid), F32), ((pixels, mid), BF16), ((pixels, wide_in), BF16)],
        gathered,
        counts,
        entry_back,
        entry_unit,
        mask,
        entry_stats,
        entry_affine,
        entry_weight,
        block_back_saved,
        late=(3, 7, 8),
        keep=(),
        after=(order[0],),
        flops=ops(pixels, mid, wide_in),
    )

    order[0] = affine_entry
    third_parts = wave_parts(
        third_wave_kernel,
        third_shape,
        third_early,
        entry_in,
        entry_in_other,
        entry_grad,
        swap_rows(entry_grad),
        flops=ops(2 * pixels, wide_in // 2, mid),
    )

    second_result = ((9, wider // 2, wider), F32)

    def most(second_parts, third_parts):
        order = [third_parts[0]]
        waves = {
            "b": sum_over_chips(
                order, second_parts[:2], second_parts[2:], 1, second_shape, (second_out, [second_result])
            ),
            "c": sum_over_chips(order, third_parts[:2], third_parts[2:], 0, third_shape),
        }
        sums = {}
        for name in "bc" + 16 * "bc":
            if name not in sums:
                result = next(waves[name])
                if result is not None:
                    sums[name] = list(result)
        return sums["b"], sums["c"]

    def none(second_parts, third_parts):
        del second_parts, third_parts
        half = (third_shape[0] // 2, third_shape[1] // 2)
        return [jnp.zeros(*second_result)], [jnp.zeros(half, BF16)] * 2

    (strided_total,), third_own = lax.cond(local[0, 1] > 0, most, none, [*second_kept, *second_sent], list(third_parts))
    third_got = exchange(third_own, steps()[0])
    shortcut_total, expand_total = call(
        first_out,
        [((wide_in // 2, last), F32), ((wider // 2, last), F32)],
        first,
        late=None,
        after=(third_own[0],),
    )
    order[0] = shortcut_total
    widen_total, closing_total, middle_total, entry_total = run_after(
        order,
        functools.partial(out_kernel, third_out, steps()[0]),
        [
            ((wide_in // 2, wider), F32),
            ((mid // 2, wide_in), F32),
            ((9, mid // 2, mid), F32),
            ((wide_in // 2, mid), F32),
        ],
        *third_own,
        *third_got,
        scratch=[(third_shape, BF16)],
        free=False,
    )
    middle_total = middle_total.reshape(3, 3, mid // 2, mid)
    strided_total = strided_total.reshape(3, 3, wider // 2, wider)
    return (
        small_image(features),
        image(image_grads),
        entry_total,
        middle_total,
        closing_total,
        widen_total,
        strided_total,
        expand_total,
        shortcut_total,
        affine_entry,
        affine_middle,
        affine_closing,
        affine_widen,
        affine_strided,
        affine_expand,
        affine_shortcut,
    )


def solution(mesh):
    image = P("img", "row", None, None)
    return jax.shard_map(
        per_device,
        mesh=mesh,
        in_specs=(image, P("img", None)) + (P(),) * 14 + (image,),
        out_specs=(
            image,
            image,
            P("row", None),
            P(None, None, "row", None),
            P("row", None),
            P("row", None),
            P(None, None, "row", None),
            P("row", None),
            P("row", None),
        )
        + (P(),) * 7,
        check_vma=False,
    )
```

```python
import functools
import math

import jax
import jax.numpy as jnp
from jax import lax
from jax.experimental import pallas as pl
from jax.experimental.pallas import tpu as pltpu
from jax.sharding import PartitionSpec as P

EPS = 1e-05
BOTH = ("img", "row")
F32 = jnp.float32
BF16 = jnp.bfloat16
LANES = 128
MIB = 1 << 20


def swap_rows(value):
    count = lax.axis_size("row")
    return lax.ppermute(value, "row", [(i, (i + 1) % count) for i in range(count)])


def gather_all(message):
    return lax.all_to_all(message, BOTH, 0, 0, tiled=True)


def gather_img(message):
    return lax.all_to_all(message, "img", 0, 0, tiled=True)


class Late:
    def __init__(self, source, buffer, semaphores):
        self.buffer = buffer
        self.shape, self.ndim, self.dtype = buffer.shape, len(buffer.shape), buffer.dtype
        parts = parts_of(self.shape)
        if parts == 1:
            self.copies = [pltpu.make_async_copy(source, buffer, semaphores.at[0])]
        else:
            self.copies = [
                pltpu.make_async_copy(source.at[i], buffer.at[i], semaphores.at[i]) for i in range(parts)
            ]
        for copy in self.copies:
            copy.start()
        self.waiting = set(range(parts))

    def ready(self, part=None):
        for i in sorted(self.waiting):
            if part is None or i == part:
                self.copies[i].wait()
                self.waiting.remove(i)
        return self.buffer

    def __getitem__(self, index):
        first = index[0] if isinstance(index, tuple) else index
        part = first if isinstance(first, int) and len(self.copies) > 1 else None
        return self.ready(part)[index]


def parts_of(shape):
    return shape[0] if len(shape) >= 3 and shape[0] == 3 else 1


class Saved:
    def __init__(self, target, buffer, semaphore):
        self.target, self.buffer, self.semaphore, self.copy = target, buffer, semaphore, None
        self.shape, self.ndim, self.dtype = buffer.shape, len(buffer.shape), buffer.dtype

    def send(self):
        if self.copy is None:
            self.copy = pltpu.make_async_copy(self.buffer, self.target, self.semaphore)
            self.copy.start()

    def __getitem__(self, index):
        return self.buffer[index]

    def __setitem__(self, index, value):
        self.buffer[index] = value


def send(*results):
    for result in results:
        if isinstance(result, Saved):
            result.send()


def call(kernel, outs, *operands, scratch=(), smem=(), late=(), flops=0, keep=(), limit=24, after=(), free=False):
    late = [place for place in (range(len(operands)) if late is None else late) if place not in smem]
    used = len(operands)
    operands += tuple(after)
    saved = [place for place in range(len(outs)) if place not in keep and not free]
    moved = sum(x.size * x.dtype.itemsize for x in operands) + sum(
        math.prod(shape) * jnp.dtype(dtype).itemsize for shape, dtype in outs
    )

    def place_of_operand(place):
        if place in smem:
            return pltpu.SMEM
        return pl.ANY if place in late or place >= used else pltpu.VMEM

    operands = [
        pltpu.with_memory_space_constraint(x, pltpu.HBM) if place in late or (place >= used and in_hbm(x)) else x
        for place, x in enumerate(operands)
    ]
    buffers = [pltpu.VMEM(operands[place].shape, operands[place].dtype) for place in late]
    buffers += [pltpu.VMEM(*outs[place]) for place in saved]
    semaphores = [pltpu.SemaphoreType.DMA((parts_of(operands[place].shape),)) for place in late]
    semaphores += [pltpu.SemaphoreType.DMA] * len(saved)

    def body(*refs):
        refs = list(refs)
        inputs, refs = refs[: len(operands)], refs[len(operands) :]
        results, refs = refs[: len(outs)], refs[len(outs) :]
        own, refs = refs[: len(scratch)], refs[len(scratch) :]
        space, marks = refs[: len(buffers)], refs[len(buffers) :]
        for number, place in enumerate(late):
            inputs[place] = Late(inputs[place], space[number], marks[number])
        for number, place in enumerate(saved):
            number += len(late)
            results[place] = Saved(results[place], space[number], marks[number])
        kernel(*inputs[:used], *results, *own)
        for place in late:
            inputs[place].ready()
        for place in saved:
            results[place].send()
        for place in saved:
            results[place].copy.wait()

    results = pl.pallas_call(
        body,
        out_shape=[
            jax.ShapeDtypeStruct(shape, dtype)
            if free
            else (pltpu.VMEM if place in keep else pltpu.HBM)(shape, dtype)
            for place, (shape, dtype) in enumerate(outs)
        ],
        in_specs=[pl.BlockSpec(memory_space=place_of_operand(place)) for place in range(len(operands))],
        out_specs=[
            pl.BlockSpec(memory_space=pl.ANY if place in saved else pltpu.VMEM) for place in range(len(outs))
        ],
        scratch_shapes=[pltpu.VMEM(shape, dtype) for shape, dtype in scratch] + buffers + semaphores,
        compiler_params=pltpu.CompilerParams(vmem_limit_bytes=limit * MIB),
        cost_estimate=pl.CostEstimate(flops=flops, bytes_accessed=moved, transcendentals=0),
    )(*operands)
    HELD.extend(results[place] for place in saved)
    return results


HELD = []


def in_hbm(value):
    return any(value is held for held in HELD)


def dot(left, right):
    return jnp.dot(left, right, preferred_element_type=F32)


def dot_back(grad, weight):
    return lax.dot_general(grad, weight, (((1,), (1,)), ((), ())), preferred_element_type=F32)


def wide(mask, width):
    return mask if width == LANES else jnp.concatenate([mask] * (width // LANES), axis=1)


def column_sum(value):
    return jnp.sum(value, axis=0, keepdims=True)


def spread_message(message, rows):
    tile = rows[...]
    for device in range(message.shape[0]):
        message[device] = tile


def put_row(rows, place, vector):
    for block in range(vector.shape[1] // LANES):
        rows[place + block : place + block + 1, :] = vector[:, block * LANES : (block + 1) * LANES]


def local_stats(raw, mask, rows, place=0):
    blocks = raw.shape[1] // LANES
    number = jnp.maximum(column_sum(mask[...]), 1.0)
    for block in range(blocks):
        columns = slice(block * LANES, (block + 1) * LANES)
        total = column_sum(raw[:, columns] * mask[...])
        centred = (raw[:, columns] - total / number) * mask[...]
        rows[place + block : place + block + 1, :] = total
        rows[place + blocks + block : place + blocks + block + 1, :] = column_sum(centred * centred)


def total_count(counts, place):
    return functools.reduce(
        jnp.add, [counts[i, place : place + 1, :] for i in range(counts.shape[0])]
    )


def join_stats(gathered, counts, place, stats, blocks):
    devices = gathered.shape[0]
    count = total_count(counts, place)
    mean = functools.reduce(jnp.add, [gathered[i, :blocks, :] for i in range(devices)]) / count
    spread = functools.reduce(jnp.add, [gathered[i, blocks : 2 * blocks, :] for i in range(devices)])
    for i in range(devices):
        number = counts[i, place : place + 1, :]
        shift = gathered[i, :blocks, :] / jnp.maximum(number, 1.0) - mean
        spread = spread + number * (shift * shift)
    scale = lax.rsqrt(spread / count + EPS)
    for block in range(blocks):
        columns = slice(block * LANES, (block + 1) * LANES)
        stats[0:1, columns] = mean[block : block + 1, :]
        stats[1:2, columns] = scale[block : block + 1, :]


def join_sums(gathered, affine):
    total = functools.reduce(jnp.add, [gathered[i] for i in range(gathered.shape[0])])
    blocks = affine.shape[1] // LANES
    for block in range(blocks):
        columns = slice(block * LANES, (block + 1) * LANES)
        affine[0:1, columns] = total[block : block + 1, :]
        affine[1:2, columns] = total[blocks + block : blocks + block + 1, :]


def chunks(rows, width, chunk=32, block=256):
    for start in range(0, width, block):
        for row in range(0, rows, chunk):
            yield slice(row, row + min(chunk, rows - row)), slice(start, start + min(block, width - start))


def silu_parts(value):
    gate = jax.nn.sigmoid(value)
    return value * gate, gate * (1.0 + value * (1.0 - gate))


def normed(raw, stats, params, columns):
    unit = (raw - stats[0:1, columns]) * stats[1:2, columns]
    return unit, unit * params[0:1, columns] + params[1:2, columns]


def act_pass(raw, mask, stats, params, unit, slope, act, skip=None, keep=None):
    rows, width = raw.shape
    for here, columns in chunks(rows, width):
        u, value = normed(raw[here, columns], stats, params, columns)
        if skip is not None:
            value = value + skip[here, columns].astype(F32)
        m = wide(mask[here, :], columns.stop - columns.start)
        out, rise = silu_parts(value)
        out = out * m
        unit[here, columns] = u
        slope[here, columns] = rise * m
        if act is not None:
            act[here, columns] = out.astype(BF16)
        if keep is not None:
            keep(here, columns, out)


def back_pass(back, unit, slope, rows):
    blocks = back.shape[1] // LANES
    for block in range(blocks):
        columns = slice(block * LANES, (block + 1) * LANES)
        value = back[:, columns] * slope[:, columns]
        back[:, columns] = value
        rows[block : block + 1, :] = column_sum(value * unit[:, columns])
        rows[blocks + block : blocks + block + 1, :] = column_sum(value)


def raw_grad(back, unit, mask, sums, stats, params, count, columns):
    width = columns.stop - columns.start
    n = wide(count, width)
    factor = params[0:1, columns] * stats[1:2, columns]
    centred = back - sums[1:2, columns] / n - unit * (sums[0:1, columns] / n)
    return factor * centred * wide(mask, width)


def grad_pass(back, unit, mask, sums, stats, params, count, grad, keep=None):
    for here, columns in chunks(*back.shape):
        value = raw_grad(
            back[here, columns], unit[here, columns], mask[here, :], sums, stats, params, count, columns
        )
        grad[here, columns] = value.astype(BF16)
        if keep is not None:
            keep(here, columns, value)


def valid(extents, image, first_row, columns, shape, step):
    place = lax.broadcasted_iota(jnp.int32, shape, 0)
    row = first_row + step * (place // columns)
    column = step * (place % columns)
    return jnp.where((row < extents[image, 0]) & (column < extents[image, 1]), 1.0, 0.0).astype(F32)


def core_number():
    return lax.axis_index("row").astype(jnp.int32)


def is_upper():
    return jnp.where(core_number() == 0, 1.0, 0.0).astype(F32)


def own_half(size):
    return pl.ds(pl.multiple_of(core_number() * size, LANES), size)


def other_half(size):
    return pl.ds(pl.multiple_of((1 - core_number()) * size, LANES), size)


def give_half(value, give):
    give[...] = value[:, other_half(give.shape[1])]
    send(give)


def entry_kernel(
    dims, extents, images, weight,
    entry_in, mask, small, above, below, small_below, raw, edge, message, give, rows,
):
    batch, height, width = dims
    pixels = height * width
    upper = is_upper()
    for b in range(batch):
        mask[b * pixels : (b + 1) * pixels, :] = valid(extents, b, 0, width, (pixels, LANES), 1)
        small[b * pixels // 4 : (b + 1) * pixels // 4, :] = valid(
            extents, b, 0, width // 2, (pixels // 4, LANES), 2
        )
        line = slice(b * width, (b + 1) * width)
        above[line, :] = valid(extents, b, -1, width, (width, LANES), 1) * (1.0 - upper)
        below[line, :] = valid(extents, b, height, width, (width, LANES), 1) * upper
        small_below[b * width // 2 : (b + 1) * width // 2, :] = (
            valid(extents, b, height, width // 2, (width // 2, LANES), 2) * upper
        )
    for here, columns in chunks(*images.shape):
        m = wide(mask[here, :], columns.stop - columns.start)
        entry_in[here, columns] = (images[here, columns].astype(F32) * m).astype(BF16)
    send(entry_in, mask, small, above, below, small_below)
    give_half(entry_in, give)
    raw[...] = dot(entry_in[...], weight[...])
    for b in range(batch):
        first = raw[b * pixels : b * pixels + width, :]
        last = raw[(b + 1) * pixels - width : (b + 1) * pixels, :]
        edge[b * width : (b + 1) * width, :] = last * upper + first * (1.0 - upper)
    rows[...] = jnp.zeros_like(rows)
    local_stats(raw, mask, rows)
    blocks = raw.shape[1] // LANES
    rows[2 * blocks : 2 * blocks + 1, :] = column_sum(mask[...])
    rows[2 * blocks + 1 : 2 * blocks + 2, :] = column_sum(small[...])
    spread_message(message, rows)


def put_blocks(target, here, columns, value):
    for start in range(columns.start, columns.stop, LANES):
        offset = start - columns.start
        target[start // LANES, here, :] = value[:, offset : offset + LANES]


def column_masks(rows, width):
    place = lax.broadcasted_iota(jnp.int32, (rows, LANES), 0) % width
    return (
        jnp.where(place == 0, 0.0, 1.0).astype(F32),
        jnp.where(place == width - 1, 0.0, 1.0).astype(F32),
    )


def fill_triple(padded, triple, batch, lines, width):
    size = lines * width
    channels = padded.shape[1]
    left_ok, right_ok = column_masks(size, width)
    for b in range(batch):
        start = 8 + b * size
        for c in range(0, channels, LANES):
            columns = slice(c, c + LANES)
            triple[b, :, c : c + LANES] = (padded[start - 1 : start - 1 + size, columns] * left_ok).astype(BF16)
            triple[b, :, channels + c : channels + c + LANES] = padded[start : start + size, columns].astype(BF16)
            triple[b, :, 2 * channels + c : 2 * channels + c + LANES] = (
                padded[start + 1 : start + 1 + size, columns] * right_ok
            ).astype(BF16)


def middle_kernel(
    dims, gathered, raw, halo, mask, above, below, params, weight,
    unit, slope, stats, out, message, triple, give, rows, padded,
):
    batch, height, width = dims
    pixels = height * width
    size = pixels + 2 * width
    blocks = raw.shape[1] // LANES
    join_stats(gathered, gathered, 2 * blocks, stats, blocks)
    everything = slice(0, raw.shape[1])
    _, value = normed(halo[...], stats, params, everything)
    rim, _ = silu_parts(value)
    padded[0:8, :] = jnp.zeros((8, raw.shape[1]), F32)
    padded[8 + batch * size :, :] = jnp.zeros((8, raw.shape[1]), F32)
    for b in range(batch):
        line = slice(b * width, (b + 1) * width)
        top = 8 + b * size
        padded[top : top + width, :] = rim[line] * wide(above[line, :], raw.shape[1])
        padded[top + size - width : top + size, :] = rim[line] * wide(below[line, :], raw.shape[1])

    def keep(here, columns, value):
        b = here.start // pixels
        start = 8 + b * size + width + here.start - b * pixels
        padded[start : start + here.stop - here.start, columns] = value

    act_pass(raw, mask, stats, params, unit, slope, None, keep=keep)
    send(unit, slope, stats)
    fill_triple(padded, triple, batch, height + 2, width)
    send(triple)
    give_taps(triple, give)
    total = None
    for tap in range(3):
        left = triple[:, tap * width : tap * width + pixels, :].reshape(batch * pixels, -1)
        part = dot(left, weight[tap])
        total = part if total is None else total + part
    out[...] = total
    local_stats(out, mask, rows)
    spread_message(message, rows)


def give_taps(taps, give):
    full, half = taps.shape[2] // 3, give.shape[2] // 3
    for tap in range(3):
        start = pl.multiple_of(tap * full + (1 - core_number()) * half, LANES)
        give[:, :, tap * half : (tap + 1) * half] = taps[:, :, pl.ds(start, half)]
    send(give)


def closing_kernel(
    gathered, counts, raw, mask, params, weight, act, unit, slope, stats, out, message, give, rows
):
    blocks = raw.shape[1] // LANES
    join_stats(gathered, counts, 4, stats, blocks)
    act_pass(raw, mask, stats, params, unit, slope, act)
    send(unit, slope, act, stats)
    give_half(act, give)
    out[...] = dot(act[...], weight[...])
    local_stats(out, mask, rows)
    spread_message(message, rows)


def widen_kernel(
    dims, gathered, counts, raw, entry_in, mask, params, weight,
    act, unit, slope, stats, short, out, edge, message, give, give_short, rows, even,
):
    batch, height, width = dims
    pixels = height * width
    blocks = raw.shape[1] // LANES
    join_stats(gathered, counts, 4, stats, blocks)

    def keep(here, columns, value):
        put_blocks(even, here, columns, value)

    act_pass(raw, mask, stats, params, unit, slope, act, skip=entry_in, keep=keep)
    send(unit, slope, act, stats)
    give_half(act, give)
    out[...] = dot(act[...], weight[...])
    for b in range(batch):
        edge[b * width : (b + 1) * width, :] = out[(b + 1) * pixels - width : (b + 1) * pixels, :]
    local_stats(out, mask, rows)
    spread_message(message, rows)
    for c in range(0, raw.shape[1], LANES):
        columns = slice(c, c + LANES)
        lines = []
        for b in range(batch):
            for i in range(height // 2):
                lines.append(even[c // LANES, pl.ds(b * pixels + 2 * i * width, width // 2, stride=2), :])
        short[:, columns] = jnp.concatenate(lines, axis=0).astype(BF16)
    send(short)
    give_half(short, give_short)


def shortcut_kernel(short, small, weight, out, rows):
    out[...] = dot(short[...], weight[...])
    send(out)
    local_stats(out, small, rows)


def strided_kernel(
    dims, gathered, counts, raw, halo, mask, small, above, params, weight,
    unit, slope, stats, out, message, taps, give, rows, padded,
):
    batch, height, width = dims
    pixels = height * width
    size = pixels + width
    half, half_width = height // 2, width // 2
    blocks = raw.shape[1] // LANES
    join_stats(gathered, counts, 4, stats, blocks)
    everything = slice(0, raw.shape[1])
    _, value = normed(halo[...], stats, params, everything)
    rim, _ = silu_parts(value)
    for block in range(padded.shape[0]):
        padded[block, 0:8, :] = jnp.zeros((8, LANES), F32)
    for b in range(batch):
        line = slice(b * width, (b + 1) * width)
        start = 8 + b * size
        put_blocks(padded, slice(start, start + width), everything, rim[line] * wide(above[line, :], raw.shape[1]))

    def keep(here, columns, value):
        b = here.start // pixels
        start = 8 + b * size + width + here.start - b * pixels
        put_blocks(padded, slice(start, start + here.stop - here.start), columns, value)

    act_pass(raw, mask, stats, params, unit, slope, None, keep=keep)
    send(unit, slope, stats)
    lines = height + 1
    not_first, _ = column_masks(lines * half_width, half_width)
    channels = raw.shape[1]
    for block in range(channels // LANES):
        for b in range(batch):
            start = 8 + b * size
            before = padded[block, pl.ds(start - 1, lines * half_width, stride=2), :] * not_first
            at = padded[block, pl.ds(start, lines * half_width, stride=2), :]
            after = padded[block, pl.ds(start + 1, lines * half_width, stride=2), :]
            for k, value in enumerate((before, at, after)):
                value = value.reshape(lines, half_width, LANES)
                place = k * channels + block * LANES
                for tap in range(3):
                    pieces = [value[tap + 2 * i] for i in range(half)]
                    taps[tap, b * half * half_width : (b + 1) * half * half_width, place : place + LANES] = (
                        jnp.concatenate(pieces, axis=0).astype(BF16)
                    )
    send(taps)
    give_taps(taps, give)
    total = None
    for tap in range(3):
        part = dot(taps[tap], weight[tap])
        total = part if total is None else total + part
    out[...] = total
    local_stats(out, small, rows)
    spread_message(message, rows)


def expand_kernel(
    gathered, counts, raw, small, params, weight, short_rows,
    act, unit, slope, stats, out, mine, theirs, give, rows,
):
    blocks = raw.shape[1] // LANES
    join_stats(gathered, counts, 5, stats, blocks)
    act_pass(raw, small, stats, params, unit, slope, act)
    send(unit, slope, act, stats)
    give_half(act, give)
    out[...] = dot(act[...], weight[...])
    local_stats(out, small, rows)
    upper = is_upper()
    size = rows.shape[0]
    number = jnp.broadcast_to(column_sum(small[...]), (8, LANES))
    mine[:size, :] = rows[...] * upper + short_rows[...] * (1.0 - upper)
    theirs[:size, :] = rows[...] * (1.0 - upper) + short_rows[...] * upper
    mine[size:, :] = number
    theirs[size:, :] = number


def pair_kernel(mine, other, message):
    size = mine.shape[0] - 8
    blocks = size // 2
    first, second = mine[size : size + 1, :], other[size : size + 1, :]
    both = first + second
    gap = mine[:blocks, :] / jnp.maximum(first, 1.0) - other[:blocks, :] / jnp.maximum(second, 1.0)
    weight = first * second / jnp.maximum(both, 1.0)
    total = mine[:blocks, :] + other[:blocks, :]
    square = mine[blocks:size, :] + other[blocks:size, :] + gap * gap * weight
    number = jnp.broadcast_to(both, (8, LANES))
    for i in range(message.shape[0]):
        message[i, :blocks, :] = total
        message[i, blocks:size, :] = square
        message[i, size:, :] = number


def join_kernel(gathered, stats):
    size = gathered.shape[1] - 8
    stats[...] = jnp.zeros_like(stats)
    join_stats(gathered, gathered, size, stats, size // 2)


def final_kernel(
    own, other, expand_raw, short_raw, small, expand_params, short_params, cotangent,
    features, grad, expand_unit, short_unit, expand_stats, short_stats, mine, theirs, rows,
):
    upper = is_upper()
    expand_stats[...] = own[...] * upper + other[...] * (1.0 - upper)
    short_stats[...] = own[...] * (1.0 - upper) + other[...] * upper
    height, width = expand_raw.shape
    blocks = width // LANES
    for block in range(blocks):
        columns = slice(block * LANES, (block + 1) * LANES)
        first, first_value = normed(expand_raw[:, columns], expand_stats, expand_params, columns)
        second, second_value = normed(short_raw[:, columns], short_stats, short_params, columns)
        out, rise = silu_parts(first_value + second_value)
        features[:, columns] = (out * small[...]).astype(BF16)
        value = cotangent[:, columns].astype(F32) * (rise * small[...])
        grad[:, columns] = value
        expand_unit[:, columns] = first
        short_unit[:, columns] = second
        rows[block : block + 1, :] = column_sum(value * first)
        rows[blocks + block : blocks + block + 1, :] = column_sum(value * second)
        rows[2 * blocks + block : 2 * blocks + block + 1, :] = column_sum(value)
    half = blocks // 2
    for stat in range(3):
        low = rows[stat * blocks : stat * blocks + half, :]
        high = rows[stat * blocks + half : (stat + 1) * blocks, :]
        mine[stat * half : (stat + 1) * half, :] = low * upper + high * (1.0 - upper)
        theirs[stat * half : (stat + 1) * half, :] = low * (1.0 - upper) + high * upper


def last_grads_kernel(
    batch, own, other, counts, grad, expand_unit, short_unit, expand_stats, short_stats,
    expand_params, short_params, small, weight, slope, unit,
    expand_affine, short_affine, expand_grad, short_grad, back, edge, message, rows,
):
    upper = is_upper()
    half = own.shape[0] // 3
    for stat in range(3):
        part = slice(stat * half, (stat + 1) * half)
        low = own[part, :] * upper + other[part, :] * (1.0 - upper)
        high = own[part, :] * (1.0 - upper) + other[part, :] * upper
        for block in range(2 * half):
            value = low[block : block + 1, :] if block < half else high[block - half : block - half + 1, :]
            columns = slice(block * LANES, (block + 1) * LANES)
            if stat == 0:
                expand_affine[0:1, columns] = value
            elif stat == 1:
                short_affine[0:1, columns] = value
            else:
                expand_affine[1:2, columns] = value
                short_affine[1:2, columns] = value
    count = total_count(counts, 5)
    for here, columns in chunks(*grad.shape):
        expand_grad[here, columns] = raw_grad(
            grad[here, columns], expand_unit[here, columns], small[here, :], expand_affine, expand_stats,
            expand_params, count, columns,
        ).astype(BF16)
        short_grad[here, columns] = raw_grad(
            grad[here, columns], short_unit[here, columns], small[here, :], short_affine, short_stats,
            short_params, count, columns,
        ).astype(BF16)
    send(expand_grad, short_grad, expand_affine, short_affine)
    back[...] = dot_back(expand_grad[...], weight[...])
    back_pass(back, unit, slope, rows)
    spread_message(message, rows)
    pixels = back.shape[0] // batch
    line = edge.shape[0] // (2 * batch)
    for b in range(batch):
        edge[b * line : (b + 1) * line, :] = back[b * pixels : b * pixels + line, :]
        edge[(batch + b) * line : (batch + b + 1) * line, :] = unit[b * pixels : b * pixels + line, :]


def short_back_kernel(dims, grad, weight, out):
    batch, height, width = dims
    pixels = height * width
    small = dot_back(grad[...], weight[...])
    out[...] = jnp.zeros(out.shape, out.dtype)
    half = width // 2
    for block in range(out.shape[0]):
        columns = slice(block * LANES, (block + 1) * LANES)
        for b in range(batch):
            for i in range(height // 2):
                place = b * pixels // 4 + i * half
                start = b * pixels + 2 * i * width
                out[block, pl.ds(start, half, stride=2), :] = small[place : place + half, columns]


def widen_back_kernel(
    dims, gathered, counts, back, unit, halo, small, small_below, stats, params, weight, out_unit, out_slope,
    affine, grad, out, message, rows, padded, full,
):
    batch, height, width = dims
    pixels = height * width
    half, half_width = height // 2, width // 2
    size = (half + 1) * half_width
    join_sums(gathered, affine)
    count = total_count(counts, 5)
    channels = back.shape[1]
    everything = slice(0, channels)
    line = batch * half_width
    rim = raw_grad(
        halo[:line, :], halo[line:, :], small_below[...], affine, stats, params, count, everything
    ).astype(BF16).astype(F32)
    for b in range(batch):
        stop = (b + 1) * size
        padded[stop - half_width : stop, :] = rim[b * half_width : (b + 1) * half_width]
    padded[batch * size :, :] = jnp.zeros((8, channels), F32)
    small_pixels = half * half_width
    for here, columns in chunks(back.shape[0], channels, chunk=small_pixels):
        value = raw_grad(
            back[here, columns], unit[here, columns], small[here, :], affine, stats, params, count, columns
        ).astype(BF16)
        grad[here, columns] = value
        b = here.start // small_pixels
        padded[b * size : b * size + small_pixels, columns] = value.astype(F32)
    send(grad, affine)
    _, not_last = column_masks(small_pixels, half_width)
    not_last = wide(not_last, channels)

    def moved(down, right):
        pieces = []
        for b in range(batch):
            start = b * size + down * half_width + right
            piece = padded[start : start + small_pixels, :]
            pieces.append(piece * not_last if right else piece)
        return jnp.concatenate(pieces, axis=0).astype(BF16)

    here, right, down, across = moved(0, 0), moved(0, 1), moved(1, 0), moved(1, 1)
    phases = {
        (0, 0): dot_back(here, weight[1, 1]),
        (0, 1): dot_back(here, weight[1, 2]) + dot_back(right, weight[1, 0]),
        (1, 0): dot_back(here, weight[2, 1]) + dot_back(down, weight[0, 1]),
        (1, 1): dot_back(here, weight[2, 2])
        + dot_back(right, weight[2, 0])
        + dot_back(down, weight[0, 2])
        + dot_back(across, weight[0, 0]),
    }
    for (a, e), value in phases.items():
        for b in range(batch):
            for i in range(half):
                place = b * small_pixels + i * half_width
                start = b * pixels + (2 * i + a) * width + e
                for block in range(full.shape[0]):
                    full[block, pl.ds(start, half_width, stride=2), :] = value[
                        place : place + half_width, block * LANES : (block + 1) * LANES
                    ]
    for block in range(full.shape[0]):
        out[:, block * LANES : (block + 1) * LANES] = full[block]
    back_pass(out, out_unit, out_slope, rows)
    spread_message(message, rows)


def block_back_kernel(
    gathered, counts, back, unit, mask, stats, params, weight, short_back, out_unit, out_slope,
    affine, grad, out, message, again, rows,
):
    join_sums(gathered, affine)
    grad_pass(back, unit, mask, affine, stats, params, total_count(counts, 4), grad)
    send(grad, affine)
    short = jnp.concatenate([short_back[block] for block in range(short_back.shape[0])], axis=1)
    out[...] = dot_back(grad[...], weight[...]) + short
    back_pass(out, out_unit, out_slope, rows)
    again[...] = out[...]
    send(again)
    spread_message(message, rows)


def middle_back_kernel(
    dims, gathered, counts, back, unit, mask, stats, params, weight, out_unit, out_slope,
    affine, grad, out, edge, message, rows,
):
    batch, height, width = dims
    pixels = height * width
    upper = is_upper()
    join_sums(gathered, affine)
    grad_pass(back, unit, mask, affine, stats, params, total_count(counts, 4), grad)
    send(grad, affine)
    out[...] = dot_back(grad[...], weight[...])
    back_pass(out, out_unit, out_slope, rows)
    spread_message(message, rows)
    for place, source in ((0, out), (batch, out_unit)):
        for b in range(batch):
            first = source[b * pixels : b * pixels + width, :]
            last = source[(b + 1) * pixels - width : (b + 1) * pixels, :]
            edge[(place + b) * width : (place + b + 1) * width, :] = last * upper + first * (1.0 - upper)


def entry_back_kernel(
    dims, gathered, counts, back, unit, halo, mask, above, below, stats, params, weight, out_unit, out_slope,
    affine, grad, out, message, rows, padded, triple,
):
    batch, height, width = dims
    pixels = height * width
    size = pixels + 2 * width
    join_sums(gathered, affine)
    count = total_count(counts, 4)
    channels = back.shape[1]
    everything = slice(0, channels)
    line = batch * width
    padded[0:8, :] = jnp.zeros((8, channels), F32)
    padded[8 + batch * size :, :] = jnp.zeros((8, channels), F32)
    up = raw_grad(halo[:line, :], halo[line:, :], above[...], affine, stats, params, count, everything)
    down = raw_grad(halo[:line, :], halo[line:, :], below[...], affine, stats, params, count, everything)
    for b in range(batch):
        here = slice(b * width, (b + 1) * width)
        top = 8 + b * size
        padded[top : top + width, :] = up[here]
        padded[top + size - width : top + size, :] = down[here]

    def keep(here, columns, value):
        b = here.start // pixels
        start = 8 + b * size + width + here.start - b * pixels
        padded[start : start + here.stop - here.start, columns] = value

    grad_pass(back, unit, mask, affine, stats, params, count, grad, keep=keep)
    send(grad, affine)
    fill_triple(padded, triple, batch, height + 2, width)
    total = None
    for row_tap in range(3):
        shift = (2 - row_tap) * width
        for col_tap in range(3):
            side = (2 - col_tap) * channels
            left = triple[:, shift : shift + pixels, side : side + channels].reshape(batch * pixels, channels)
            part = dot_back(left, weight[row_tap, col_tap])
            total = part if total is None else total + part
    out[...] = total
    back_pass(out, out_unit, out_slope, rows)
    spread_message(message, rows)


def entry_grad_kernel(gathered, counts, back, unit, mask, stats, params, affine, grad):
    join_sums(gathered, affine)
    grad_pass(back, unit, mask, affine, stats, params, total_count(counts, 4), grad)


def images_kernel(grad, weight, block_back, mask, out):
    step = 256
    for start in range(0, out.shape[1], step):
        columns = slice(start, start + step)
        value = dot_back(grad[...], weight[columns, :]) + block_back[:, columns]
        out[:, columns] = (value * wide(mask[...], step)).astype(BF16)


def dot_pixels(left, grad):
    return lax.dot_general(left, grad, (((0,), (0,)), ((), ())), preferred_element_type=F32)


def chip_grad(left, left_other, grad, grad_other, columns=slice(None)):
    half = left_other.shape[1]
    return dot_pixels(left[:, own_half(half)], grad[:, columns]) + dot_pixels(
        left_other[...], grad_other[:, columns]
    )


class View:
    def __init__(self, refs, group):
        self.ref = refs[group] if len(refs) > 1 else refs[0]
        self.lead = () if len(refs) > 1 else (group,)
        self.rows = self.ref.shape[-2]

    def __getitem__(self, here):
        return self.ref[self.lead + (here, slice(None))]

    def __setitem__(self, here, value):
        self.ref[self.lead + (here, slice(None))] = value


def half_rows(bit, flip, rows):
    mine = (lax.axis_index("img").astype(jnp.int32) >> bit) & 1
    return pl.ds(pl.multiple_of((1 - mine if flip else mine) * rows, 16), rows)


def deal(full, parts):
    rows, width = parts[0].shape
    for outs, flip in ((parts[2:], True), (parts[:2], False)):
        for group, (out, bit) in enumerate(zip(outs, steps()[0])):
            out[...] = full[half_rows(bit, flip, rows), group * width : (group + 1) * width]


def first_wave_kernel(
    short, short_other, strided, strided_other,
    short_grad, short_grad_other, expand_grad, expand_grad_other, full
):
    rows = short_other.shape[1]
    step = 512
    for start in range(0, full.shape[1], step):
        columns = slice(start, start + step)
        full[:rows, columns] = chip_grad(
            short, short_other, short_grad, short_grad_other, columns
        ).astype(BF16)
        full[rows:, columns] = chip_grad(
            strided, strided_other, expand_grad, expand_grad_other, columns
        ).astype(BF16)


def second_wave_kernel(
    taps, taps_other, strided_grad, strided_grad_other, *results
):
    *parts, full = results
    half = taps_other.shape[2] // 3
    channels = 2 * half
    for row_tap in range(3):
        for col_tap in range(3):
            start = pl.multiple_of(col_tap * channels + core_number() * half, LANES)
            own = dot_pixels(taps[row_tap, :, pl.ds(start, half)], strided_grad[...])
            other = dot_pixels(
                taps_other[row_tap, :, col_tap * half : (col_tap + 1) * half], strided_grad_other[...]
            )
            place_row = (3 * row_tap + col_tap) * half
            full[place_row : place_row + half, :] = (own + other).astype(BF16)
    deal(full, parts)


def fill_rest(full, row):
    if row < full.shape[0]:
        full[row:, :] = jnp.zeros((full.shape[0] - row, full.shape[1]), full.dtype)


def third_early_kernel(
    dims, block, block_other, widen_grad, widen_grad_other, act, act_other, closing_grad,
    closing_grad_other, triple, triple_other, middle_grad, middle_grad_other, full,
):
    batch, height, width = dims
    pixels = height * width
    step = full.shape[1]
    row = 0
    for left, left_other, grad, grad_other in (
        (block, block_other, widen_grad, widen_grad_other),
        (act, act_other, closing_grad, closing_grad_other),
    ):
        rows = left_other.shape[1]
        for start in range(0, grad.shape[1], step):
            full[row : row + rows, :] = chip_grad(
                left, left_other, grad, grad_other, slice(start, start + step)
            ).astype(BF16)
            row += rows
    half = triple_other.shape[2] // 3
    channels = 2 * half
    for row_tap in range(3):
        lines = slice(row_tap * width, row_tap * width + pixels)
        for col_tap in range(3):
            start = pl.multiple_of(col_tap * channels + core_number() * half, LANES)
            own = triple[:, lines, pl.ds(start, half)].reshape(batch * pixels, half)
            other = triple_other[:, lines, col_tap * half : (col_tap + 1) * half].reshape(batch * pixels, half)
            value = dot_pixels(own, middle_grad[...]) + dot_pixels(other, middle_grad_other[...])
            full[row : row + half, :] = value.astype(BF16)
            row += half


def third_wave_kernel(early, entry_in, entry_in_other, entry_grad, entry_grad_other, *results):
    *parts, full = results
    row, rows = early.shape[0], entry_in_other.shape[1]
    full[row : row + rows, :] = chip_grad(entry_in, entry_in_other, entry_grad, entry_grad_other).astype(BF16)
    fill_rest(full, row + rows)
    full[:row, :] = early[...]
    deal(full, parts)


def split_refs(refs, sizes):
    parts, start = [], 0
    for size in sizes:
        parts.append(refs[start : start + size])
        start += size
    return parts


def added(first, second):
    return (first.astype(F32) + second.astype(F32)).astype(BF16)


def halve_kernel(sizes, bits, *refs):
    kept, got, keep, pass_on = split_refs(refs, sizes)
    for outs, flip in ((pass_on, True), (keep, False)):
        for group, bit in enumerate(bits):
            out, first, second = View(outs, group), View(kept, group), View(got, group)
            here = half_rows(bit, flip, out.rows)
            out[:] = added(first[here], second[here])


def add_kernel(kept, got, out):
    out[...] = added(kept[...], got[...])


def double_kernel(sizes, bits, *refs):
    own, got, outs = split_refs(refs, sizes)
    for group, bit in enumerate(bits):
        out, first, second = View(outs, group), View(own, group), View(got, group)
        out[half_rows(bit, False, first.rows)] = first[:]
        out[half_rows(bit, True, first.rows)] = second[:]


def first_out(full, short, expand):
    rows = short.shape[0]
    short[...] = full[:rows, :].astype(F32)
    send(short)
    expand[...] = full[rows:, :].astype(F32)


def second_out(full, strided):
    rows = strided.shape[1]
    for tap in range(9):
        strided[tap] = full[tap * rows : (tap + 1) * rows, :].astype(F32)


def third_out(full, widen, closing, middle, entry):
    step = full.shape[1]
    row = 0
    for out in (widen, closing):
        rows = out.shape[0]
        for start in range(0, out.shape[1], step):
            out[:, start : start + step] = full[row : row + rows, :].astype(F32)
            row += rows
        send(out)
    rows = middle.shape[1]
    for tap in range(9):
        middle[tap] = full[row : row + rows, :].astype(F32)
        row += rows
    send(middle)
    entry[...] = full[row : row + entry.shape[0], :].astype(F32)


def out_kernel(finish, bits, own_a, own_b, got_a, got_b, *refs):
    outs, full = refs[:-1], refs[-1]
    rows, width = own_a.shape
    for group, (bit, own, got) in enumerate(zip(bits, (own_a, own_b), (got_a, got_b))):
        columns = slice(group * width, (group + 1) * width)
        full[half_rows(bit, False, rows), columns] = own[...]
        full[half_rows(bit, True, rows), columns] = got[...]
    finish(full, *outs)


def steps():
    bits = lax.axis_size("img").bit_length() - 1
    return [(0, 1), (1, 0)] + [(bit, bit) for bit in range(2, bits)]


def to_chip(value, bit):
    count = lax.axis_size("img")
    return lax.ppermute(value, "img", [(i, i ^ (1 << bit)) for i in range(count)])


def exchange(values, bits):
    return [to_chip(value, bit) for value, bit in zip(values, bits)]


def run_after(order, kernel, shapes, *operands, scratch=(), free=True):
    results = call(kernel, shapes, *operands, free=free, after=(order[0],), scratch=scratch)
    order[0] = results[0]
    return results


def group_shapes(bits, rows, width):
    return [((2, rows, width), BF16)] if bits[0] == bits[1] else [((rows, width), BF16)] * 2


def halve(order, kept, got, bits, rows, width):
    shapes = group_shapes(bits, rows, width)
    sizes = (len(kept), len(got), len(shapes), len(shapes))
    results = run_after(order, functools.partial(halve_kernel, sizes, bits), shapes * 2, *kept, *got)
    return results[: len(shapes)], results[len(shapes) :]


def sum_over_chips(order, kept, sent, number, shape, finish=None):
    todo = steps()
    rows, width = shape[0] >> (number + 1), shape[1] // 2
    halvings = number + 1
    for number in range(number, len(todo)):
        got = exchange(sent, todo[number])
        yield None
        following = todo[number + 1] if number + 1 < len(todo) else None
        if following is not None and number + 1 == halvings and (number == 0 or rows % 32 == 0):
            halvings += 1
            rows //= 2
            kept, sent = halve(order, kept, got, following, rows, width)
        else:
            kept = sent = run_after(order, add_kernel, [((2, rows, width), BF16)], kept[0], got[0])
    own = kept
    for number in reversed(range(1, halvings)):
        got = exchange(own, todo[number])
        yield None
        rows *= 2
        shapes = group_shapes(todo[number - 1], rows, width)
        sizes = (len(own), len(got), len(shapes))
        own = run_after(order, functools.partial(double_kernel, sizes, todo[number]), shapes, *own, *got)
    if finish is not None:
        got = exchange(own, todo[0])
        yield None
        kernel, outs = finish
        own = run_after(
            order,
            functools.partial(out_kernel, kernel, todo[0]),
            outs,
            *own,
            *got,
            scratch=[(shape, BF16)],
            free=False,
        )
    yield own


def per_device(
    images,
    extents,
    entry_weight,
    middle_weight,
    closing_weight,
    widen_weight,
    strided_weight,
    expand_weight,
    shortcut_weight,
    entry_affine,
    middle_affine,
    closing_affine,
    widen_affine,
    strided_affine,
    expand_affine,
    shortcut_affine,
    cotangent,
):
    batch, height, width, wide_in = images.shape
    dims = (batch, height, width)
    pixels = batch * height * width
    small_pixels = pixels // 4
    chips = lax.axis_size("img")
    devices = chips * lax.axis_size("row")
    row = lax.axis_index("row")
    local = extents - jnp.stack([row * height, 0]).astype(jnp.int32)
    mid, wider, last = entry_weight.shape[1], widen_weight.shape[1], expand_weight.shape[1]

    def message_rows(channels):
        return max(8, 2 * channels // LANES)

    def message(channels):
        return ((devices, message_rows(channels), LANES), F32)

    def rows(channels):
        return ((message_rows(channels), LANES), F32)

    def stat(channels):
        return ((8, channels), F32)

    def level(count, channels):
        return [((count, channels), BF16), ((count, channels), F32), ((count, channels), F32), stat(channels)]

    def ops(count, *sizes):
        total = 2 * count
        for size in sizes:
            total *= size
        return total

    entry_in, mask, small, above, below, small_below, entry_raw, edge, sent, give = call(
        functools.partial(entry_kernel, dims),
        [
            ((pixels, wide_in), BF16),
            ((pixels, LANES), F32),
            ((small_pixels, LANES), F32),
            ((batch * width, LANES), F32),
            ((batch * width, LANES), F32),
            ((batch * width // 2, LANES), F32),
            ((pixels, mid), F32),
            ((batch * width, mid), F32),
            message(mid),
            ((pixels, wide_in // 2), BF16),
        ],
        local,
        images.reshape(pixels, wide_in),
        entry_weight,
        scratch=[rows(mid)],
        smem=(0,),
        late=(1, 2,),
        keep=(6, 7, 8),
        flops=ops(pixels, wide_in, mid),
    )
    halo = swap_rows(edge)
    entry_in_other = swap_rows(give)
    counts = gather_all(sent)
    padded_rows = batch * (height + 2) * width
    entry_unit, entry_slope, entry_stats, middle_raw, sent, triple, give = call(
        functools.partial(middle_kernel, dims),
        level(pixels, mid)[1:]
        + [
            ((pixels, mid), F32),
            message(mid),
            ((batch, (height + 2) * width, 3 * mid), BF16),
            ((batch, (height + 2) * width, 3 * mid // 2), BF16),
        ],
        counts,
        entry_raw,
        halo,
        mask,
        above,
        below,
        entry_affine,
        middle_weight.reshape(3, 3 * mid, mid),
        scratch=[rows(mid), ((padded_rows + 16, mid), F32)],

        late=(3, 4, 5, 6, 7),
        keep=(3, 4),
        flops=ops(pixels, 9, mid, mid),
    )
    triple_other = swap_rows(give)
    gathered = gather_all(sent)
    middle_act, middle_unit, middle_slope, middle_stats, closing_raw, sent, give = call(
        closing_kernel,
        level(pixels, mid) + [((pixels, wide_in), F32), message(wide_in), ((pixels, mid // 2), BF16)],
        gathered,
        counts,
        middle_raw,
        mask,
        middle_affine,
        closing_weight,
        scratch=[rows(wide_in)],

        late=(5,),
        keep=(4, 5),
        flops=ops(pixels, mid, wide_in),
    )
    middle_act_other = swap_rows(give)
    gathered = gather_all(sent)
    block_out, closing_unit, block_slope, closing_stats, shortcut_in, widen_raw, edge, sent, give, give_short = call(
        functools.partial(widen_kernel, dims),
        level(pixels, wide_in)
        + [
            ((small_pixels, wide_in), BF16),
            ((pixels, wider), F32),
            ((batch * width, wider), F32),
            message(wider),
            ((pixels, wide_in // 2), BF16),
            ((small_pixels, wide_in // 2), BF16),
        ],
        gathered,
        counts,
        closing_raw,
        entry_in,
        mask,
        closing_affine,
        widen_weight,
        scratch=[rows(wider), ((wide_in // LANES, pixels, LANES), F32)],

        late=(3, 6,),
        keep=(5, 6, 7),
        flops=ops(pixels, wide_in, wider),
    )
    halo = swap_rows(edge)
    block_other, short_other = swap_rows(give), swap_rows(give_short)
    gathered = gather_all(sent)
    shortcut_raw, shortcut_rows = call(
        shortcut_kernel,
        [((small_pixels, last), F32), rows(last)],
        shortcut_in,
        small,
        shortcut_weight,
        late=(0, 2),
        keep=(),
        flops=ops(small_pixels, wide_in, last),
    )
    widen_unit, widen_slope, widen_stats, strided_raw, sent, taps, give = call(
        functools.partial(strided_kernel, dims),
        level(pixels, wider)[1:]
        + [
            ((small_pixels, wider), F32),
            message(wider),
            ((3, small_pixels, 3 * wider), BF16),
            ((3, small_pixels, 3 * wider // 2), BF16),
        ],
        gathered,
        counts,
        widen_raw,
        halo,
        mask,
        small,
        above,
        widen_affine,
        strided_weight.reshape(3, 3 * wider, wider),
        scratch=[rows(wider), ((wider // LANES, batch * (height + 1) * width + 16, LANES), F32)],

        late=(8,),
        keep=(3, 4),
        flops=ops(small_pixels, 9, wider, wider),
    )
    taps_other = swap_rows(give)
    gathered = gather_all(sent)
    pair_rows = message_rows(last) + 8
    strided_act, strided_unit, strided_slope, strided_stats, expand_raw, mine, theirs, give = call(
        expand_kernel,
        level(small_pixels, wider)
        + [
            ((small_pixels, last), F32),
            ((pair_rows, LANES), F32),
            ((pair_rows, LANES), F32),
            ((small_pixels, wider // 2), BF16),
        ],
        gathered,
        counts,
        strided_raw,
        small,
        strided_affine,
        expand_weight,
        shortcut_rows,
        scratch=[rows(last)],

        late=(5, 6,),
        keep=(4, 5, 6),
        flops=ops(small_pixels, wider, last),
    )
    strided_act_other = swap_rows(give)
    (sent,) = call(pair_kernel, [((chips, pair_rows, LANES), F32)], mine, swap_rows(theirs), keep=(0,))
    (own_stats,) = call(join_kernel, [stat(last)], gather_img(sent), keep=(0,))
    half_rows = 3 * last // (2 * LANES)
    features, final_grad, expand_unit, shortcut_unit, expand_stats, shortcut_stats, mine, theirs = call(
        final_kernel,
        [
            ((small_pixels, last), BF16),
            ((small_pixels, last), F32),
            ((small_pixels, last), F32),
            ((small_pixels, last), F32),
            stat(last),
            stat(last),
            ((half_rows, LANES), F32),
            ((half_rows, LANES), F32),
        ],
        own_stats,
        swap_rows(own_stats),
        expand_raw,
        shortcut_raw,
        small,
        expand_affine,
        shortcut_affine,
        cotangent.reshape(small_pixels, last),
        late=(3, 7,),
        keep=(1, 2, 3, 4, 5, 6, 7),
        scratch=[((3 * last // LANES, LANES), F32)],

    )

    joined = mine + swap_rows(theirs)
    own_sums = jnp.sum(gather_img(jnp.broadcast_to(joined[None], (chips,) + joined.shape)), axis=0)
    affine_expand, affine_shortcut, expand_grad, shortcut_grad, strided_back, edge, sent = call(
        functools.partial(last_grads_kernel, batch),
        [
            ((2, last), F32),
            ((2, last), F32),
            ((small_pixels, last), BF16),
            ((small_pixels, last), BF16),
            ((small_pixels, wider), F32),
            ((batch * width, wider), F32),
            message(wider),
        ],
        own_sums,
        swap_rows(own_sums),
        counts,
        final_grad,
        expand_unit,
        shortcut_unit,
        expand_stats,
        shortcut_stats,
        expand_affine,
        shortcut_affine,
        small,
        expand_weight,
        strided_slope,
        strided_unit,
        scratch=[rows(wider)],

        late=(11, 12, 13,),
        keep=(4, 5, 6),
        flops=ops(small_pixels, wider, last),
    )
    halo = swap_rows(edge)
    gathered = gather_all(sent)

    def small_image(value):
        return value.reshape(batch, height // 2, width // 2, value.shape[-1])

    def image(value):
        return value.reshape(batch, height, width, value.shape[-1])

    order = [affine_expand]

    def wave_parts(kernel, shape, *operands, flops, free=True):
        parts = call(
            kernel,
            [((shape[0] // 2, shape[1] // 2), BF16)] * 4,
            *operands,
            scratch=[(shape, BF16)],
            flops=flops,
            late=None,
            free=free,
            after=(order[0],),
        )
        order[0] = parts[0]
        return parts

    first_shape = ((wide_in + wider) // 2, last)
    (first,) = call(
        first_wave_kernel,
        [(first_shape, BF16)],
        shortcut_in,
        short_other,
        strided_act,
        strided_act_other,
        shortcut_grad,
        swap_rows(shortcut_grad),
        expand_grad,
        swap_rows(expand_grad),

        flops=ops(2 * small_pixels, *first_shape),
        late=None,
        after=(order[0],),
    )
    order[0] = first
    first = lax.psum(first, "img")

    affine_strided, strided_grad, widen_back, sent = call(
        functools.partial(widen_back_kernel, dims),
        [((2, wider), F32), ((small_pixels, wider), BF16), ((pixels, wider), F32), message(wider)],
        gathered,
        counts,
        strided_back,
        strided_unit,
        halo,
        small,
        small_below,
        strided_stats,
        strided_affine,
        strided_weight,
        widen_unit,
        widen_slope,
        scratch=[
            rows(wider),
            ((batch * (height // 2 + 1) * width // 2 + 8, wider), F32),
            ((wider // LANES, pixels, LANES), F32),
        ],
        late=(3, 9, 10, 11),
        keep=(2, 3),
        after=(order[0],),
        flops=ops(small_pixels, 9, wider, wider),
    )
    gathered = gather_all(sent)
    order[0] = affine_strided
    strided_grad_other = swap_rows(strided_grad)
    (short_back,) = call(
        functools.partial(short_back_kernel, dims),
        [((wide_in // LANES, pixels, LANES), F32)],
        shortcut_grad,
        shortcut_weight,
        late=(0, 1),
        keep=(),
        after=(order[0],),
        flops=ops(small_pixels, wide_in, last),
    )
    order[0] = short_back
    affine_widen, widen_grad, block_back, sent, block_back_saved = call(
        block_back_kernel,
        [
            ((2, wider), F32),
            ((pixels, wider), BF16),
            ((pixels, wide_in), F32),
            message(wide_in),
            ((pixels, wide_in), F32),
        ],
        gathered,
        counts,
        widen_back,
        widen_unit,
        mask,
        widen_stats,
        widen_affine,
        widen_weight,
        short_back,
        closing_unit,
        block_slope,
        scratch=[rows(wide_in)],
        late=(3, 7, 8, 9, 10),
        keep=(2, 3),
        after=(order[0],),
        flops=ops(pixels, wide_in, wider),
    )
    gathered = gather_all(sent)

    order[0] = affine_widen
    widen_grad_other = swap_rows(widen_grad)
    second_shape = (9 * wider // 2, wider)
    second_parts = wave_parts(
        second_wave_kernel,
        second_shape,
        taps,
        taps_other,
        strided_grad,
        strided_grad_other,
        flops=ops(2 * small_pixels, *second_shape),
        free=False,
    )
    second_got = exchange(second_parts[2:], steps()[0])

    affine_closing, closing_grad, middle_back, edge, sent = call(
        functools.partial(middle_back_kernel, dims),
        [
            ((2, wide_in), F32),
            ((pixels, wide_in), BF16),
            ((pixels, mid), F32),
            ((2 * batch * width, mid), F32),
            message(mid),
        ],
        gathered,
        counts,
        block_back,
        closing_unit,
        mask,
        closing_stats,
        closing_affine,
        closing_weight,
        middle_unit,
        middle_slope,
        scratch=[rows(mid)],

        late=(3, 7, 8, 9,),
        keep=(2, 3, 4),
        after=(order[0],),
        flops=ops(pixels, wide_in, mid),
    )
    halo = swap_rows(edge)
    gathered = gather_all(sent)
    order[0] = affine_closing
    closing_grad_other = swap_rows(closing_grad)
    affine_middle, middle_grad, entry_back, sent = call(
        functools.partial(entry_back_kernel, dims),
        [((2, mid), F32), ((pixels, mid), BF16), ((pixels, mid), F32), message(mid)],
        gathered,
        counts,
        middle_back,
        middle_unit,
        halo,
        mask,
        above,
        below,
        middle_stats,
        middle_affine,
        middle_weight,
        entry_unit,
        entry_slope,
        scratch=[rows(mid), ((padded_rows + 16, mid), F32), ((batch, (height + 2) * width, 3 * mid), BF16)],
        late=(3, 10, 11, 12),
        keep=(2, 3),
        after=(order[0],),
        flops=ops(pixels, 9, mid, mid),
    )
    gathered = gather_all(sent)
    order[0] = affine_middle
    middle_grad_other = swap_rows(middle_grad)
    third_sizes = (wide_in // 2 * wider // mid, wide_in // 2, 9 * mid // 2, wide_in // 2)
    third_shape = (-(-sum(third_sizes) // 256) * 256, mid)
    (third_early,) = call(
        functools.partial(third_early_kernel, dims),
        [((sum(third_sizes[:3]), mid), BF16)],
        block_out,
        block_other,
        widen_grad,
        widen_grad_other,
        middle_act,
        middle_act_other,
        closing_grad,
        closing_grad_other,
        triple,
        triple_other,
        middle_grad,
        middle_grad_other,
        flops=ops(2 * pixels, *third_shape),
        late=None,
        after=(order[0],),
    )
    order[0] = third_early
    second_kept, second_sent = halve(
        order, second_parts[:2], second_got, steps()[1], second_shape[0] // 4, second_shape[1] // 2
    )
    affine_entry, entry_grad = call(
        entry_grad_kernel,
        [((2, mid), F32), ((pixels, mid), BF16)],
        gathered,
        counts,
        entry_back,
        entry_unit,
        mask,
        entry_stats,
        entry_affine,
        late=(3,),
        keep=(),
        after=(order[0],),
    )

    order[0] = affine_entry
    third_parts = wave_parts(
        third_wave_kernel,
        third_shape,
        third_early,
        entry_in,
        entry_in_other,
        entry_grad,
        swap_rows(entry_grad),
        flops=ops(2 * pixels, wide_in // 2, mid),
    )

    second_result = ((9, wider // 2, wider), F32)

    def most(second_parts, third_parts):
        order = [third_parts[0]]
        waves = {
            "b": sum_over_chips(
                order, second_parts[:2], second_parts[2:], 1, second_shape, (second_out, [second_result])
            ),
            "c": sum_over_chips(order, third_parts[:2], third_parts[2:], 0, third_shape),
        }
        sums = {}
        for name in "bc" + 16 * "bc":
            if name not in sums:
                result = next(waves[name])
                if result is not None:
                    sums[name] = list(result)
        return sums["b"], sums["c"]

    def none(second_parts, third_parts):
        del second_parts, third_parts
        half = (third_shape[0] // 2, third_shape[1] // 2)
        return [jnp.zeros(*second_result)], [jnp.zeros(half, BF16)] * 2

    (strided_total,), third_own = lax.cond(local[0, 1] > 0, most, none, [*second_kept, *second_sent], list(third_parts))
    third_got = exchange(third_own, steps()[0])
    shortcut_total, expand_total = call(
        first_out,
        [((wide_in // 2, last), F32), ((wider // 2, last), F32)],
        first,
        late=None,
        after=(third_own[0],),
    )
    (image_grads,) = call(
        images_kernel,
        [((pixels, wide_in), BF16)],
        entry_grad,
        entry_weight,
        block_back_saved,
        mask,
        late=None,
        after=(shortcut_total,),
        flops=ops(pixels, mid, wide_in),
    )
    order[0] = image_grads
    widen_total, closing_total, middle_total, entry_total = run_after(
        order,
        functools.partial(out_kernel, third_out, steps()[0]),
        [
            ((wide_in // 2, wider), F32),
            ((mid // 2, wide_in), F32),
            ((9, mid // 2, mid), F32),
            ((wide_in // 2, mid), F32),
        ],
        *third_own,
        *third_got,
        scratch=[(third_shape, BF16)],
        free=False,
    )
    middle_total = middle_total.reshape(3, 3, mid // 2, mid)
    strided_total = strided_total.reshape(3, 3, wider // 2, wider)
    return (
        small_image(features),
        image(image_grads),
        entry_total,
        middle_total,
        closing_total,
        widen_total,
        strided_total,
        expand_total,
        shortcut_total,
        affine_entry,
        affine_middle,
        affine_closing,
        affine_widen,
        affine_strided,
        affine_expand,
        affine_shortcut,
    )


def solution(mesh):
    image = P("img", "row", None, None)
    return jax.shard_map(
        per_device,
        mesh=mesh,
        in_specs=(image, P("img", None)) + (P(),) * 14 + (image,),
        out_specs=(
            image,
            image,
            P("row", None),
            P(None, None, "row", None),
            P("row", None),
            P("row", None),
            P(None, None, "row", None),
            P("row", None),
            P("row", None),
        )
        + (P(),) * 7,
        check_vma=False,
    )
```
